512 devices in a mesh: dp: 8 (over y_lo, core), ctx: 64 (over x, y_hi, z).
Axes of the slice: x: 4, y: 8 (y_hi: 2, y_lo: 4; y = y_hi * 4 + y_lo), z: 8, core: 2. Of those that a mesh axis runs over, the one named last changes fastest.
Arguments:
- frozen_query: bfloat16 [8, 8192, 4096], P('dp', 'ctx'), may hold values from -27 to 27, as said below
- frozen_key_value: bfloat16 [8, 8192, 1024], P('dp', 'ctx'), may hold values from -6 to 6, as said below
- lowrank: bfloat16 [8, 8192, 48], P('dp', 'ctx'), may hold values from -6 to 6
- adapter_up_weight: bfloat16 [16, 5120], replicated, may hold values from -0.5 to 0.5
- output_gradient: bfloat16 [8, 8192, 4096], P('dp', 'ctx'), may hold values from -6 to 6
Outputs:
- attended: bfloat16 [8, 8192, 4096], P('dp', 'ctx')
- grad_lowrank: float32 [8, 8192, 48], P('dp', 'ctx')
- grad_up: float32 [16, 5120], replicated
The draws below stay inside these ranges and needn't reach their ends.
Inputs may be any that keep to these rules, and one draw needn't show every extreme that they name: `frozen_query`: finite values. `frozen_key_value`: finite values.
All inputs are finite; a program needn't handle non-finite values.
Results may differ from the reference program's by a relative error of at most 0.005.
The reference program's roundings to bfloat16 on the way (of `queries`, `key_rows`, `weights`, `score_grad` and `grad_query`) count: a program that leaves them out, or rounds other values in their place, can miss the bound.
Values may be sent and summed in bfloat16 or wider, within the bound.
No kernel may reach another device: no remote copies, remote signals or barrier semaphores. Data moves between devices by JAX's collectives and lax.ppermute only.
A program may use at most 64 MiB of HBM per device.

```python
import math
import jax
import jax.numpy as jnp
from jax import lax

HEADS = 32
KV_HEADS = 4
D_HEAD = 128
ADAPTER_RANK = 16
GROUP = 512
SEQS = 8
SPAN = 8192
ADAPTER_COLUMNS = 5120


def draw_frozen_query(key, part):
    key = jax.random.fold_in(key, 2)
    values = jnp.clip(jax.random.normal(key, (SEQS, SPAN, KV_HEADS, HEADS // KV_HEADS, D_HEAD), jnp.float32), -6.0, 6.0)
    return values.reshape(SEQS, SPAN, HEADS * D_HEAD).astype(jnp.bfloat16)


def draw_frozen_key_value(key, part):
    key = jax.random.fold_in(key, 1)
    key_first, key_second = jax.random.split(key)
    key_rows = jnp.clip(jax.random.normal(key_first, (SEQS, SPAN, KV_HEADS, D_HEAD), jnp.float32), -6.0, 6.0)
    value_rows = jnp.clip(jax.random.normal(key_second, (SEQS, SPAN, KV_HEADS, D_HEAD), jnp.float32), -6.0, 6.0)
    joined = jnp.concatenate([key_rows.reshape(SEQS, SPAN, KV_HEADS * D_HEAD), value_rows.reshape(SEQS, SPAN, KV_HEADS * D_HEAD)], axis=2)
    return joined.astype(jnp.bfloat16)


def steps_of(key, extent, pieces, smallest, high):
    def one(position, blocks):
        steps = jax.random.uniform(jax.random.fold_in(jax.random.fold_in(key, 6), position), (blocks,), jnp.float32, smallest / len(pieces), high / len(pieces))
        return jnp.repeat(jnp.exp(steps), extent[position] // blocks).reshape((-1,) + (1,) * (len(extent) - position - 1))

    level = one(*pieces[0])
    for cut in pieces[1:]:
        level = level * one(*cut)
    return level


def centred(key, dims, scale, limit, shards=(), dtype=jnp.bfloat16):
    loudness = steps_of(key, dims, shards, -0.22, 0.18) if shards else 1.0
    drawn = jax.random.normal(key, dims, jnp.float32) * scale * loudness
    return jnp.minimum(jnp.maximum(drawn, -limit), limit).astype(dtype)


def setup_inputs(seed: int = 0) -> dict:
    arg_keys = jax.random.split(jax.random.key(seed), 6)
    frozen_query = draw_frozen_query(jax.random.fold_in(arg_keys[5], 71), 0)
    frozen_key_value = draw_frozen_key_value(jax.random.fold_in(arg_keys[5], 71), 0)
    lowrank = centred(arg_keys[2], (SEQS, SPAN, 3 * ADAPTER_RANK), 1.0, 6.0, ((0, 8), (1, 64)))
    adapter_up_weight = centred(arg_keys[3], (ADAPTER_RANK, ADAPTER_COLUMNS), 0.08, 0.5)
    output_gradient = centred(arg_keys[4], (SEQS, SPAN, HEADS * D_HEAD), 1.0, 6.0, ((0, 8), (1, 64)))
    return {"frozen_query": frozen_query, "frozen_key_value": frozen_key_value, "lowrank": lowrank, "adapter_up_weight": adapter_up_weight, "output_gradient": output_gradient}


def roll_half(source, amount):
    half_heads = KV_HEADS // 2
    return jnp.concatenate([source[:, :half_heads], jnp.roll(source[:, half_heads:], amount, axis=0)], axis=1)

def attend_group(query_g, key_g, value_g, grad_g):
    score_scale = 1.0 / math.sqrt(D_HEAD)
    query_f = query_g.astype(jnp.float32)
    key_f = key_g.astype(jnp.float32)
    value_f = value_g.astype(jnp.float32)
    grad_f = grad_g.astype(jnp.float32)
    logits = jnp.einsum('tgd,ud->gtu', query_f, key_f) * score_scale
    row_ids = lax.broadcasted_iota(jnp.int32, (GROUP, GROUP), 0)
    col_ids = lax.broadcasted_iota(jnp.int32, (GROUP, GROUP), 1)
    causal = col_ids <= row_ids
    logits = jnp.where(causal, logits, -1e+30)
    peak_row = lax.optimization_barrier(jnp.max(logits, axis=-1, keepdims=True))
    exp_terms = jnp.exp(logits - peak_row)
    weights = exp_terms / lax.optimization_barrier(jnp.sum(exp_terms, axis=-1, keepdims=True))
    weights_b = lax.optimization_barrier(weights.astype(jnp.bfloat16)).astype(jnp.float32)
    output_f = jnp.einsum('gtu,ud->tgd', weights_b, value_f)
    row_dot = jnp.einsum('tgd,tgd->gt', grad_f, output_f)
    prob_grad = jnp.einsum('tgd,ud->gtu', grad_f, value_f)
    score_grad = lax.optimization_barrier((weights_b * (prob_grad - row_dot[:, :, None])).astype(jnp.bfloat16)).astype(jnp.float32)
    grad_query = jnp.einsum('gtu,ud->tgd', score_grad, key_f) * score_scale
    grad_key = jnp.einsum('gtu,tgd->ud', score_grad, query_f) * score_scale
    grad_value = jnp.einsum('gtu,tgd->ud', weights_b, grad_f)
    return (output_f.astype(jnp.bfloat16), grad_query, grad_key, grad_value)

def single_sequence_input(frozen_query, frozen_key_value, rank_width, output_gradient, adapter_up_weight):
    per_head_width = HEADS * D_HEAD
    key_column_width = KV_HEADS * D_HEAD
    group_size = HEADS // KV_HEADS
    offset_rows = GROUP // 2
    groups = SPAN // GROUP
    query_up_weight = adapter_up_weight[:, :per_head_width]
    key_up_weight = adapter_up_weight[:, per_head_width:per_head_width + key_column_width]
    value_up_weight = adapter_up_weight[:, per_head_width + key_column_width:]
    low_query = rank_width[:, :ADAPTER_RANK]
    low_key = rank_width[:, ADAPTER_RANK:2 * ADAPTER_RANK]
    low_value = rank_width[:, 2 * ADAPTER_RANK:]
    queries = (frozen_query + 2.0 * jnp.dot(low_query, query_up_weight, preferred_element_type=jnp.float32)).astype(jnp.bfloat16)
    key_rows = (frozen_key_value[:, :key_column_width] + 2.0 * jnp.dot(low_key, key_up_weight, preferred_element_type=jnp.float32)).astype(jnp.bfloat16)
    value_rows = (frozen_key_value[:, key_column_width:] + 2.0 * jnp.dot(low_value, value_up_weight, preferred_element_type=jnp.float32)).astype(jnp.bfloat16)
    query_heads = queries.reshape(SPAN, KV_HEADS, group_size, D_HEAD)
    key_heads = key_rows.reshape(SPAN, KV_HEADS, D_HEAD)
    value_heads = value_rows.reshape(SPAN, KV_HEADS, D_HEAD)
    grad_heads = output_gradient.reshape(SPAN, KV_HEADS, group_size, D_HEAD)

    def arrange(source):
        rolled = roll_half(source, -offset_rows)
        shaped = rolled.reshape((groups, GROUP) + rolled.shape[1:])
        moved = jnp.moveaxis(shaped, 2, 0)
        return moved.reshape((KV_HEADS * groups, GROUP) + rolled.shape[2:])

    def restore(source):
        shaped = source.reshape((KV_HEADS, groups, GROUP) + source.shape[2:])
        moved = jnp.moveaxis(shaped, 0, 2).reshape((SPAN, KV_HEADS) + source.shape[2:])
        return roll_half(moved, offset_rows)
    outputs = lax.map(lambda gradient_parts: attend_group(*gradient_parts), (arrange(query_heads), arrange(key_heads), arrange(value_heads), arrange(grad_heads)))
    attended = restore(outputs[0]).reshape(SPAN, per_head_width)
    grad_query = restore(outputs[1]).reshape(SPAN, per_head_width).astype(jnp.bfloat16)
    grad_key = restore(outputs[2]).reshape(SPAN, key_column_width).astype(jnp.bfloat16)
    grad_value = restore(outputs[3]).reshape(SPAN, key_column_width).astype(jnp.bfloat16)
    grad_low = 2.0 * jnp.concatenate([jnp.dot(grad_query, query_up_weight.T, preferred_element_type=jnp.float32), jnp.dot(grad_key, key_up_weight.T, preferred_element_type=jnp.float32), jnp.dot(grad_value, value_up_weight.T, preferred_element_type=jnp.float32)], axis=1)
    up_terms = 2.0 * jnp.concatenate([jnp.dot(low_query.T, grad_query, preferred_element_type=jnp.float32), jnp.dot(low_key.T, grad_key, preferred_element_type=jnp.float32), jnp.dot(low_value.T, grad_value, preferred_element_type=jnp.float32)], axis=1)
    return (attended, grad_low, up_terms)

def reference(frozen_query, frozen_key_value, lowrank, adapter_up_weight, output_gradient):
    gradient_results = lax.map(lambda gradient_parts: single_sequence_input(gradient_parts[0], gradient_parts[1], gradient_parts[2], gradient_parts[3], adapter_up_weight), (frozen_query, frozen_key_value, lowrank, output_gradient))
    return (gradient_results[0], gradient_results[1], lax.optimization_barrier(jnp.sum(gradient_results[2], axis=0)))
```

```python
import math

import jax
import jax.numpy as jnp
from jax import lax
from jax.experimental import pallas as pl
from jax.experimental.pallas import tpu as pltpu
from jax.sharding import PartitionSpec as P

HEADS = 32
KV_HEADS = 4
D_HEAD = 128
RANK = 16
GROUP = 512
ROWS = 128
MESSAGE = ROWS + RANK
SHARE = HEADS // KV_HEADS
WIDE = SHARE * D_HEAD
TERMS = WIDE + 2 * D_HEAD
Z_RING = 8
BLOCKED = -1e30
F32 = jnp.float32
BF16 = jnp.bfloat16


def mul(a, b):
    return lax.dot_general(a, b, (((1,), (0,)), ((), ())), preferred_element_type=F32)


def mul_t(a, b):
    return lax.dot_general(a, b, (((1,), (1,)), ((), ())), preferred_element_type=F32)


def prepare_kernel(place, frozen, low, up, light, heavy):
    zeros = jnp.zeros((RANK, 2 * 2 * D_HEAD), BF16)
    up_k = jnp.concatenate([zeros, up[:, : 4 * D_HEAD], zeros], axis=0)
    up_v = jnp.concatenate([zeros, zeros, up[:, 4 * D_HEAD :]], axis=0)
    lows = low[0]
    keys = (frozen[0, :, : 4 * D_HEAD].astype(F32) + 2.0 * mul(lows, up_k)).astype(BF16)
    values = (frozen[0, :, 4 * D_HEAD :].astype(F32) + 2.0 * mul(lows, up_v)).astype(BF16)
    row = lax.broadcasted_iota(jnp.int32, (3 * RANK, 3 * RANK), 0)
    col = lax.broadcasted_iota(jnp.int32, (3 * RANK, 3 * RANK), 1)
    turned = mul_t((row == col).astype(F32).astype(BF16), lows).astype(BF16)
    tail = jnp.concatenate(
        [turned[RANK : 2 * RANK], turned[2 * RANK :], turned[:RANK], jnp.zeros((RANK, D_HEAD), BF16)],
        axis=1,
    )
    half = 2 * D_HEAD

    def write(plain, moved):
        plain[:ROWS, :half] = keys[:, :half]
        plain[:ROWS, half:] = values[:, :half]
        plain[ROWS:, :] = tail
        moved[:ROWS, :half] = keys[:, half:]
        moved[:ROWS, half:] = values[:, half:]
        moved[ROWS:, :] = tail

    @pl.when(place[0] == 0)
    def _():
        write(light, heavy)

    @pl.when(place[0] != 0)
    def _():
        write(heavy, light)


def attend(place, query, grad, low, up_q, up_k, up_v, blocks, closed, attended, terms):
    head = pl.program_id(0)
    key_cols = pl.ds(pl.multiple_of(head * D_HEAD, D_HEAD), D_HEAD)
    value_cols = pl.ds(pl.multiple_of((head + 2) * D_HEAD, D_HEAD), D_HEAD)
    bias = jnp.where(place[1] == 1, 0.0, BLOCKED).astype(F32)
    scale = 1.0 / math.sqrt(D_HEAD)
    keys = jnp.concatenate([b(slice(0, ROWS), key_cols) for b in blocks], axis=0)
    values = jnp.concatenate([b(slice(0, ROWS), value_cols) for b in blocks], axis=0)
    tail = slice(ROWS, MESSAGE)
    low_k = jnp.concatenate([b(tail, slice(0, D_HEAD)) for b in blocks], axis=1)
    low_v = jnp.concatenate([b(tail, slice(D_HEAD, 2 * D_HEAD)) for b in blocks], axis=1)
    low_q = blocks[0](tail, slice(2 * D_HEAD, 3 * D_HEAD))
    keys_t = keys.T
    values_t = values.T
    up_rows = up_q[...]
    padded = jnp.concatenate([up_rows, jnp.zeros((2 * RANK, WIDE), BF16)], axis=0)
    queries = (query[0].astype(F32) + 2.0 * mul(low[0], padded)).astype(BF16)
    grads = grad[0]
    row = lax.broadcasted_iota(jnp.int32, (ROWS, 2 * ROWS), 0)
    col = lax.broadcasted_iota(jnp.int32, (ROWS, 2 * ROWS), 1)
    causal = row <= jnp.where(col >= ROWS, col - ROWS, col)
    low_grad = jnp.zeros((RANK, ROWS), F32)
    all_queries, all_grads, all_weights, all_scores = [], [], [], []
    for pair in range(SHARE // 2):
        sides = [slice((2 * pair + s) * D_HEAD, (2 * pair + s + 1) * D_HEAD) for s in range(2)]
        query_two = jnp.concatenate([queries[:, s] for s in sides], axis=0)
        grad_two = jnp.concatenate([grads[:, s] for s in sides], axis=0)
        logits = mul_t(keys, query_two)
        parts = [jnp.where(causal, logits[:ROWS], BLOCKED)]
        for i, shut in enumerate(closed):
            part = logits[(i + 1) * ROWS : (i + 2) * ROWS]
            parts.append(part + bias if shut else part)
        logits = jnp.concatenate(parts, axis=0)
        peak = jnp.max(logits, axis=0, keepdims=True)
        exps = jnp.exp2((logits - peak) * (scale * math.log2(math.e)))
        weights = (exps * (1.0 / jnp.sum(exps, axis=0, keepdims=True))).astype(BF16)
        out_t = mul(values_t, weights)
        prob_grad = mul_t(values, grad_two)
        weights_f = weights.astype(F32)
        product = weights_f * prob_grad
        row_dot = jnp.sum(product, axis=0, keepdims=True)
        scores = (product - weights_f * row_dot).astype(BF16)
        grad_query_t = (mul(keys_t, scores) * scale).astype(BF16)
        for i, side in enumerate(sides):
            mine = slice(i * ROWS, (i + 1) * ROWS)
            attended[0, :, side] = out_t[:, mine].T.astype(BF16)
            low_grad = low_grad + mul(up_rows[:, side], grad_query_t[:, mine])
            terms[0, :, side] = (2.0 * mul_t(low_q, grad_query_t[:, mine])).astype(terms.dtype)
        all_queries.append(query_two)
        all_grads.append(grad_two)
        all_weights.append(weights)
        all_scores.append(scores)
    grad_keys = mul(jnp.concatenate(all_scores, axis=1), jnp.concatenate(all_queries, axis=0))
    grad_keys = (grad_keys * scale).astype(BF16)
    grad_values = mul(jnp.concatenate(all_weights, axis=1), jnp.concatenate(all_grads, axis=0)).astype(BF16)
    terms[0, :, WIDE : WIDE + D_HEAD] = (2.0 * mul(low_k, grad_keys)).astype(terms.dtype)
    terms[0, :, WIDE + D_HEAD :] = (2.0 * mul(low_v, grad_values)).astype(terms.dtype)
    return 2.0 * low_grad, 2.0 * mul_t(up_k[...], grad_keys), 2.0 * mul_t(up_v[...], grad_values)


def light_kernel(place, query, grad, low, up_q, up_k, up_v, own, one, attended, terms, low_terms):
    blocks = [lambda r, c: own[r, c], lambda r, c: one[r, c]]
    by_query, by_key, by_value = attend(
        place, query, grad, low, up_q, up_k, up_v, blocks, [True], attended, terms
    )
    found = jnp.concatenate(
        [jnp.concatenate([by_query, jnp.zeros_like(by_query)], axis=1), by_key, by_value], axis=0
    )

    @pl.when(pl.program_id(0) == 0)
    def _():
        low_terms[...] = found

    @pl.when(pl.program_id(0) != 0)
    def _():
        low_terms[...] += found


def heavy_kernel(
    place, query, grad, low, up_q, up_k, up_v, own, one_even, one_odd, two, three, before,
    _attended, _terms, attended, terms, mine, back_one, back_two, back_three,
):
    odd = place[1] == 1
    blocks = [
        lambda r, c: own[r, c],
        lambda r, c: jnp.where(odd, one_odd[r, c], one_even[r, c]),
        lambda r, c: two[r, c],
        lambda r, c: three[r, c],
    ]

    @pl.when(pl.program_id(0) == 0)
    def _():
        mine[...] = before[:, :ROWS]
        back_one[...] = before[RANK:, ROWS:]
        back_two[...] = jnp.zeros_like(back_two)
        back_three[...] = jnp.zeros_like(back_three)

    by_query, by_key, by_value = attend(
        place, query, grad, low, up_q, up_k, up_v, blocks, [False, False, True], attended, terms
    )
    mine[:RANK, :] += by_query
    mine[RANK : 2 * RANK, :] += by_key[:, :ROWS]
    mine[2 * RANK :, :] += by_value[:, :ROWS]
    for i, back in enumerate((back_one, back_two, back_three)):
        block = slice((i + 1) * ROWS, (i + 2) * ROWS)
        back[:RANK, :] += by_key[:, block]
        back[RANK:, :] += by_value[:, block]


def whole(*shape):
    return pl.BlockSpec(shape, lambda head, place: (0,) * len(shape))


def at_half(rows, width, first=0):
    return pl.BlockSpec((rows, width), lambda head, place: (0, first + place[0] * 2 + head))


def wide_half():
    return pl.BlockSpec((1, ROWS, WIDE), lambda head, place: (0, 0, place[0] * 2 + head))


def term_half():
    return pl.BlockSpec((1, RANK, TERMS), lambda head, place: (place[0] * 2 + head, 0, 0))


def common_specs():
    return [
        wide_half(),
        wide_half(),
        whole(1, ROWS, 3 * RANK),
        at_half(RANK, WIDE),
        at_half(RANK, D_HEAD, HEADS),
        at_half(RANK, D_HEAD, HEADS + KV_HEADS),
    ]


def params():
    return pltpu.CompilerParams(
        dimension_semantics=("arbitrary",), vmem_limit_bytes=40 * 1024 * 1024
    )


def cost(blocks):
    sizes = 16 * blocks * ROWS * ROWS
    return pl.CostEstimate(
        flops=12 * sizes * D_HEAD, bytes_accessed=6 * ROWS * WIDE * 2, transcendentals=sizes
    )


def exchange(value, axis, groups=None):
    return lax.all_to_all(value, axis, 0, 0, axis_index_groups=groups)


def summed(parts):
    return jnp.sum(parts.astype(F32), axis=0).astype(BF16)


def everywhere(terms):
    seqs, spans = lax.axis_size("dp"), lax.axis_size("ctx")
    along = [[first + i for i in range(Z_RING)] for first in range(0, spans, Z_RING)]
    across = [list(range(i, spans, Z_RING)) for i in range(Z_RING)]
    shape = terms.shape
    part = summed(exchange(terms.reshape(seqs, -1, TERMS), "dp"))
    part = summed(exchange(jnp.broadcast_to(part, (Z_RING,) + part.shape), "ctx", along))
    part = summed(exchange(jnp.broadcast_to(part, (spans // Z_RING,) + part.shape), "ctx", across))
    return exchange(jnp.broadcast_to(part, (seqs,) + part.shape), "dp").reshape(shape)


def shards(frozen_query, frozen_key_value, lowrank, adapter_up_weight, output_gradient):
    spans = lax.axis_size("ctx")
    position = lax.axis_index("ctx") % (GROUP // ROWS)
    light_half = position // 2
    odd = position % 2
    light_place = jnp.stack([light_half, odd]).astype(jnp.int32)
    heavy_place = jnp.stack([1 - light_half, odd]).astype(jnp.int32)
    message = jax.ShapeDtypeStruct((MESSAGE, 4 * D_HEAD), BF16)
    message_spec = whole(MESSAGE, 4 * D_HEAD)
    up_block = pl.BlockSpec((RANK, 8 * D_HEAD), lambda head, place: (0, HEADS // 8))
    light, heavy = pl.pallas_call(
        prepare_kernel,
        out_shape=(message, message),
        grid_spec=pltpu.PrefetchScalarGridSpec(
            num_scalar_prefetch=1,
            grid=(1,),
            in_specs=[whole(1, ROWS, 8 * D_HEAD), whole(1, ROWS, 3 * RANK), up_block],
            out_specs=[message_spec, message_spec],
        ),
        name="prepare",
    )(light_place, frozen_key_value, lowrank, adapter_up_weight)

    def send(value, by, step=1):
        return lax.ppermute(value, "ctx", [(i, (i + by) % spans) for i in range(0, spans, step)])

    one = send(light, 1)
    one_odd = send(heavy, 1, 2)
    two = send(light, 2)
    three = send(light, 3, 2)
    wide_out = jax.ShapeDtypeStruct((1, ROWS, HEADS * D_HEAD), BF16)
    terms_out = jax.ShapeDtypeStruct((KV_HEADS, RANK, TERMS), BF16)
    arguments = (frozen_query, output_gradient, lowrank) + (adapter_up_weight,) * 3
    attended, terms, low_terms = pl.pallas_call(
        light_kernel,
        out_shape=(wide_out, terms_out, jax.ShapeDtypeStruct((3 * RANK, 2 * ROWS), F32)),
        grid_spec=pltpu.PrefetchScalarGridSpec(
            num_scalar_prefetch=1,
            grid=(2,),
            in_specs=common_specs() + [message_spec] * 2,
            out_specs=[wide_half(), term_half(), whole(3 * RANK, 2 * ROWS)],
        ),
        compiler_params=params(),
        cost_estimate=cost(2),
        name="light_heads",
    )(light_place, *arguments, light, one)
    back_out = jax.ShapeDtypeStruct((2 * RANK, ROWS), F32)
    back_spec = whole(2 * RANK, ROWS)
    attended, terms, mine, *backs = pl.pallas_call(
        heavy_kernel,
        out_shape=(wide_out, terms_out, jax.ShapeDtypeStruct((3 * RANK, ROWS), F32)) + (back_out,) * 3,
        grid_spec=pltpu.PrefetchScalarGridSpec(
            num_scalar_prefetch=1,
            grid=(2,),
            in_specs=common_specs()
            + [message_spec] * 5
            + [whole(3 * RANK, 2 * ROWS)]
            + [pl.BlockSpec(memory_space=pl.ANY)] * 2,
            out_specs=[wide_half(), term_half(), whole(3 * RANK, ROWS)] + [back_spec] * 3,
        ),
        input_output_aliases={13: 0, 14: 1},
        compiler_params=params(),
        cost_estimate=cost(4),
        name="heavy_heads",
    )(heavy_place, *arguments, heavy, one, one_odd, two, three, low_terms, attended, terms)
    returned = send(backs[0], -1) + send(backs[1], -2)
    last = [(i, (i - 3) % spans) for i in range(1, spans, 2)]
    returned = returned + lax.ppermute(backs[2], "ctx", last)
    grad_low = (mine + jnp.pad(returned, ((RANK, 0), (0, 0)))).T
    total = everywhere(terms).astype(F32)
    pieces = [total[:, :, :WIDE], total[:, :, WIDE : WIDE + D_HEAD], total[:, :, WIDE + D_HEAD :]]
    grad_up = jnp.concatenate(
        [jnp.moveaxis(p, 0, 1).reshape(RANK, -1) for p in pieces], axis=1
    )
    return (attended, grad_low[None], grad_up)


def solution(mesh):
    return jax.shard_map(
        shards,
        mesh=mesh,
        in_specs=(
            P("dp", "ctx", None),
            P("dp", "ctx", None),
            P("dp", "ctx", None),
            P(),
            P("dp", "ctx", None),
        ),
        out_specs=(P("dp", "ctx", None), P("dp", "ctx", None), P()),
        check_vma=False,
    )
```

```python
import functools
import math

import jax
import jax.numpy as jnp
from jax import lax
from jax.experimental import pallas as pl
from jax.experimental.pallas import tpu as pltpu
from jax.sharding import PartitionSpec as P

HEADS = 32
KV_HEADS = 4
D_HEAD = 128
RANK = 16
GROUP = 512
ROWS = 128
MESSAGE = ROWS + RANK
SHARE = HEADS // KV_HEADS
WIDE = SHARE * D_HEAD
TILES = SHARE + 2
PART = TILES // 2 * RANK
BACK = 2 * RANK
Z_RING = 8
BLOCKED = -1e30
F32 = jnp.float32
BF16 = jnp.bfloat16


def mul(a, b):
    return lax.dot_general(a, b, (((1,), (0,)), ((), ())), preferred_element_type=F32)


def mul_t(a, b):
    return lax.dot_general(a, b, (((1,), (1,)), ((), ())), preferred_element_type=F32)


def t_mul(a, b):
    return lax.dot_general(a, b, (((0,), (0,)), ((), ())), preferred_element_type=F32)


def prepare_kernel(frozen, low, up, light, heavy):
    low_k, low_v = low[0, RANK : 2 * RANK, :], low[0, 2 * RANK :, :]
    wide = KV_HEADS * D_HEAD
    keys = (frozen[0, :, :wide].astype(F32) + 2.0 * t_mul(low_k, up[:, :wide])).astype(BF16)
    values = (frozen[0, :, wide:].astype(F32) + 2.0 * t_mul(low_v, up[:, wide:])).astype(BF16)
    tail = jnp.concatenate([low_k, low_v, jnp.zeros((RANK, 2 * D_HEAD), BF16)], axis=1)
    half = 2 * D_HEAD

    def write(plain, moved):
        plain[:ROWS, :half] = keys[:, :half]
        plain[:ROWS, half:] = values[:, :half]
        plain[ROWS:, :] = tail
        moved[:ROWS, :half] = keys[:, half:]
        moved[:ROWS, half:] = values[:, half:]
        moved[ROWS:, :] = tail

    plain_light = lax.axis_index("ctx") % 4 < 2

    @pl.when(plain_light)
    def _():
        write(light, heavy)

    @pl.when(jnp.logical_not(plain_light))
    def _():
        write(heavy, light)


def stack_kernel(query, grad, low, up_q, queries, grads):
    found = (query[0].astype(F32) + 2.0 * t_mul(low[0, :RANK, :], up_q[...])).astype(BF16)
    for i in range(SHARE):
        rows, cols = slice(i * ROWS, (i + 1) * ROWS), slice(i * D_HEAD, (i + 1) * D_HEAD)
        queries[rows, :] = found[:, cols]
        grads[rows, :] = grad[0, :, cols]


def attend(place, query, grad, low, up_q, up_k, up_v, blocks, closed, attended, terms):
    head = pl.program_id(0)
    key_cols = pl.ds(pl.multiple_of(head * D_HEAD, D_HEAD), D_HEAD)
    value_cols = pl.ds(pl.multiple_of((head + 2) * D_HEAD, D_HEAD), D_HEAD)
    bias = jnp.where(place[1] == 1, 0.0, BLOCKED).astype(F32)
    scale = 1.0 / math.sqrt(D_HEAD)
    keys = jnp.concatenate([b(slice(0, ROWS), key_cols) for b in blocks], axis=0)
    values = jnp.concatenate([b(slice(0, ROWS), value_cols) for b in blocks], axis=0)
    tail = slice(ROWS, MESSAGE)
    low_k = jnp.concatenate([b(tail, slice(0, D_HEAD)) for b in blocks], axis=1)
    low_v = jnp.concatenate([b(tail, slice(D_HEAD, 2 * D_HEAD)) for b in blocks], axis=1)
    low_q = low[0, :RANK, :]
    keys_t = keys.T
    values_t = values.T
    up_rows = up_q[...]
    wide = 2 * ROWS
    row = lax.broadcasted_iota(jnp.int32, (ROWS, wide), 0)
    col = lax.broadcasted_iota(jnp.int32, (ROWS, wide), 1)
    causal = row <= jnp.where(col >= ROWS, col - ROWS, col)
    sides = [slice(h * D_HEAD, (h + 1) * D_HEAD) for h in range(SHARE)]
    all_queries = query[...]
    all_grads = grad[...]
    pairs = [slice(i * wide, (i + 1) * wide) for i in range(SHARE // 2)]
    products = [(mul_t(keys, all_queries[p]), mul_t(values, all_grads[p])) for p in pairs]
    all_weights, all_scores = [], []
    for logits, prob_grad in products:
        parts = [jnp.where(causal, logits[:ROWS], BLOCKED)]
        for i, shut in enumerate(closed):
            part = logits[(i + 1) * ROWS : (i + 2) * ROWS]
            parts.append(part + bias if shut else part)
        logits = jnp.concatenate(parts, axis=0)
        peak = jnp.max(logits, axis=0, keepdims=True)
        exps = jnp.exp2((logits - peak) * (scale * math.log2(math.e)))
        weights = (exps * (1.0 / jnp.sum(exps, axis=0, keepdims=True))).astype(BF16)
        weights_f = weights.astype(F32)
        product = weights_f * prob_grad
        row_dot = jnp.sum(product, axis=0, keepdims=True)
        all_weights.append(weights)
        all_scores.append((product - weights_f * row_dot).astype(BF16))
    grad_queries = []
    for i in range(SHARE // 2):
        out_t = mul(values_t, all_weights[i])
        grad_query_t = (mul(keys_t, all_scores[i]) * scale).astype(BF16)
        for k in range(2):
            mine = slice(k * ROWS, (k + 1) * ROWS)
            attended[0, :, sides[2 * i + k]] = out_t[:, mine].T.astype(BF16)
            grad_queries.append(grad_query_t[:, mine])
    stacked = jnp.concatenate(grad_queries, axis=0)
    low_grad = mul(up_rows, stacked)
    found = [2.0 * mul_t(low_q, stacked)]
    grad_keys = mul(jnp.concatenate(all_scores, axis=1), all_queries)
    grad_keys = (grad_keys * scale).astype(BF16)
    grad_values = mul(jnp.concatenate(all_weights, axis=1), all_grads).astype(BF16)
    found += [2.0 * mul(low_k, grad_keys), 2.0 * mul(low_v, grad_values)]
    found = jnp.concatenate(found, axis=1).astype(BF16)
    for tile in range(TILES):
        rows = slice(tile * RANK % PART, tile * RANK % PART + RANK)
        terms[tile * RANK // PART, rows, :] = found[:, tile * D_HEAD : (tile + 1) * D_HEAD]
    return 2.0 * low_grad, 2.0 * mul_t(up_k[...], grad_keys), 2.0 * mul_t(up_v[...], grad_values)


def light_kernel(place, query, grad, low, up_q, up_k, up_v, own, one, attended, terms, low_terms):
    blocks = [lambda r, c: own[r, c], lambda r, c: one[r, c]]
    by_query, by_key, by_value = attend(
        place, query, grad, low, up_q, up_k, up_v, blocks, [True], attended, terms
    )
    found = jnp.concatenate(
        [jnp.concatenate([by_query, jnp.zeros_like(by_query)], axis=1), by_key, by_value], axis=0
    )

    @pl.when(pl.program_id(0) == 0)
    def _():
        low_terms[...] = found

    @pl.when(pl.program_id(0) != 0)
    def _():
        low_terms[...] += found


def heavy_kernel(
    place, query, grad, low, up_q, up_k, up_v, own, one_even, one_odd, two, three, before,
    _attended, _terms, attended, terms, mine, back_one, back_two, back_three,
):
    odd = place[1] == 1
    blocks = [
        lambda r, c: own[r, c],
        lambda r, c: jnp.where(odd, one_odd[r, c], one_even[r, c]),
        lambda r, c: two[r, c],
        lambda r, c: three[r, c],
    ]

    @pl.when(pl.program_id(0) == 0)
    def _():
        mine[...] = before[:, :ROWS]
        back_one[...] = before[RANK:, ROWS:]
        back_two[...] = jnp.zeros_like(back_two)
        back_three[...] = jnp.zeros_like(back_three)

    by_query, by_key, by_value = attend(
        place, query, grad, low, up_q, up_k, up_v, blocks, [False, False, True], attended, terms
    )
    mine[:RANK, :] += by_query
    mine[RANK : 2 * RANK, :] += by_key[:, :ROWS]
    mine[2 * RANK :, :] += by_value[:, :ROWS]
    for i, back in enumerate((back_one, back_two, back_three)):
        block = slice((i + 1) * ROWS, (i + 2) * ROWS)
        back[:RANK, :] += by_key[:, block]
        back[RANK:, :] += by_value[:, block]


def whole(*shape):
    return pl.BlockSpec(shape, lambda head, place: (0,) * len(shape))


def at_half(rows, width, first=0):
    return pl.BlockSpec((rows, width), lambda head, place: (0, first + place[0] * 2 + head))


def wide_half():
    return pl.BlockSpec((1, ROWS, WIDE), lambda head, place: (0, 0, place[0] * 2 + head))


def term_half():
    return pl.BlockSpec((2, PART, D_HEAD), lambda head, place: (place[0] * 2 + head, 0, 0))


def common_specs():
    stacked = pl.BlockSpec((SHARE * ROWS, D_HEAD), lambda head, place: (place[0] * 2 + head, 0))
    return [
        stacked,
        stacked,
        whole(1, 3 * RANK, ROWS),
        at_half(RANK, WIDE),
        at_half(RANK, D_HEAD, HEADS),
        at_half(RANK, D_HEAD, HEADS + KV_HEADS),
    ]


def params():
    return pltpu.CompilerParams(
        dimension_semantics=("arbitrary",), vmem_limit_bytes=28 * 1024 * 1024
    )


def cost(blocks):
    sizes = 16 * blocks * ROWS * ROWS
    return pl.CostEstimate(
        flops=12 * sizes * D_HEAD, bytes_accessed=6 * ROWS * WIDE * 2, transcendentals=sizes
    )


def exchange(value, axis, groups=None):
    return lax.all_to_all(value, axis, 0, 0, axis_index_groups=groups)


def total(parts, rows):
    return jnp.sum(parts[:, :rows, :].astype(F32), axis=0).astype(BF16)


def along_kernel(spans, parts, back_one, back_two, back_three, out):
    rows = parts.shape[1]
    out[:, :rows, :] = jnp.broadcast_to(total(parts, rows), (Z_RING, rows, D_HEAD))
    out[:, rows:, :] = jnp.zeros((Z_RING, BACK, D_HEAD), BF16)
    place = lax.axis_index("ctx") % Z_RING
    for by, back in enumerate((back_one, back_two, back_three)):
        out[(place + Z_RING - 1 - by) % Z_RING, rows:, :] = back[...].astype(BF16)


def across_kernel(spans, parts, out, near):
    rows = parts.shape[1] - BACK
    place = lax.axis_index("ctx") % Z_RING
    ahead = jnp.zeros((BACK, D_HEAD), F32)
    behind = jnp.zeros((BACK, D_HEAD), F32)
    for i in range(Z_RING):
        came = parts[i, rows:, :].astype(F32)
        ahead = ahead + jnp.where(i > place, came, 0.0)
        behind = behind + jnp.where(i > place, 0.0, came)
    near[...] = ahead
    found = jnp.concatenate([total(parts, rows), behind.astype(BF16)], axis=0)
    out[...] = jnp.broadcast_to(found, out.shape)


def gather_kernel(spans, parts, near, mine, out, low_grad):
    rows = parts.shape[1] - BACK
    out[...] = jnp.broadcast_to(total(parts, rows), out.shape)
    after = (lax.axis_index("ctx") // Z_RING + 1) % (spans // Z_RING)
    low_grad[0, :RANK, :] = mine[:RANK, :]
    low_grad[0, RANK:, :] = mine[RANK:, :] + near[...] + parts[after, rows:, :].astype(F32)


def assemble_kernel(spans, parts, grad_up):
    for tile in range(KV_HEADS * TILES):
        head, inside = tile // TILES, tile % TILES
        column = head * SHARE + inside if inside < SHARE else HEADS + (inside - SHARE) * KV_HEADS + head
        rows = slice(inside * RANK % PART, inside * RANK % PART + RANK)
        grad_up[:, column * D_HEAD : (column + 1) * D_HEAD] = parts[
            2 * head + inside * RANK // PART, rows, :
        ].astype(F32)


def small(kernel, spans, name, out_shape, *operands):
    return pl.pallas_call(
        functools.partial(kernel, spans),
        out_shape=out_shape,
        compiler_params=pltpu.CompilerParams(vmem_limit_bytes=16 * 1024 * 1024),
        name=name,
    )(*operands)


def everywhere(terms, mine, backs):
    seqs, spans = lax.axis_size("dp"), lax.axis_size("ctx")
    along = [[first + i for i in range(Z_RING)] for first in range(0, spans, Z_RING)]
    across = [list(range(i, spans, Z_RING)) for i in range(Z_RING)]
    shape = terms.shape
    rows = shape[0] * shape[1] // seqs
    sent = lambda n, m: jax.ShapeDtypeStruct((n, m, D_HEAD), BF16)
    parts = exchange(terms.reshape(seqs, rows, D_HEAD), "dp")
    parts = small(along_kernel, spans, "along", sent(Z_RING, rows + BACK), parts, *backs)
    parts = exchange(parts, "ctx", along)
    near = jax.ShapeDtypeStruct((BACK, ROWS), F32)
    parts, near = small(across_kernel, spans, "across", (sent(spans // Z_RING, rows + BACK), near), parts)
    parts = exchange(parts, "ctx", across)
    low_grad = jax.ShapeDtypeStruct((1, 3 * RANK, ROWS), F32)
    parts, low_grad = small(
        gather_kernel, spans, "gather", (sent(seqs, rows), low_grad), parts, near, mine
    )
    parts = exchange(parts, "dp").reshape(shape)
    grad_up = jax.ShapeDtypeStruct((RANK, (HEADS + 2 * KV_HEADS) * D_HEAD), F32)
    return jnp.swapaxes(low_grad, 1, 2), small(assemble_kernel, spans, "assemble", grad_up, parts)


def shards(frozen_query, frozen_key_value, lowrank, adapter_up_weight, output_gradient):
    spans = lax.axis_size("ctx")
    position = lax.axis_index("ctx") % (GROUP // ROWS)
    light_half = position // 2
    odd = position % 2
    light_place = jnp.stack([light_half, odd]).astype(jnp.int32)
    heavy_place = jnp.stack([1 - light_half, odd]).astype(jnp.int32)
    message = jax.ShapeDtypeStruct((MESSAGE, 4 * D_HEAD), BF16)
    message_spec = whole(MESSAGE, 4 * D_HEAD)
    columns_first = jnp.swapaxes(lowrank, 1, 2)
    only = lambda *shape: pl.BlockSpec(shape, lambda i: (0,) * len(shape))
    light, heavy = pl.pallas_call(
        prepare_kernel,
        out_shape=(message, message),
        grid=(1,),
        in_specs=[
            only(1, ROWS, 8 * D_HEAD),
            only(1, 3 * RANK, ROWS),
            pl.BlockSpec((RANK, 8 * D_HEAD), lambda i: (0, HEADS // 8)),
        ],
        out_specs=[only(MESSAGE, 4 * D_HEAD)] * 2,
        compiler_params=pltpu.CompilerParams(vmem_limit_bytes=8 * 1024 * 1024),
        name="prepare",
    )(frozen_key_value, columns_first, adapter_up_weight)

    def send(value, by, step=1):
        return lax.ppermute(value, "ctx", [(i, (i + by) % spans) for i in range(0, spans, step)])

    one = send(light, 1)
    one_odd = send(heavy, 1, 2)
    two = send(one, 1)
    three = send(light, 3, 2)
    wide_out = jax.ShapeDtypeStruct((1, ROWS, HEADS * D_HEAD), BF16)
    terms_out = jax.ShapeDtypeStruct((2 * KV_HEADS, PART, D_HEAD), BF16)
    stacked_out = jax.ShapeDtypeStruct((HEADS * ROWS, D_HEAD), BF16)
    wide_block = pl.BlockSpec((1, ROWS, WIDE), lambda i: (0, 0, i))
    stacked_block = pl.BlockSpec((SHARE * ROWS, D_HEAD), lambda i: (i, 0))
    queries, grads = pl.pallas_call(
        stack_kernel,
        out_shape=(stacked_out, stacked_out),
        grid=(KV_HEADS,),
        in_specs=[
            wide_block,
            wide_block,
            only(1, 3 * RANK, ROWS),
            pl.BlockSpec((RANK, WIDE), lambda i: (0, i)),
        ],
        out_specs=[stacked_block, stacked_block],
        compiler_params=pltpu.CompilerParams(vmem_limit_bytes=16 * 1024 * 1024),
        cost_estimate=pl.CostEstimate(
            flops=2 * ROWS * RANK * WIDE * 4, bytes_accessed=16 * ROWS * WIDE * 2, transcendentals=0
        ),
        name="stack",
    )(frozen_query, output_gradient, columns_first, adapter_up_weight)
    arguments = (queries, grads, columns_first) + (adapter_up_weight,) * 3
    attended, terms, low_terms = pl.pallas_call(
        light_kernel,
        out_shape=(wide_out, terms_out, jax.ShapeDtypeStruct((3 * RANK, 2 * ROWS), F32)),
        grid_spec=pltpu.PrefetchScalarGridSpec(
            num_scalar_prefetch=1,
            grid=(2,),
            in_specs=common_specs() + [message_spec] * 2,
            out_specs=[wide_half(), term_half(), whole(3 * RANK, 2 * ROWS)],
        ),
        compiler_params=params(),
        cost_estimate=cost(2),
        name="light_heads",
    )(light_place, *arguments, light, one)
    back_out = jax.ShapeDtypeStruct((2 * RANK, ROWS), F32)
    back_spec = whole(2 * RANK, ROWS)
    attended, terms, mine, *backs = pl.pallas_call(
        heavy_kernel,
        out_shape=(wide_out, terms_out, jax.ShapeDtypeStruct((3 * RANK, ROWS), F32)) + (back_out,) * 3,
        grid_spec=pltpu.PrefetchScalarGridSpec(
            num_scalar_prefetch=1,
            grid=(2,),
            in_specs=common_specs()
            + [message_spec] * 5
            + [whole(3 * RANK, 2 * ROWS)]
            + [pl.BlockSpec(memory_space=pl.ANY)] * 2,
            out_specs=[wide_half(), term_half(), whole(3 * RANK, ROWS)] + [back_spec] * 3,
        ),
        input_output_aliases={13: 0, 14: 1},
        compiler_params=params(),
        cost_estimate=cost(4),
        name="heavy_heads",
    )(heavy_place, *arguments, heavy, one, one_odd, two, three, low_terms, attended, terms)
    grad_low, grad_up = everywhere(terms, mine, backs)
    return (attended, grad_low, grad_up)


def solution(mesh):
    return jax.shard_map(
        shards,
        mesh=mesh,
        in_specs=(
            P("dp", "ctx", None),
            P("dp", "ctx", None),
            P("dp", "ctx", None),
            P(),
            P("dp", "ctx", None),
        ),
        out_specs=(P("dp", "ctx", None), P("dp", "ctx", None), P()),
        check_vma=False,
    )
```

```python
import functools
import math

import jax
import jax.numpy as jnp
from jax import lax
from jax.experimental import pallas as pl
from jax.experimental.pallas import tpu as pltpu
from jax.sharding import PartitionSpec as P

HEADS = 32
KV_HEADS = 4
D_HEAD = 128
RANK = 16
GROUP = 512
ROWS = 128
MESSAGE = ROWS + RANK
SHARE = HEADS // KV_HEADS
WIDE = SHARE * D_HEAD
TILES = SHARE + 2
PART = TILES // 2 * RANK
BACK = 2 * RANK
Z_RING = 8
BLOCKED = -1e30
F32 = jnp.float32
BF16 = jnp.bfloat16


def mul(a, b):
    return lax.dot_general(a, b, (((1,), (0,)), ((), ())), preferred_element_type=F32)


def mul_t(a, b):
    return lax.dot_general(a, b, (((1,), (1,)), ((), ())), preferred_element_type=F32)


def t_mul(a, b):
    return lax.dot_general(a, b, (((0,), (0,)), ((), ())), preferred_element_type=F32)


def prepare_kernel(frozen, low, up, light, heavy):
    low_k, low_v = low[0, RANK : 2 * RANK, :], low[0, 2 * RANK :, :]
    wide = KV_HEADS * D_HEAD
    keys = (frozen[0, :, :wide].astype(F32) + 2.0 * t_mul(low_k, up[:, :wide])).astype(BF16)
    values = (frozen[0, :, wide:].astype(F32) + 2.0 * t_mul(low_v, up[:, wide:])).astype(BF16)
    tail = jnp.concatenate([low_k, low_v, jnp.zeros((RANK, 2 * D_HEAD), BF16)], axis=1)
    half = 2 * D_HEAD

    def write(plain, moved):
        plain[:ROWS, :half] = keys[:, :half]
        plain[:ROWS, half:] = values[:, :half]
        plain[ROWS:, :] = tail
        moved[:ROWS, :half] = keys[:, half:]
        moved[:ROWS, half:] = values[:, half:]
        moved[ROWS:, :] = tail

    plain_light = lax.axis_index("ctx") % 4 < 2

    @pl.when(plain_light)
    def _():
        write(light, heavy)

    @pl.when(jnp.logical_not(plain_light))
    def _():
        write(heavy, light)


def stack_kernel(query, grad, low, up_q, queries, grads):
    found = (query[0].astype(F32) + 2.0 * t_mul(low[0, :RANK, :], up_q[...])).astype(BF16)
    for i in range(SHARE):
        rows, cols = slice(i * ROWS, (i + 1) * ROWS), slice(i * D_HEAD, (i + 1) * D_HEAD)
        queries[rows, :] = found[:, cols]
        grads[rows, :] = grad[0, :, cols]


def attend(place, query, grad, low, up_q, up_k, up_v, blocks, closed, attended, terms):
    head = pl.program_id(0)
    key_cols = pl.ds(pl.multiple_of(head * D_HEAD, D_HEAD), D_HEAD)
    value_cols = pl.ds(pl.multiple_of((head + 2) * D_HEAD, D_HEAD), D_HEAD)
    bias = jnp.where(place[1] == 1, 0.0, BLOCKED).astype(F32)
    scale = 1.0 / math.sqrt(D_HEAD)
    keys = jnp.concatenate([b(slice(0, ROWS), key_cols) for b in blocks], axis=0)
    values = jnp.concatenate([b(slice(0, ROWS), value_cols) for b in blocks], axis=0)
    tail = slice(ROWS, MESSAGE)
    low_k = jnp.concatenate([b(tail, slice(0, D_HEAD)) for b in blocks], axis=1)
    low_v = jnp.concatenate([b(tail, slice(D_HEAD, 2 * D_HEAD)) for b in blocks], axis=1)
    low_q = low[0, :RANK, :]
    keys_t = keys.T
    values_t = values.T
    up_rows = up_q[...]
    wide = 2 * ROWS
    row = lax.broadcasted_iota(jnp.int32, (ROWS, wide), 0)
    col = lax.broadcasted_iota(jnp.int32, (ROWS, wide), 1)
    causal = row <= jnp.where(col >= ROWS, col - ROWS, col)
    sides = [slice(h * D_HEAD, (h + 1) * D_HEAD) for h in range(SHARE)]
    all_queries = query[...]
    all_grads = grad[...]
    pairs = [slice(i * wide, (i + 1) * wide) for i in range(SHARE // 2)]
    products = [(mul_t(keys, all_queries[p]), mul_t(values, all_grads[p])) for p in pairs]
    all_weights, all_scores = [], []
    for logits, prob_grad in products:
        parts = [jnp.where(causal, logits[:ROWS], BLOCKED)]
        for i, shut in enumerate(closed):
            part = logits[(i + 1) * ROWS : (i + 2) * ROWS]
            parts.append(part + bias if shut else part)
        logits = jnp.concatenate(parts, axis=0)
        peak = jnp.max(logits, axis=0, keepdims=True)
        exps = jnp.exp2((logits - peak) * (scale * math.log2(math.e)))
        weights = (exps * (1.0 / jnp.sum(exps, axis=0, keepdims=True))).astype(BF16)
        weights_f = weights.astype(F32)
        product = weights_f * prob_grad
        row_dot = jnp.sum(product, axis=0, keepdims=True)
        all_weights.append(weights)
        all_scores.append((product - weights_f * row_dot).astype(BF16))
    grad_queries = []
    for i in range(SHARE // 2):
        out_t = mul(values_t, all_weights[i])
        grad_query_t = (mul(keys_t, all_scores[i]) * scale).astype(BF16)
        for k in range(2):
            mine = slice(k * ROWS, (k + 1) * ROWS)
            attended[0, :, sides[2 * i + k]] = out_t[:, mine].T.astype(BF16)
            grad_queries.append(grad_query_t[:, mine])
    stacked = jnp.concatenate(grad_queries, axis=0)
    low_grad = mul(up_rows, stacked)
    found = [2.0 * mul_t(low_q, stacked)]
    grad_keys = mul(jnp.concatenate(all_scores, axis=1), all_queries)
    grad_keys = (grad_keys * scale).astype(BF16)
    grad_values = mul(jnp.concatenate(all_weights, axis=1), all_grads).astype(BF16)
    found += [2.0 * mul(low_k, grad_keys), 2.0 * mul(low_v, grad_values)]
    found = jnp.concatenate(found, axis=1).astype(BF16)
    for tile in range(TILES):
        rows = slice(tile * RANK % PART, tile * RANK % PART + RANK)
        terms[tile * RANK // PART, rows, :] = found[:, tile * D_HEAD : (tile + 1) * D_HEAD]
    return 2.0 * low_grad, 2.0 * mul_t(up_k[...], grad_keys), 2.0 * mul_t(up_v[...], grad_values)


def light_kernel(place, query, grad, low, up_q, up_k, up_v, own, one, attended, terms, low_terms):
    blocks = [lambda r, c: own[r, c], lambda r, c: one[r, c]]
    by_query, by_key, by_value = attend(
        place, query, grad, low, up_q, up_k, up_v, blocks, [True], attended, terms
    )
    found = jnp.concatenate(
        [jnp.concatenate([by_query, jnp.zeros_like(by_query)], axis=1), by_key, by_value], axis=0
    )

    @pl.when(pl.program_id(0) == 0)
    def _():
        low_terms[...] = found

    @pl.when(pl.program_id(0) != 0)
    def _():
        low_terms[...] += found


def heavy_kernel(
    place, query, grad, low, up_q, up_k, up_v, own, one_even, one_odd, two_even, two_odd, three, before,
    _attended, _terms, attended, terms, mine, back_one, back_two, back_three,
):
    odd = place[1] == 1
    blocks = [
        lambda r, c: own[r, c],
        lambda r, c: jnp.where(odd, one_odd[r, c], one_even[r, c]),
        lambda r, c: jnp.where(odd, two_odd[r, c], two_even[r, c]),
        lambda r, c: three[r, c],
    ]

    @pl.when(pl.program_id(0) == 0)
    def _():
        mine[...] = before[:, :ROWS]
        back_one[...] = before[RANK:, ROWS:]
        back_two[...] = jnp.zeros_like(back_two)
        back_three[...] = jnp.zeros_like(back_three)

    by_query, by_key, by_value = attend(
        place, query, grad, low, up_q, up_k, up_v, blocks, [False, False, True], attended, terms
    )
    mine[:RANK, :] += by_query
    mine[RANK : 2 * RANK, :] += by_key[:, :ROWS]
    mine[2 * RANK :, :] += by_value[:, :ROWS]
    for i, back in enumerate((back_one, back_two, back_three)):
        block = slice((i + 1) * ROWS, (i + 2) * ROWS)
        back[:RANK, :] += by_key[:, block]
        back[RANK:, :] += by_value[:, block]


def whole(*shape):
    return pl.BlockSpec(shape, lambda head, place: (0,) * len(shape))


def at_half(rows, width, first=0):
    return pl.BlockSpec((rows, width), lambda head, place: (0, first + place[0] * 2 + head))


def wide_half():
    return pl.BlockSpec((1, ROWS, WIDE), lambda head, place: (0, 0, place[0] * 2 + head))


def term_half():
    return pl.BlockSpec((2, PART, D_HEAD), lambda head, place: (place[0] * 2 + head, 0, 0))


def common_specs():
    stacked = pl.BlockSpec((SHARE * ROWS, D_HEAD), lambda head, place: (place[0] * 2 + head, 0))
    return [
        stacked,
        stacked,
        whole(1, 3 * RANK, ROWS),
        at_half(RANK, WIDE),
        at_half(RANK, D_HEAD, HEADS),
        at_half(RANK, D_HEAD, HEADS + KV_HEADS),
    ]


def params():
    return pltpu.CompilerParams(
        dimension_semantics=("arbitrary",), vmem_limit_bytes=28 * 1024 * 1024
    )


def cost(blocks):
    sizes = 16 * blocks * ROWS * ROWS
    return pl.CostEstimate(
        flops=12 * sizes * D_HEAD, bytes_accessed=6 * ROWS * WIDE * 2, transcendentals=sizes
    )


def exchange(value, axis, groups=None):
    return lax.all_to_all(value, axis, 0, 0, axis_index_groups=groups)


def total(parts, rows):
    return jnp.sum(parts[:, :rows, :].astype(F32), axis=0).astype(BF16)


def along_kernel(spans, parts, back_one, back_two, back_three, out):
    rows = parts.shape[1]
    out[:, :rows, :] = jnp.broadcast_to(total(parts, rows), (Z_RING, rows, D_HEAD))
    out[:, rows:, :] = jnp.zeros((Z_RING, BACK, D_HEAD), BF16)
    place = lax.axis_index("ctx") % Z_RING
    for by, back in enumerate((back_one, back_two, back_three)):
        out[(place + Z_RING - 1 - by) % Z_RING, rows:, :] = back[...].astype(BF16)


def across_kernel(spans, parts, out, near):
    rows = parts.shape[1] - BACK
    place = lax.axis_index("ctx") % Z_RING
    ahead = jnp.zeros((BACK, D_HEAD), F32)
    behind = jnp.zeros((BACK, D_HEAD), F32)
    for i in range(Z_RING):
        came = parts[i, rows:, :].astype(F32)
        ahead = ahead + jnp.where(i > place, came, 0.0)
        behind = behind + jnp.where(i > place, 0.0, came)
    near[...] = ahead
    found = jnp.concatenate([total(parts, rows), behind.astype(BF16)], axis=0)
    out[...] = jnp.broadcast_to(found, out.shape)


def gather_kernel(spans, parts, near, mine, out, low_grad):
    rows = parts.shape[1] - BACK
    out[...] = jnp.broadcast_to(total(parts, rows), out.shape)
    after = (lax.axis_index("ctx") // Z_RING + 1) % (spans // Z_RING)
    low_grad[0, :RANK, :] = mine[:RANK, :]
    low_grad[0, RANK:, :] = mine[RANK:, :] + near[...] + parts[after, rows:, :].astype(F32)


def assemble_kernel(spans, parts, grad_up):
    for tile in range(KV_HEADS * TILES):
        head, inside = tile // TILES, tile % TILES
        column = head * SHARE + inside if inside < SHARE else HEADS + (inside - SHARE) * KV_HEADS + head
        rows = slice(inside * RANK % PART, inside * RANK % PART + RANK)
        grad_up[:, column * D_HEAD : (column + 1) * D_HEAD] = parts[
            2 * head + inside * RANK // PART, rows, :
        ].astype(F32)


def small(kernel, spans, name, out_shape, *operands):
    return pl.pallas_call(
        functools.partial(kernel, spans),
        out_shape=out_shape,
        compiler_params=pltpu.CompilerParams(vmem_limit_bytes=16 * 1024 * 1024),
        name=name,
    )(*operands)


def everywhere(terms, mine, backs):
    seqs, spans = lax.axis_size("dp"), lax.axis_size("ctx")
    along = [[first + i for i in range(Z_RING)] for first in range(0, spans, Z_RING)]
    across = [list(range(i, spans, Z_RING)) for i in range(Z_RING)]
    shape = terms.shape
    rows = shape[0] * shape[1] // seqs
    sent = lambda n, m: jax.ShapeDtypeStruct((n, m, D_HEAD), BF16)
    parts = exchange(terms.reshape(seqs, rows, D_HEAD), "dp")
    parts = small(along_kernel, spans, "along", sent(Z_RING, rows + BACK), parts, *backs)
    parts = exchange(parts, "ctx", along)
    near = jax.ShapeDtypeStruct((BACK, ROWS), F32)
    parts, near = small(across_kernel, spans, "across", (sent(spans // Z_RING, rows + BACK), near), parts)
    parts = exchange(parts, "ctx", across)
    low_grad = jax.ShapeDtypeStruct((1, 3 * RANK, ROWS), F32)
    parts, low_grad = small(
        gather_kernel, spans, "gather", (sent(seqs, rows), low_grad), parts, near, mine
    )
    parts = exchange(parts, "dp").reshape(shape)
    grad_up = jax.ShapeDtypeStruct((RANK, (HEADS + 2 * KV_HEADS) * D_HEAD), F32)
    return jnp.swapaxes(low_grad, 1, 2), small(assemble_kernel, spans, "assemble", grad_up, parts)


def shards(frozen_query, frozen_key_value, lowrank, adapter_up_weight, output_gradient):
    spans = lax.axis_size("ctx")
    position = lax.axis_index("ctx") % (GROUP // ROWS)
    light_half = position // 2
    odd = position % 2
    light_place = jnp.stack([light_half, odd]).astype(jnp.int32)
    heavy_place = jnp.stack([1 - light_half, odd]).astype(jnp.int32)
    message = jax.ShapeDtypeStruct((MESSAGE, 4 * D_HEAD), BF16)
    message_spec = whole(MESSAGE, 4 * D_HEAD)
    columns_first = jnp.swapaxes(lowrank, 1, 2)
    only = lambda *shape: pl.BlockSpec(shape, lambda i: (0,) * len(shape))
    light, heavy = pl.pallas_call(
        prepare_kernel,
        out_shape=(message, message),
        grid=(1,),
        in_specs=[
            only(1, ROWS, 8 * D_HEAD),
            only(1, 3 * RANK, ROWS),
            pl.BlockSpec((RANK, 8 * D_HEAD), lambda i: (0, HEADS // 8)),
        ],
        out_specs=[only(MESSAGE, 4 * D_HEAD)] * 2,
        compiler_params=pltpu.CompilerParams(vmem_limit_bytes=56 * 1024 * 1024),
        name="prepare",
    )(frozen_key_value, columns_first, adapter_up_weight)

    def send(value, by, step=1):
        return lax.ppermute(value, "ctx", [(i, (i + by) % spans) for i in range(0, spans, step)])

    one = send(light, 1)
    two_even = send(light, 2, 2)
    one_odd = send(heavy, 1, 2)
    two_odd = send(one, 1, 2)
    three = send(two_even, 1, 2)
    wide_out = jax.ShapeDtypeStruct((1, ROWS, HEADS * D_HEAD), BF16)
    terms_out = jax.ShapeDtypeStruct((2 * KV_HEADS, PART, D_HEAD), BF16)
    stacked_out = jax.ShapeDtypeStruct((HEADS * ROWS, D_HEAD), BF16)
    wide_block = pl.BlockSpec((1, ROWS, WIDE), lambda i: (0, 0, i))
    stacked_block = pl.BlockSpec((SHARE * ROWS, D_HEAD), lambda i: (i, 0))
    queries, grads = pl.pallas_call(
        stack_kernel,
        out_shape=(stacked_out, stacked_out),
        grid=(KV_HEADS,),
        in_specs=[
            wide_block,
            wide_block,
            only(1, 3 * RANK, ROWS),
            pl.BlockSpec((RANK, WIDE), lambda i: (0, i)),
        ],
        out_specs=[stacked_block, stacked_block],
        compiler_params=pltpu.CompilerParams(vmem_limit_bytes=16 * 1024 * 1024),
        cost_estimate=pl.CostEstimate(
            flops=2 * ROWS * RANK * WIDE * 4, bytes_accessed=16 * ROWS * WIDE * 2, transcendentals=0
        ),
        name="stack",
    )(frozen_query, output_gradient, columns_first, adapter_up_weight)
    arguments = (queries, grads, columns_first) + (adapter_up_weight,) * 3
    attended, terms, low_terms = pl.pallas_call(
        light_kernel,
        out_shape=(wide_out, terms_out, jax.ShapeDtypeStruct((3 * RANK, 2 * ROWS), F32)),
        grid_spec=pltpu.PrefetchScalarGridSpec(
            num_scalar_prefetch=1,
            grid=(2,),
            in_specs=common_specs() + [message_spec] * 2,
            out_specs=[wide_half(), term_half(), whole(3 * RANK, 2 * ROWS)],
        ),
        compiler_params=params(),
        cost_estimate=cost(2),
        name="light_heads",
    )(light_place, *arguments, light, one)
    back_out = jax.ShapeDtypeStruct((2 * RANK, ROWS), F32)
    back_spec = whole(2 * RANK, ROWS)
    attended, terms, mine, *backs = pl.pallas_call(
        heavy_kernel,
        out_shape=(wide_out, terms_out, jax.ShapeDtypeStruct((3 * RANK, ROWS), F32)) + (back_out,) * 3,
        grid_spec=pltpu.PrefetchScalarGridSpec(
            num_scalar_prefetch=1,
            grid=(2,),
            in_specs=common_specs()
            + [message_spec] * 6
            + [whole(3 * RANK, 2 * ROWS)]
            + [pl.BlockSpec(memory_space=pl.ANY)] * 2,
            out_specs=[wide_half(), term_half(), whole(3 * RANK, ROWS)] + [back_spec] * 3,
        ),
        input_output_aliases={14: 0, 15: 1},
        compiler_params=params(),
        cost_estimate=cost(4),
        name="heavy_heads",
    )(heavy_place, *arguments, heavy, one, one_odd, two_even, two_odd, three, low_terms, attended, terms)
    grad_low, grad_up = everywhere(terms, mine, backs)
    return (attended, grad_low, grad_up)


def solution(mesh):
    return jax.shard_map(
        shards,
        mesh=mesh,
        in_specs=(
            P("dp", "ctx", None),
            P("dp", "ctx", None),
            P("dp", "ctx", None),
            P(),
            P("dp", "ctx", None),
        ),
        out_specs=(P("dp", "ctx", None), P("dp", "ctx", None), P()),
        check_vma=False,
    )
```

```python
import math

import jax
import jax.numpy as jnp
from jax import lax
from jax.experimental import pallas as pl
from jax.experimental.pallas import tpu as pltpu
from jax.sharding import PartitionSpec as P

HEADS = 32
KV_HEADS = 4
D_HEAD = 128
RANK = 16
GROUP = 512
ROWS = 128
MESSAGE = ROWS + RANK
SHARE = HEADS // KV_HEADS
WIDE = SHARE * D_HEAD
TILES = SHARE + 2
PART = TILES // 2 * RANK
BACK = 2 * RANK
X_SIZE, Y_LOW, Z_SIZE, CORES = 4, 4, 8, 2
Y_SIZE = 2 * Y_LOW
BLOCKED = -1e30
F32 = jnp.float32
BF16 = jnp.bfloat16


def mul(a, b):
    return lax.dot_general(a, b, (((1,), (0,)), ((), ())), preferred_element_type=F32)


def mul_t(a, b):
    return lax.dot_general(a, b, (((1,), (1,)), ((), ())), preferred_element_type=F32)


def t_mul(a, b):
    return lax.dot_general(a, b, (((0,), (0,)), ((), ())), preferred_element_type=F32)


def prepare_kernel(frozen, low, up, light, heavy):
    low_k, low_v = low[0, RANK : 2 * RANK, :], low[0, 2 * RANK :, :]
    wide = KV_HEADS * D_HEAD
    keys = (frozen[0, :, :wide].astype(F32) + 2.0 * t_mul(low_k, up[:, :wide])).astype(BF16)
    values = (frozen[0, :, wide:].astype(F32) + 2.0 * t_mul(low_v, up[:, wide:])).astype(BF16)
    tail = jnp.concatenate([low_k, low_v, jnp.zeros((RANK, 2 * D_HEAD), BF16)], axis=1)
    half = 2 * D_HEAD

    def write(plain, moved):
        plain[:ROWS, :half] = keys[:, :half]
        plain[:ROWS, half:] = values[:, :half]
        plain[ROWS:, :] = tail
        moved[:ROWS, :half] = keys[:, half:]
        moved[:ROWS, half:] = values[:, half:]
        moved[ROWS:, :] = tail

    plain_light = lax.axis_index("ctx") % 4 < 2

    @pl.when(plain_light)
    def _():
        write(light, heavy)

    @pl.when(jnp.logical_not(plain_light))
    def _():
        write(heavy, light)


def stack_kernel(query, grad, low, up_q, queries, grads):
    found = (query[0].astype(F32) + 2.0 * t_mul(low[0, :RANK, :], up_q[...])).astype(BF16)
    for i in range(SHARE):
        rows, cols = slice(i * ROWS, (i + 1) * ROWS), slice(i * D_HEAD, (i + 1) * D_HEAD)
        queries[rows, :] = found[:, cols]
        grads[rows, :] = grad[0, :, cols]


def attend(place, query, grad, low, up_q, up_k, up_v, blocks, closed, attended, terms):
    head = pl.program_id(0)
    key_cols = pl.ds(pl.multiple_of(head * D_HEAD, D_HEAD), D_HEAD)
    value_cols = pl.ds(pl.multiple_of((head + 2) * D_HEAD, D_HEAD), D_HEAD)
    bias = jnp.where(place[1] == 1, 0.0, BLOCKED).astype(F32)
    scale = 1.0 / math.sqrt(D_HEAD)
    keys = jnp.concatenate([b(slice(0, ROWS), key_cols) for b in blocks], axis=0)
    values = jnp.concatenate([b(slice(0, ROWS), value_cols) for b in blocks], axis=0)
    tail = slice(ROWS, MESSAGE)
    low_k = jnp.concatenate([b(tail, slice(0, D_HEAD)) for b in blocks], axis=1)
    low_v = jnp.concatenate([b(tail, slice(D_HEAD, 2 * D_HEAD)) for b in blocks], axis=1)
    low_q = low[0, :RANK, :]
    keys_t = keys.T
    values_t = values.T
    up_rows = up_q[...]
    wide = 2 * ROWS
    row = lax.broadcasted_iota(jnp.int32, (ROWS, wide), 0)
    col = lax.broadcasted_iota(jnp.int32, (ROWS, wide), 1)
    causal = row <= jnp.where(col >= ROWS, col - ROWS, col)
    sides = [slice(h * D_HEAD, (h + 1) * D_HEAD) for h in range(SHARE)]
    all_queries = query[...]
    all_grads = grad[...]
    pairs = [slice(i * wide, (i + 1) * wide) for i in range(SHARE // 2)]
    products = [(mul_t(keys, all_queries[p]), mul_t(values, all_grads[p])) for p in pairs]
    all_weights, all_scores = [], []
    for logits, prob_grad in products:
        parts = [jnp.where(causal, logits[:ROWS], BLOCKED)]
        for i, shut in enumerate(closed):
            part = logits[(i + 1) * ROWS : (i + 2) * ROWS]
            parts.append(part + bias if shut else part)
        logits = jnp.concatenate(parts, axis=0)
        peak = jnp.max(logits, axis=0, keepdims=True)
        exps = jnp.exp2((logits - peak) * (scale * math.log2(math.e)))
        weights = (exps * (1.0 / jnp.sum(exps, axis=0, keepdims=True))).astype(BF16)
        weights_f = weights.astype(F32)
        product = weights_f * prob_grad
        row_dot = jnp.sum(product, axis=0, keepdims=True)
        all_weights.append(weights)
        all_scores.append((product - weights_f * row_dot).astype(BF16))
    grad_queries = []
    for i in range(SHARE // 2):
        out_t = mul(values_t, all_weights[i])
        grad_query_t = (mul(keys_t, all_scores[i]) * scale).astype(BF16)
        for k in range(2):
            mine = slice(k * ROWS, (k + 1) * ROWS)
            attended[0, :, sides[2 * i + k]] = out_t[:, mine].T.astype(BF16)
            grad_queries.append(grad_query_t[:, mine])
    stacked = jnp.concatenate(grad_queries, axis=0)
    low_grad = mul(up_rows, stacked)
    found = [2.0 * mul_t(low_q, stacked)]
    grad_keys = mul(jnp.concatenate(all_scores, axis=1), all_queries)
    grad_keys = (grad_keys * scale).astype(BF16)
    grad_values = mul(jnp.concatenate(all_weights, axis=1), all_grads).astype(BF16)
    found += [2.0 * mul(low_k, grad_keys), 2.0 * mul(low_v, grad_values)]
    found = jnp.concatenate(found, axis=1).astype(BF16)
    for tile in range(TILES):
        rows = slice(tile * RANK % PART, tile * RANK % PART + RANK)
        terms[tile * RANK // PART, rows, :] = found[:, tile * D_HEAD : (tile + 1) * D_HEAD]
    return 2.0 * low_grad, 2.0 * mul_t(up_k[...], grad_keys), 2.0 * mul_t(up_v[...], grad_values)


def light_kernel(place, query, grad, low, up_q, up_k, up_v, own, one, attended, terms, low_terms):
    blocks = [lambda r, c: own[r, c], lambda r, c: one[r, c]]
    by_query, by_key, by_value = attend(
        place, query, grad, low, up_q, up_k, up_v, blocks, [True], attended, terms
    )
    found = jnp.concatenate(
        [jnp.concatenate([by_query, jnp.zeros_like(by_query)], axis=1), by_key, by_value], axis=0
    )

    @pl.when(pl.program_id(0) == 0)
    def _():
        low_terms[...] = found

    @pl.when(pl.program_id(0) != 0)
    def _():
        low_terms[...] += found


def heavy_kernel(
    place, query, grad, low, up_q, up_k, up_v, own, one_even, one_odd, two_even, two_odd, three, before,
    _attended, _terms, attended, terms, mine, back_one, back_two, back_three,
):
    odd = place[1] == 1
    blocks = [
        lambda r, c: own[r, c],
        lambda r, c: jnp.where(odd, one_odd[r, c], one_even[r, c]),
        lambda r, c: jnp.where(odd, two_odd[r, c], two_even[r, c]),
        lambda r, c: three[r, c],
    ]

    @pl.when(pl.program_id(0) == 0)
    def _():
        mine[...] = before[:, :ROWS]
        back_one[...] = before[RANK:, ROWS:]
        back_two[...] = jnp.zeros_like(back_two)
        back_three[...] = jnp.zeros_like(back_three)

    by_query, by_key, by_value = attend(
        place, query, grad, low, up_q, up_k, up_v, blocks, [False, False, True], attended, terms
    )
    mine[:RANK, :] += by_query
    mine[RANK : 2 * RANK, :] += by_key[:, :ROWS]
    mine[2 * RANK :, :] += by_value[:, :ROWS]
    for i, back in enumerate((back_one, back_two, back_three)):
        block = slice((i + 1) * ROWS, (i + 2) * ROWS)
        back[:RANK, :] += by_key[:, block]
        back[RANK:, :] += by_value[:, block]


def whole(*shape):
    return pl.BlockSpec(shape, lambda head, place: (0,) * len(shape))


def at_half(rows, width, first=0):
    return pl.BlockSpec((rows, width), lambda head, place: (0, first + place[0] * 2 + head))


def wide_half():
    return pl.BlockSpec((1, ROWS, WIDE), lambda head, place: (0, 0, place[0] * 2 + head))


def term_half():
    return pl.BlockSpec((2, PART, D_HEAD), lambda head, place: (place[0] * 2 + head, 0, 0))


def common_specs():
    stacked = pl.BlockSpec((SHARE * ROWS, D_HEAD), lambda head, place: (place[0] * 2 + head, 0))
    return [
        stacked,
        stacked,
        whole(1, 3 * RANK, ROWS),
        at_half(RANK, WIDE),
        at_half(RANK, D_HEAD, HEADS),
        at_half(RANK, D_HEAD, HEADS + KV_HEADS),
    ]


def params():
    return pltpu.CompilerParams(
        dimension_semantics=("arbitrary",), vmem_limit_bytes=28 * 1024 * 1024
    )


def cost(blocks):
    sizes = 16 * blocks * ROWS * ROWS
    return pl.CostEstimate(
        flops=12 * sizes * D_HEAD, bytes_accessed=6 * ROWS * WIDE * 2, transcendentals=sizes
    )


def exchange(value, groups):
    return lax.all_to_all(value, ("dp", "ctx"), 0, 0, axis_index_groups=groups)


def index_of(x, y, z, core):
    dp = y % Y_LOW * CORES + core
    return dp * (2 * X_SIZE * Z_SIZE) + (x * 2 + y // Y_LOW) * Z_SIZE + z


def lines():
    xs, ys, zs, cores = range(X_SIZE), range(Y_SIZE), range(Z_SIZE), range(CORES)
    by_x = [[index_of(x, y, z, c) for x in xs for c in cores] for y in ys for z in zs]
    by_z = [[index_of(x, y, z, c) for z in zs] for x in xs for y in ys for c in cores]
    by_y = [[index_of(x, y, z, c) for y in ys] for x in xs for z in zs for c in cores]
    return by_x, by_z, by_y


def total(parts, rows):
    return jnp.sum(parts[:, :rows, :].astype(F32), axis=0).astype(BF16)


def along_kernel(parts, back_one, back_two, back_three, out):
    rows = parts.shape[1]
    out[:, :rows, :] = jnp.broadcast_to(total(parts, rows), (Z_SIZE, rows, D_HEAD))
    out[:, rows:, :] = jnp.zeros((Z_SIZE, BACK, D_HEAD), BF16)
    z = lax.axis_index("ctx") % Z_SIZE
    for by, back in enumerate((back_one, back_two, back_three)):
        out[(z + Z_SIZE - 1 - by) % Z_SIZE, rows:, :] = back[...].astype(BF16)


def beside_kernel(parts, out, near):
    rows = parts.shape[1] - BACK
    z = lax.axis_index("ctx") % Z_SIZE
    ahead = jnp.zeros((BACK, D_HEAD), F32)
    behind = jnp.zeros((BACK, D_HEAD), F32)
    for i in range(Z_SIZE):
        came = parts[i, rows:, :].astype(F32)
        ahead = ahead + jnp.where(i > z, came, 0.0)
        behind = behind + jnp.where(i > z, 0.0, came)
    near[...] = ahead
    found = jnp.concatenate([total(parts, rows), behind.astype(BF16)], axis=0)
    out[...] = jnp.broadcast_to(found, out.shape)


def across_kernel(parts, out, near):
    rows = parts.shape[1] - BACK
    high = lax.axis_index("ctx") // Z_SIZE % 2
    y = high * Y_LOW + lax.axis_index("dp") // CORES
    came = parts[(y + Y_LOW) % Y_SIZE, rows:, :].astype(F32)
    near[...] = jnp.where(high == 1, 0.0, came)
    behind = jnp.where(high == 1, came, 0.0).astype(BF16)
    found = jnp.concatenate([total(parts, rows), behind], axis=0)
    out[...] = jnp.broadcast_to(found, out.shape)


def assemble_kernel(parts, mine, near_z, near_y, grad_up, low_grad):
    for tile in range(KV_HEADS * TILES):
        head, inside = tile // TILES, tile % TILES
        column = head * SHARE + inside if inside < SHARE else HEADS + (inside - SHARE) * KV_HEADS + head
        rows = slice(inside * RANK % PART, inside * RANK % PART + RANK)
        grad_up[:, column * D_HEAD : (column + 1) * D_HEAD] = parts[
            2 * head + inside * RANK // PART, rows, :
        ].astype(F32)
    x = lax.axis_index("ctx") // (2 * Z_SIZE)
    after = (x + 1) % X_SIZE * CORES + lax.axis_index("dp") % CORES
    low_grad[0, :RANK, :] = mine[:RANK, :]
    returned = near_z[...] + near_y[...] + parts[after, PART:, :].astype(F32)
    low_grad[0, RANK:, :] = mine[RANK:, :] + returned


def small(kernel, name, out_shape, *operands):
    return pl.pallas_call(
        kernel,
        out_shape=out_shape,
        compiler_params=pltpu.CompilerParams(vmem_limit_bytes=16 * 1024 * 1024),
        name=name,
    )(*operands)


def everywhere(terms, mine, backs):
    by_x, by_z, by_y = lines()
    sent = jax.ShapeDtypeStruct((Z_SIZE, PART + BACK, D_HEAD), BF16)
    near = jax.ShapeDtypeStruct((BACK, ROWS), F32)
    parts = small(along_kernel, "along", sent, exchange(terms, by_x), *backs)
    parts, near_z = small(beside_kernel, "beside", (sent, near), exchange(parts, by_z))
    parts, near_y = small(across_kernel, "across", (sent, near), exchange(parts, by_y))
    parts = exchange(parts, by_x)
    grad_up = jax.ShapeDtypeStruct((RANK, (HEADS + 2 * KV_HEADS) * D_HEAD), F32)
    low_grad = jax.ShapeDtypeStruct((1, 3 * RANK, ROWS), F32)
    grad_up, low_grad = small(
        assemble_kernel, "assemble", (grad_up, low_grad), parts, mine, near_z, near_y
    )
    return jnp.swapaxes(low_grad, 1, 2), grad_up


def shards(frozen_query, frozen_key_value, lowrank, adapter_up_weight, output_gradient):
    spans = lax.axis_size("ctx")
    position = lax.axis_index("ctx") % (GROUP // ROWS)
    light_half = position // 2
    odd = position % 2
    light_place = jnp.stack([light_half, odd]).astype(jnp.int32)
    heavy_place = jnp.stack([1 - light_half, odd]).astype(jnp.int32)
    message = jax.ShapeDtypeStruct((MESSAGE, 4 * D_HEAD), BF16)
    message_spec = whole(MESSAGE, 4 * D_HEAD)
    columns_first = jnp.swapaxes(lowrank, 1, 2)
    only = lambda *shape: pl.BlockSpec(shape, lambda i: (0,) * len(shape))
    light, heavy = pl.pallas_call(
        prepare_kernel,
        out_shape=(message, message),
        grid=(1,),
        in_specs=[
            only(1, ROWS, 8 * D_HEAD),
            only(1, 3 * RANK, ROWS),
            pl.BlockSpec((RANK, 8 * D_HEAD), lambda i: (0, HEADS // 8)),
        ],
        out_specs=[only(MESSAGE, 4 * D_HEAD)] * 2,
        compiler_params=pltpu.CompilerParams(vmem_limit_bytes=56 * 1024 * 1024),
        name="prepare",
    )(frozen_key_value, columns_first, adapter_up_weight)

    def send(value, by, step=1):
        return lax.ppermute(value, "ctx", [(i, (i + by) % spans) for i in range(0, spans, step)])

    one = send(light, 1)
    two_even = send(light, 2, 2)
    one_odd = send(heavy, 1, 2)
    two_odd = send(one, 1, 2)
    three = send(two_even, 1, 2)
    wide_out = jax.ShapeDtypeStruct((1, ROWS, HEADS * D_HEAD), BF16)
    terms_out = jax.ShapeDtypeStruct((2 * KV_HEADS, PART, D_HEAD), BF16)
    stacked_out = jax.ShapeDtypeStruct((HEADS * ROWS, D_HEAD), BF16)
    wide_block = pl.BlockSpec((1, ROWS, WIDE), lambda i: (0, 0, i))
    stacked_block = pl.BlockSpec((SHARE * ROWS, D_HEAD), lambda i: (i, 0))
    queries, grads = pl.pallas_call(
        stack_kernel,
        out_shape=(stacked_out, stacked_out),
        grid=(KV_HEADS,),
        in_specs=[
            wide_block,
            wide_block,
            only(1, 3 * RANK, ROWS),
            pl.BlockSpec((RANK, WIDE), lambda i: (0, i)),
        ],
        out_specs=[stacked_block, stacked_block],
        compiler_params=pltpu.CompilerParams(vmem_limit_bytes=16 * 1024 * 1024),
        cost_estimate=pl.CostEstimate(
            flops=2 * ROWS * RANK * WIDE * 4, bytes_accessed=16 * ROWS * WIDE * 2, transcendentals=0
        ),
        name="stack",
    )(frozen_query, output_gradient, columns_first, adapter_up_weight)
    arguments = (queries, grads, columns_first) + (adapter_up_weight,) * 3
    attended, terms, low_terms = pl.pallas_call(
        light_kernel,
        out_shape=(wide_out, terms_out, jax.ShapeDtypeStruct((3 * RANK, 2 * ROWS), F32)),
        grid_spec=pltpu.PrefetchScalarGridSpec(
            num_scalar_prefetch=1,
            grid=(2,),
            in_specs=common_specs() + [message_spec] * 2,
            out_specs=[wide_half(), term_half(), whole(3 * RANK, 2 * ROWS)],
        ),
        compiler_params=params(),
        cost_estimate=cost(2),
        name="light_heads",
    )(light_place, *arguments, light, one)
    back_out = jax.ShapeDtypeStruct((2 * RANK, ROWS), F32)
    back_spec = whole(2 * RANK, ROWS)
    attended, terms, mine, *backs = pl.pallas_call(
        heavy_kernel,
        out_shape=(wide_out, terms_out, jax.ShapeDtypeStruct((3 * RANK, ROWS), F32)) + (back_out,) * 3,
        grid_spec=pltpu.PrefetchScalarGridSpec(
            num_scalar_prefetch=1,
            grid=(2,),
            in_specs=common_specs()
            + [message_spec] * 6
            + [whole(3 * RANK, 2 * ROWS)]
            + [pl.BlockSpec(memory_space=pl.ANY)] * 2,
            out_specs=[wide_half(), term_half(), whole(3 * RANK, ROWS)] + [back_spec] * 3,
        ),
        input_output_aliases={14: 0, 15: 1},
        compiler_params=params(),
        cost_estimate=cost(4),
        name="heavy_heads",
    )(heavy_place, *arguments, heavy, one, one_odd, two_even, two_odd, three, low_terms, attended, terms)
    grad_low, grad_up = everywhere(terms, mine, backs)
    return (attended, grad_low, grad_up)


def solution(mesh):
    return jax.shard_map(
        shards,
        mesh=mesh,
        in_specs=(
            P("dp", "ctx", None),
            P("dp", "ctx", None),
            P("dp", "ctx", None),
            P(),
            P("dp", "ctx", None),
        ),
        out_specs=(P("dp", "ctx", None), P("dp", "ctx", None), P()),
        check_vma=False,
    )
```

```python
import functools
import math

import jax
import jax.numpy as jnp
from jax import lax
from jax.experimental import pallas as pl
from jax.experimental.pallas import tpu as pltpu
from jax.sharding import PartitionSpec as P

HEADS = 32
KV_HEADS = 4
D_HEAD = 128
RANK = 16
GROUP = 512
ROWS = 128
MESSAGE = ROWS + RANK
SHARE = HEADS // KV_HEADS
WIDE = SHARE * D_HEAD
TILES = SHARE + 2
PART = TILES // 2 * RANK
BACK = 2 * RANK
X_SIZE, Y_LOW, Z_SIZE, CORES = 4, 4, 8, 2
Y_SIZE = 2 * Y_LOW
BLOCKED = -1e30
F32 = jnp.float32
BF16 = jnp.bfloat16


def mul(a, b):
    return lax.dot_general(a, b, (((1,), (0,)), ((), ())), preferred_element_type=F32)


def mul_t(a, b):
    return lax.dot_general(a, b, (((1,), (1,)), ((), ())), preferred_element_type=F32)


def t_mul(a, b):
    return lax.dot_general(a, b, (((0,), (0,)), ((), ())), preferred_element_type=F32)


def prepare_kernel(frozen, low, up, light, heavy):
    low_k, low_v = low[0, RANK : 2 * RANK, :], low[0, 2 * RANK :, :]
    wide = KV_HEADS * D_HEAD
    keys = (frozen[0, :, :wide].astype(F32) + 2.0 * t_mul(low_k, up[:, :wide])).astype(BF16)
    values = (frozen[0, :, wide:].astype(F32) + 2.0 * t_mul(low_v, up[:, wide:])).astype(BF16)
    tail = jnp.concatenate([low_k, low_v, jnp.zeros((RANK, 2 * D_HEAD), BF16)], axis=1)
    half = 2 * D_HEAD

    def write(plain, moved):
        plain[:ROWS, :half] = keys[:, :half]
        plain[:ROWS, half:] = values[:, :half]
        plain[ROWS:, :] = tail
        moved[:ROWS, :half] = keys[:, half:]
        moved[:ROWS, half:] = values[:, half:]
        moved[ROWS:, :] = tail

    plain_light = lax.axis_index("ctx") % 4 < 2

    @pl.when(plain_light)
    def _():
        write(light, heavy)

    @pl.when(jnp.logical_not(plain_light))
    def _():
        write(heavy, light)


def stack_kernel(query, grad, low, up_q, queries, grads):
    found = (query[0].astype(F32) + 2.0 * t_mul(low[0, :RANK, :], up_q[...])).astype(BF16)
    for i in range(SHARE):
        rows, cols = slice(i * ROWS, (i + 1) * ROWS), slice(i * D_HEAD, (i + 1) * D_HEAD)
        queries[rows, :] = found[:, cols]
        grads[rows, :] = grad[0, :, cols]


def attend(place, head, all_queries, all_grads, low_q, ups, blocks, closed, attended, terms):
    up_rows, up_k, up_v = ups
    key_cols = pl.ds(pl.multiple_of(head * D_HEAD, D_HEAD), D_HEAD)
    value_cols = pl.ds(pl.multiple_of((head + 2) * D_HEAD, D_HEAD), D_HEAD)
    bias = jnp.where(place[1] == 1, 0.0, BLOCKED).astype(F32)
    scale = 1.0 / math.sqrt(D_HEAD)
    keys = jnp.concatenate([b(slice(0, ROWS), key_cols) for b in blocks], axis=0)
    values = jnp.concatenate([b(slice(0, ROWS), value_cols) for b in blocks], axis=0)
    tail = slice(ROWS, MESSAGE)
    low_k = jnp.concatenate([b(tail, slice(0, D_HEAD)) for b in blocks], axis=1)
    low_v = jnp.concatenate([b(tail, slice(D_HEAD, 2 * D_HEAD)) for b in blocks], axis=1)
    keys_t = keys.T
    values_t = values.T
    wide = 2 * ROWS
    row = lax.broadcasted_iota(jnp.int32, (ROWS, wide), 0)
    col = lax.broadcasted_iota(jnp.int32, (ROWS, wide), 1)
    causal = row <= jnp.where(col >= ROWS, col - ROWS, col)
    pairs = [slice(i * wide, (i + 1) * wide) for i in range(SHARE // 2)]
    products = [(mul_t(keys, all_queries[p]), mul_t(values, all_grads[p])) for p in pairs]
    all_weights, all_scores = [], []
    for logits, prob_grad in products:
        parts = [jnp.where(causal, logits[:ROWS], BLOCKED)]
        for i, shut in enumerate(closed):
            part = logits[(i + 1) * ROWS : (i + 2) * ROWS]
            parts.append(part + bias if shut else part)
        logits = jnp.concatenate(parts, axis=0)
        peak = jnp.max(logits, axis=0, keepdims=True)
        exps = jnp.exp2((logits - peak) * (scale * math.log2(math.e)))
        weights = (exps * (1.0 / jnp.sum(exps, axis=0, keepdims=True))).astype(BF16)
        weights_f = weights.astype(F32)
        product = weights_f * prob_grad
        row_dot = jnp.sum(product, axis=0, keepdims=True)
        all_weights.append(weights)
        all_scores.append((product - weights_f * row_dot).astype(BF16))
    grad_queries = []
    for i in range(SHARE // 2):
        out_t = mul(values_t, all_weights[i])
        grad_query_t = (mul(keys_t, all_scores[i]) * scale).astype(BF16)
        for k in range(2):
            mine = slice(k * ROWS, (k + 1) * ROWS)
            attended(2 * i + k)[...] = out_t[:, mine].T.astype(BF16)
            grad_queries.append(grad_query_t[:, mine])
    stacked = jnp.concatenate(grad_queries, axis=0)
    low_grad = mul(up_rows, stacked)
    found = [2.0 * mul_t(low_q, stacked)]
    grad_keys = mul(jnp.concatenate(all_scores, axis=1), all_queries)
    grad_keys = (grad_keys * scale).astype(BF16)
    grad_values = mul(jnp.concatenate(all_weights, axis=1), all_grads).astype(BF16)
    found += [2.0 * mul(low_k, grad_keys), 2.0 * mul(low_v, grad_values)]
    found = jnp.concatenate(found, axis=1).astype(BF16)
    for tile in range(TILES):
        rows = slice(tile * RANK % PART, tile * RANK % PART + RANK)
        terms(tile * RANK // PART)[rows, :] = found[:, tile * D_HEAD : (tile + 1) * D_HEAD]
    return 2.0 * low_grad, 2.0 * mul_t(up_k, grad_keys), 2.0 * mul_t(up_v, grad_values)


def light_heads(place, query, grad, low, up, blocks, closed, attended, terms, low_terms, held, sems):
    sums, copies = [], []
    for head in range(2):
        chosen = place[0] * 2 + head
        rows = pl.ds(pl.multiple_of(chosen * WIDE, WIDE), WIDE)
        ups = [
            up[:, pl.ds(pl.multiple_of(first * D_HEAD + chosen * width, D_HEAD), width)]
            for first, width in ((0, WIDE), (HEADS, D_HEAD), (HEADS + KV_HEADS, D_HEAD))
        ]
        found = attend(
            place, head, query[rows, :], grad[rows, :], low[0, :RANK, :], ups, blocks, closed,
            lambda k, head=head: held.at[head, 0, :, k * D_HEAD : (k + 1) * D_HEAD],
            lambda i, chosen=chosen: terms.at[2 * chosen + i],
        )
        sums = [a + b for a, b in zip(sums, found)] if sums else found
        copies.append(
            pltpu.make_async_copy(held.at[head], attended.at[:, :, rows], sems.at[head])
        )
        copies[-1].start()
    by_query, by_key, by_value = sums
    low_terms[...] = jnp.zeros_like(low_terms)
    reach = by_key.shape[1]
    low_terms[:RANK, :ROWS] = by_query
    low_terms[RANK : 2 * RANK, :reach] = by_key
    low_terms[2 * RANK :, :reach] = by_value
    for copy in copies:
        copy.wait()


def early_kernel(place, query, grad, low, up, own, attended, terms, low_terms, held, sems):
    @pl.when(place[2] == 1)
    def _():
        blocks = [lambda r, c: own[r, c]]
        light_heads(place, query, grad, low, up, blocks, [], attended, terms, low_terms, held, sems)


def light_kernel(
    place, query, grad, low, up, own, one, terms_before, low_before, _attended,
    attended, terms, low_terms, held, sems,
):
    @pl.when(place[2] == 1)
    def _():
        terms[...] = terms_before[...]
        low_terms[...] = low_before[...]

    @pl.when(place[2] == 0)
    def _():
        blocks = [lambda r, c: own[r, c], lambda r, c: one[r, c]]
        light_heads(
            place, query, grad, low, up, blocks, [True], attended, terms, low_terms, held, sems
        )


def heavy_kernel(
    place, query, grad, low, up_q, up_k, up_v, own, one_even, one_odd, two_even, two_odd, three, before,
    _attended, _terms, attended, terms, mine, back_one, back_two, back_three,
):
    odd = place[1] == 1
    blocks = [
        lambda r, c: own[r, c],
        lambda r, c: jnp.where(odd, one_odd[r, c], one_even[r, c]),
        lambda r, c: jnp.where(odd, two_odd[r, c], two_even[r, c]),
        lambda r, c: three[r, c],
    ]

    @pl.when(pl.program_id(0) == 0)
    def _():
        mine[...] = before[:, :ROWS]
        back_one[...] = before[RANK:, ROWS:]
        back_two[...] = jnp.zeros_like(back_two)
        back_three[...] = jnp.zeros_like(back_three)

    ups = (up_q[...], up_k[...], up_v[...])
    by_query, by_key, by_value = attend(
        place, pl.program_id(0), query[...], grad[...], low[0, :RANK, :], ups, blocks, [False, False, True],
        lambda k: attended.at[0, :, k * D_HEAD : (k + 1) * D_HEAD],
        lambda i: terms.at[i],
    )
    mine[:RANK, :] += by_query
    mine[RANK : 2 * RANK, :] += by_key[:, :ROWS]
    mine[2 * RANK :, :] += by_value[:, :ROWS]
    for i, back in enumerate((back_one, back_two, back_three)):
        block = slice((i + 1) * ROWS, (i + 2) * ROWS)
        back[:RANK, :] += by_key[:, block]
        back[RANK:, :] += by_value[:, block]


def whole(*shape):
    return pl.BlockSpec(shape, lambda head, place: (0,) * len(shape))


def at_half(rows, width, first=0):
    return pl.BlockSpec((rows, width), lambda head, place: (0, first + place[0] * 2 + head))


def wide_half():
    return pl.BlockSpec((1, ROWS, WIDE), lambda head, place: (0, 0, place[0] * 2 + head))


def term_half():
    return pl.BlockSpec((2, PART, D_HEAD), lambda head, place: (place[0] * 2 + head, 0, 0))


def common_specs():
    stacked = pl.BlockSpec((SHARE * ROWS, D_HEAD), lambda head, place: (place[0] * 2 + head, 0))
    return [
        stacked,
        stacked,
        whole(1, 3 * RANK, ROWS),
        at_half(RANK, WIDE),
        at_half(RANK, D_HEAD, HEADS),
        at_half(RANK, D_HEAD, HEADS + KV_HEADS),
    ]


def params():
    return pltpu.CompilerParams(
        dimension_semantics=("arbitrary",), vmem_limit_bytes=28 * 1024 * 1024
    )


def cost(blocks):
    sizes = 16 * blocks * ROWS * ROWS
    return pl.CostEstimate(
        flops=12 * sizes * D_HEAD, bytes_accessed=6 * ROWS * WIDE * 2, transcendentals=sizes
    )


def exchange(value, groups):
    return lax.all_to_all(value, ("dp", "ctx"), 0, 0, axis_index_groups=groups)


def index_of(x, y, z, core):
    dp = y % Y_LOW * CORES + core
    return dp * (2 * X_SIZE * Z_SIZE) + (x * 2 + y // Y_LOW) * Z_SIZE + z


def lines():
    xs, ys, zs, cores = range(X_SIZE), range(Y_SIZE), range(Z_SIZE), range(CORES)
    by_x = [[index_of(x, y, z, c) for x in xs for c in cores] for y in ys for z in zs]
    by_z = [[index_of(x, y, z, c) for z in zs] for x in xs for y in ys for c in cores]
    by_y = [[index_of(x, y, z, c) for y in ys] for x in xs for z in zs for c in cores]
    return by_x, by_z, by_y


def total(parts, rows):
    return jnp.sum(parts[:, :rows, :].astype(F32), axis=0).astype(BF16)


def along_kernel(parts, back_one, back_two, back_three, out):
    rows = parts.shape[1]
    out[:, :rows, :] = jnp.broadcast_to(total(parts, rows), (Z_SIZE, rows, D_HEAD))
    out[:, rows:, :] = jnp.zeros((Z_SIZE, BACK, D_HEAD), BF16)
    z = lax.axis_index("ctx") % Z_SIZE
    for by, back in enumerate((back_one, back_two, back_three)):
        out[(z + Z_SIZE - 1 - by) % Z_SIZE, rows:, :] = back[...].astype(BF16)


def beside_kernel(parts, out, near):
    rows = parts.shape[1] - BACK
    z = lax.axis_index("ctx") % Z_SIZE
    ahead = jnp.zeros((BACK, D_HEAD), F32)
    behind = jnp.zeros((BACK, D_HEAD), F32)
    for i in range(Z_SIZE):
        came = parts[i, rows:, :].astype(F32)
        ahead = ahead + jnp.where(i > z, came, 0.0)
        behind = behind + jnp.where(i > z, 0.0, came)
    near[...] = ahead
    found = jnp.concatenate([total(parts, rows), behind.astype(BF16)], axis=0)
    out[...] = jnp.broadcast_to(found, out.shape)


def across_kernel(parts, out, near):
    rows = parts.shape[1] - BACK
    high = lax.axis_index("ctx") // Z_SIZE % 2
    y = high * Y_LOW + lax.axis_index("dp") // CORES
    came = parts[(y + Y_LOW) % Y_SIZE, rows:, :].astype(F32)
    near[...] = jnp.where(high == 1, 0.0, came)
    behind = jnp.where(high == 1, came, 0.0).astype(BF16)
    found = jnp.concatenate([total(parts, rows), behind], axis=0)
    out[...] = jnp.broadcast_to(found, out.shape)


def assemble_kernel(parts, mine, near_z, near_y, grad_up, low_grad):
    for tile in range(KV_HEADS * TILES):
        head, inside = tile // TILES, tile % TILES
        column = head * SHARE + inside if inside < SHARE else HEADS + (inside - SHARE) * KV_HEADS + head
        rows = slice(inside * RANK % PART, inside * RANK % PART + RANK)
        grad_up[:, column * D_HEAD : (column + 1) * D_HEAD] = parts[
            2 * head + inside * RANK // PART, rows, :
        ].astype(F32)
    x = lax.axis_index("ctx") // (2 * Z_SIZE)
    after = (x + 1) % X_SIZE * CORES + lax.axis_index("dp") % CORES
    low_grad[0, :RANK, :] = mine[:RANK, :]
    returned = near_z[...] + near_y[...] + parts[after, PART:, :].astype(F32)
    low_grad[0, RANK:, :] = mine[RANK:, :] + returned


def small(kernel, name, out_shape, *operands):
    return pl.pallas_call(
        kernel,
        out_shape=out_shape,
        compiler_params=pltpu.CompilerParams(vmem_limit_bytes=16 * 1024 * 1024),
        name=name,
    )(*operands)


def everywhere(terms, mine, backs):
    by_x, by_z, by_y = lines()
    sent = jax.ShapeDtypeStruct((Z_SIZE, PART + BACK, D_HEAD), BF16)
    near = jax.ShapeDtypeStruct((BACK, ROWS), F32)
    parts = small(along_kernel, "along", sent, exchange(terms, by_x), *backs)
    parts, near_z = small(beside_kernel, "beside", (sent, near), exchange(parts, by_z))
    parts, near_y = small(across_kernel, "across", (sent, near), exchange(parts, by_y))
    parts = exchange(parts, by_x)
    grad_up = jax.ShapeDtypeStruct((RANK, (HEADS + 2 * KV_HEADS) * D_HEAD), F32)
    low_grad = jax.ShapeDtypeStruct((1, 3 * RANK, ROWS), F32)
    grad_up, low_grad = small(
        assemble_kernel, "assemble", (grad_up, low_grad), parts, mine, near_z, near_y
    )
    return jnp.swapaxes(low_grad, 1, 2), grad_up


def shards(frozen_query, frozen_key_value, lowrank, adapter_up_weight, output_gradient):
    spans = lax.axis_size("ctx")
    position = lax.axis_index("ctx") % (GROUP // ROWS)
    light_half = position // 2
    odd = position % 2
    early = lax.axis_index("ctx") % Z_SIZE == 0
    light_place = jnp.stack([light_half, odd, early]).astype(jnp.int32)
    heavy_place = jnp.stack([1 - light_half, odd]).astype(jnp.int32)
    message = jax.ShapeDtypeStruct((MESSAGE, 4 * D_HEAD), BF16)
    message_spec = whole(MESSAGE, 4 * D_HEAD)
    columns_first = jnp.swapaxes(lowrank, 1, 2)
    only = lambda *shape: pl.BlockSpec(shape, lambda i: (0,) * len(shape))
    light, heavy = pl.pallas_call(
        prepare_kernel,
        out_shape=(message, message),
        grid=(1,),
        in_specs=[
            only(1, ROWS, 8 * D_HEAD),
            only(1, 3 * RANK, ROWS),
            pl.BlockSpec((RANK, 8 * D_HEAD), lambda i: (0, HEADS // 8)),
        ],
        out_specs=[only(MESSAGE, 4 * D_HEAD)] * 2,
        compiler_params=pltpu.CompilerParams(vmem_limit_bytes=56 * 1024 * 1024),
        name="prepare",
    )(frozen_key_value, columns_first, adapter_up_weight)

    def send(value, by, step=1):
        return lax.ppermute(value, "ctx", [(i, (i + by) % spans) for i in range(0, spans, step)])

    one = send(light, 1)
    two_even = send(light, 2, 2)
    one_odd = send(heavy, 1, 2)
    wide_out = jax.ShapeDtypeStruct((1, ROWS, HEADS * D_HEAD), BF16)
    terms_out = jax.ShapeDtypeStruct((2 * KV_HEADS, PART, D_HEAD), BF16)
    stacked_out = jax.ShapeDtypeStruct((HEADS * ROWS, D_HEAD), BF16)
    wide_block = pl.BlockSpec((1, ROWS, WIDE), lambda i: (0, 0, i))
    stacked_block = pl.BlockSpec((SHARE * ROWS, D_HEAD), lambda i: (i, 0))
    queries, grads = pl.pallas_call(
        stack_kernel,
        out_shape=(stacked_out, stacked_out),
        grid=(KV_HEADS,),
        in_specs=[
            wide_block,
            wide_block,
            only(1, 3 * RANK, ROWS),
            pl.BlockSpec((RANK, WIDE), lambda i: (0, i)),
        ],
        out_specs=[stacked_block, stacked_block],
        compiler_params=pltpu.CompilerParams(vmem_limit_bytes=51 * 1024 * 1024),
        cost_estimate=pl.CostEstimate(
            flops=2 * ROWS * RANK * WIDE * 4, bytes_accessed=16 * ROWS * WIDE * 2, transcendentals=0
        ),
        name="stack",
    )(frozen_query, output_gradient, columns_first, adapter_up_weight)
    arguments = (queries, grads, columns_first) + (adapter_up_weight,) * 3
    light_arguments = (light_place, queries, grads, columns_first, adapter_up_weight, light)
    light_outs = (wide_out, terms_out, jax.ShapeDtypeStruct((3 * RANK, 2 * ROWS), F32))
    vmem = pl.BlockSpec(memory_space=pltpu.VMEM)
    light_call = functools.partial(
        pl.pallas_call,
        out_shape=light_outs,
        out_specs=[pl.BlockSpec(memory_space=pl.ANY), vmem, vmem],
        scratch_shapes=[pltpu.VMEM((2, 1, ROWS, WIDE), BF16), pltpu.SemaphoreType.DMA((2,))],
        compiler_params=pltpu.CompilerParams(vmem_limit_bytes=28 * 1024 * 1024),
        cost_estimate=cost(2),
    )
    in_smem = [pl.BlockSpec(memory_space=pltpu.SMEM)]
    attended, terms, low_terms = light_call(
        early_kernel, in_specs=in_smem + [vmem] * 5, name="early_heads"
    )(*light_arguments)
    one, two_even, attended = lax.optimization_barrier((one, two_even, attended))
    two_odd = send(one, 1, 2)
    three = send(two_even, 1, 2)
    attended, terms, low_terms = light_call(
        light_kernel,
        in_specs=in_smem + [vmem] * 8 + [pl.BlockSpec(memory_space=pl.ANY)],
        input_output_aliases={9: 0},
        name="light_heads",
    )(*light_arguments, one, terms, low_terms, attended)
    back_out = jax.ShapeDtypeStruct((2 * RANK, ROWS), F32)
    back_spec = whole(2 * RANK, ROWS)
    attended, terms, mine, *backs = pl.pallas_call(
        heavy_kernel,
        out_shape=(wide_out, terms_out, jax.ShapeDtypeStruct((3 * RANK, ROWS), F32)) + (back_out,) * 3,
        grid_spec=pltpu.PrefetchScalarGridSpec(
            num_scalar_prefetch=1,
            grid=(2,),
            in_specs=common_specs()
            + [message_spec] * 6
            + [whole(3 * RANK, 2 * ROWS)]
            + [pl.BlockSpec(memory_space=pl.ANY)] * 2,
            out_specs=[wide_half(), term_half(), whole(3 * RANK, ROWS)] + [back_spec] * 3,
        ),
        input_output_aliases={14: 0, 15: 1},
        compiler_params=params(),
        cost_estimate=cost(4),
        name="heavy_heads",
    )(heavy_place, *arguments, heavy, one, one_odd, two_even, two_odd, three, low_terms, attended, terms)
    grad_low, grad_up = everywhere(terms, mine, backs)
    return (attended, grad_low, grad_up)


def solution(mesh):
    return jax.shard_map(
        shards,
        mesh=mesh,
        in_specs=(
            P("dp", "ctx", None),
            P("dp", "ctx", None),
            P("dp", "ctx", None),
            P(),
            P("dp", "ctx", None),
        ),
        out_specs=(P("dp", "ctx", None), P("dp", "ctx", None), P()),
        check_vma=False,
    )
```

```python
import functools
import math

import jax
import jax.numpy as jnp
from jax import lax
from jax.experimental import pallas as pl
from jax.experimental.pallas import tpu as pltpu
from jax.sharding import PartitionSpec as P

HEADS = 32
KV_HEADS = 4
D_HEAD = 128
RANK = 16
GROUP = 512
ROWS = 128
MESSAGE = ROWS + RANK
SHARE = HEADS // KV_HEADS
WIDE = SHARE * D_HEAD
TILES = SHARE + 2
PART = TILES // 2 * RANK
BACK = 2 * RANK
X_SIZE, Y_LOW, Z_SIZE, CORES = 4, 4, 8, 2
Y_SIZE = 2 * Y_LOW
BLOCKED = -1e30
F32 = jnp.float32
BF16 = jnp.bfloat16


def mul(a, b):
    return lax.dot_general(a, b, (((1,), (0,)), ((), ())), preferred_element_type=F32)


def mul_t(a, b):
    return lax.dot_general(a, b, (((1,), (1,)), ((), ())), preferred_element_type=F32)


def t_mul(a, b):
    return lax.dot_general(a, b, (((0,), (0,)), ((), ())), preferred_element_type=F32)


def prepare_kernel(frozen, low, up, light, heavy):
    low_q, low_k, low_v = (low[0, i * RANK : (i + 1) * RANK, :] for i in range(3))
    wide = KV_HEADS * D_HEAD
    keys = (frozen[0, :, :wide].astype(F32) + 2.0 * t_mul(low_k, up[:, :wide])).astype(BF16)
    values = (frozen[0, :, wide:].astype(F32) + 2.0 * t_mul(low_v, up[:, wide:])).astype(BF16)
    tail = jnp.concatenate([low_k, low_v, low_q, jnp.zeros((RANK, D_HEAD), BF16)], axis=1)
    half = 2 * D_HEAD

    def write(plain, moved):
        plain[:ROWS, :half] = keys[:, :half]
        plain[:ROWS, half:] = values[:, :half]
        plain[ROWS:, :] = tail
        moved[:ROWS, :half] = keys[:, half:]
        moved[:ROWS, half:] = values[:, half:]
        moved[ROWS:, :] = tail

    plain_light = lax.axis_index("ctx") % 4 < 2

    @pl.when(plain_light)
    def _():
        write(light, heavy)

    @pl.when(jnp.logical_not(plain_light))
    def _():
        write(heavy, light)


def stack_kernel(query, grad, low_all, up, queries, grads, held, low, sems):
    copies = [pltpu.make_async_copy(low_all.at[0, pl.ds(0, RANK), :], low, sems.at[0])]
    for i in range(KV_HEADS):
        wide = query.at[0, :, pl.ds(i * WIDE, WIDE)]
        copies.append(pltpu.make_async_copy(wide, held.at[i], sems.at[1 + i]))
    for i in range(HEADS):
        head = grad.at[0, :, pl.ds(i * D_HEAD, D_HEAD)]
        place = grads.at[pl.ds(i * ROWS, ROWS), :]
        copies.append(pltpu.make_async_copy(head, place, sems.at[1 + KV_HEADS + i]))
    for copy in copies:
        copy.start()
    copies[0].wait()
    for i in range(KV_HEADS):
        added = 2.0 * t_mul(low[...], up[:, i * WIDE : (i + 1) * WIDE])
        copies[1 + i].wait()
        found = (held[i].astype(F32) + added).astype(BF16)
        for k in range(SHARE):
            rows = slice((i * SHARE + k) * ROWS, (i * SHARE + k + 1) * ROWS)
            queries[rows, :] = found[:, k * D_HEAD : (k + 1) * D_HEAD]
    for copy in copies[1 + KV_HEADS :]:
        copy.wait()


def attend(place, head, all_queries, all_grads, ups, blocks, closed, attended, terms):
    up_rows, up_k, up_v = ups
    key_cols = pl.ds(pl.multiple_of(head * D_HEAD, D_HEAD), D_HEAD)
    value_cols = pl.ds(pl.multiple_of((head + 2) * D_HEAD, D_HEAD), D_HEAD)
    bias = jnp.where(place[1] == 1, 0.0, BLOCKED).astype(F32)
    scale = 1.0 / math.sqrt(D_HEAD)
    keys = jnp.concatenate([b(slice(0, ROWS), key_cols) for b in blocks], axis=0)
    values = jnp.concatenate([b(slice(0, ROWS), value_cols) for b in blocks], axis=0)
    tail = slice(ROWS, MESSAGE)
    low_k = jnp.concatenate([b(tail, slice(0, D_HEAD)) for b in blocks], axis=1)
    low_v = jnp.concatenate([b(tail, slice(D_HEAD, 2 * D_HEAD)) for b in blocks], axis=1)
    low_q = blocks[0](tail, slice(2 * D_HEAD, 3 * D_HEAD))
    keys_t = keys.T
    values_t = values.T
    wide = 2 * ROWS
    row = lax.broadcasted_iota(jnp.int32, (ROWS, wide), 0)
    col = lax.broadcasted_iota(jnp.int32, (ROWS, wide), 1)
    causal = row <= jnp.where(col >= ROWS, col - ROWS, col)
    pairs = [slice(i * wide, (i + 1) * wide) for i in range(SHARE // 2)]
    products = [(mul_t(keys, all_queries[p]), mul_t(values, all_grads[p])) for p in pairs]
    all_weights, all_scores = [], []
    for logits, prob_grad in products:
        parts = [jnp.where(causal, logits[:ROWS], BLOCKED)]
        for i, shut in enumerate(closed):
            part = logits[(i + 1) * ROWS : (i + 2) * ROWS]
            parts.append(part + bias if shut else part)
        logits = jnp.concatenate(parts, axis=0)
        peak = jnp.max(logits, axis=0, keepdims=True)
        exps = jnp.exp2((logits - peak) * (scale * math.log2(math.e)))
        weights = (exps * (1.0 / jnp.sum(exps, axis=0, keepdims=True))).astype(BF16)
        weights_f = weights.astype(F32)
        product = weights_f * prob_grad
        row_dot = jnp.sum(product, axis=0, keepdims=True)
        all_weights.append(weights)
        all_scores.append((product - weights_f * row_dot).astype(BF16))
    grad_queries = []
    for i in range(SHARE // 2):
        out_t = mul(values_t, all_weights[i])
        grad_query_t = (mul(keys_t, all_scores[i]) * scale).astype(BF16)
        for k in range(2):
            mine = slice(k * ROWS, (k + 1) * ROWS)
            attended(2 * i + k)[...] = out_t[:, mine].T.astype(BF16)
            grad_queries.append(grad_query_t[:, mine])
    stacked = jnp.concatenate(grad_queries, axis=0)
    low_grad = mul(up_rows, stacked)
    found = [2.0 * mul_t(low_q, stacked)]
    grad_keys = mul(jnp.concatenate(all_scores, axis=1), all_queries)
    grad_keys = (grad_keys * scale).astype(BF16)
    grad_values = mul(jnp.concatenate(all_weights, axis=1), all_grads).astype(BF16)
    found += [2.0 * mul(low_k, grad_keys), 2.0 * mul(low_v, grad_values)]
    found = jnp.concatenate(found, axis=1).astype(BF16)
    for tile in range(TILES):
        rows = slice(tile * RANK % PART, tile * RANK % PART + RANK)
        terms(tile * RANK // PART)[rows, :] = found[:, tile * D_HEAD : (tile + 1) * D_HEAD]
    return 2.0 * low_grad, 2.0 * mul_t(up_k, grad_keys), 2.0 * mul_t(up_v, grad_values)


def light_heads(place, query, grad, up, blocks, closed, attended, terms, low_terms, held, sems):
    sums, copies = [], []
    for head in range(2):
        chosen = place[0] * 2 + head
        rows = pl.ds(pl.multiple_of(chosen * WIDE, WIDE), WIDE)
        ups = [
            up[:, pl.ds(pl.multiple_of(first * D_HEAD + chosen * width, D_HEAD), width)]
            for first, width in ((0, WIDE), (HEADS, D_HEAD), (HEADS + KV_HEADS, D_HEAD))
        ]
        found = attend(
            place, head, query[rows, :], grad[rows, :], ups, blocks, closed,
            lambda k, head=head: held.at[head, 0, :, k * D_HEAD : (k + 1) * D_HEAD],
            lambda i, chosen=chosen: terms.at[2 * chosen + i],
        )
        sums = [a + b for a, b in zip(sums, found)] if sums else found
        copies.append(
            pltpu.make_async_copy(held.at[head], attended.at[:, :, rows], sems.at[head])
        )
        copies[-1].start()
    by_query, by_key, by_value = sums
    low_terms[...] = jnp.zeros_like(low_terms)
    reach = by_key.shape[1]
    low_terms[:RANK, :ROWS] = by_query
    low_terms[RANK : 2 * RANK, :reach] = by_key
    low_terms[2 * RANK :, :reach] = by_value
    for copy in copies:
        copy.wait()


def early_kernel(place, query, grad, up, own, attended, terms, low_terms, held, sems):
    @pl.when(place[2] == 1)
    def _():
        blocks = [lambda r, c: own[r, c]]
        light_heads(place, query, grad, up, blocks, [], attended, terms, low_terms, held, sems)


def light_kernel(
    place, query, grad, up, own, one, terms_before, low_before, _attended,
    attended, terms, low_terms, held, sems,
):
    @pl.when(place[2] == 1)
    def _():
        terms[...] = terms_before[...]
        low_terms[...] = low_before[...]

    @pl.when(place[2] == 0)
    def _():
        blocks = [lambda r, c: own[r, c], lambda r, c: one[r, c]]
        light_heads(
            place, query, grad, up, blocks, [True], attended, terms, low_terms, held, sems
        )


def heavy_kernel(
    place, query, grad, up_q, up_k, up_v, own, one_even, one_odd, two_even, two_odd, three, before,
    _attended, _terms, attended, terms, mine, back_one, back_two, back_three,
):
    odd = place[1] == 1
    blocks = [
        lambda r, c: own[r, c],
        lambda r, c: jnp.where(odd, one_odd[r, c], one_even[r, c]),
        lambda r, c: jnp.where(odd, two_odd[r, c], two_even[r, c]),
        lambda r, c: three[r, c],
    ]

    @pl.when(pl.program_id(0) == 0)
    def _():
        mine[...] = before[:, :ROWS]
        back_one[...] = before[RANK:, ROWS:]
        back_two[...] = jnp.zeros_like(back_two)
        back_three[...] = jnp.zeros_like(back_three)

    ups = (up_q[...], up_k[...], up_v[...])
    by_query, by_key, by_value = attend(
        place, pl.program_id(0), query[...], grad[...], ups, blocks, [False, False, True],
        lambda k: attended.at[0, :, k * D_HEAD : (k + 1) * D_HEAD],
        lambda i: terms.at[i],
    )
    mine[:RANK, :] += by_query
    mine[RANK : 2 * RANK, :] += by_key[:, :ROWS]
    mine[2 * RANK :, :] += by_value[:, :ROWS]
    for i, back in enumerate((back_one, back_two, back_three)):
        block = slice((i + 1) * ROWS, (i + 2) * ROWS)
        back[:RANK, :] += by_key[:, block]
        back[RANK:, :] += by_value[:, block]


def whole(*shape):
    return pl.BlockSpec(shape, lambda head, place: (0,) * len(shape))


def at_half(rows, width, first=0):
    return pl.BlockSpec((rows, width), lambda head, place: (0, first + place[0] * 2 + head))


def wide_half():
    return pl.BlockSpec((1, ROWS, WIDE), lambda head, place: (0, 0, place[0] * 2 + head))


def term_half():
    return pl.BlockSpec((2, PART, D_HEAD), lambda head, place: (place[0] * 2 + head, 0, 0))


def common_specs():
    stacked = pl.BlockSpec((SHARE * ROWS, D_HEAD), lambda head, place: (place[0] * 2 + head, 0))
    return [
        stacked,
        stacked,
        at_half(RANK, WIDE),
        at_half(RANK, D_HEAD, HEADS),
        at_half(RANK, D_HEAD, HEADS + KV_HEADS),
    ]


def params():
    return pltpu.CompilerParams(
        dimension_semantics=("arbitrary",), vmem_limit_bytes=28 * 1024 * 1024
    )


def cost(blocks):
    sizes = 16 * blocks * ROWS * ROWS
    return pl.CostEstimate(
        flops=12 * sizes * D_HEAD, bytes_accessed=6 * ROWS * WIDE * 2, transcendentals=sizes
    )


def exchange(value, groups):
    return lax.all_to_all(value, ("dp", "ctx"), 0, 0, axis_index_groups=groups)


def index_of(x, y, z, core):
    dp = y % Y_LOW * CORES + core
    return dp * (2 * X_SIZE * Z_SIZE) + (x * 2 + y // Y_LOW) * Z_SIZE + z


def lines():
    xs, ys, zs, cores = range(X_SIZE), range(Y_SIZE), range(Z_SIZE), range(CORES)
    by_x = [[index_of(x, y, z, c) for x in xs for c in cores] for y in ys for z in zs]
    by_z = [[index_of(x, y, z, c) for z in zs] for x in xs for y in ys for c in cores]
    by_y = [[index_of(x, y, z, c) for y in ys] for x in xs for z in zs for c in cores]
    return by_x, by_z, by_y


def total(parts, rows):
    return jnp.sum(parts[:, :rows, :].astype(F32), axis=0).astype(BF16)


def along_kernel(parts, back_one, back_two, back_three, out):
    rows = parts.shape[1]
    out[:, :rows, :] = jnp.broadcast_to(total(parts, rows), (Z_SIZE, rows, D_HEAD))
    out[:, rows:, :] = jnp.zeros((Z_SIZE, BACK, D_HEAD), BF16)
    z = lax.axis_index("ctx") % Z_SIZE
    for by, back in enumerate((back_one, back_two, back_three)):
        out[(z + Z_SIZE - 1 - by) % Z_SIZE, rows:, :] = back[...].astype(BF16)


def beside_kernel(parts, out, near):
    rows = parts.shape[1] - BACK
    z = lax.axis_index("ctx") % Z_SIZE
    ahead = jnp.zeros((BACK, D_HEAD), F32)
    behind = jnp.zeros((BACK, D_HEAD), F32)
    for i in range(Z_SIZE):
        came = parts[i, rows:, :].astype(F32)
        ahead = ahead + jnp.where(i > z, came, 0.0)
        behind = behind + jnp.where(i > z, 0.0, came)
    near[...] = ahead
    found = jnp.concatenate([total(parts, rows), behind.astype(BF16)], axis=0)
    out[...] = jnp.broadcast_to(found, out.shape)


def across_kernel(parts, out, near):
    rows = parts.shape[1] - BACK
    high = lax.axis_index("ctx") // Z_SIZE % 2
    y = high * Y_LOW + lax.axis_index("dp") // CORES
    came = parts[(y + Y_LOW) % Y_SIZE, rows:, :].astype(F32)
    near[...] = jnp.where(high == 1, 0.0, came)
    behind = jnp.where(high == 1, came, 0.0).astype(BF16)
    found = jnp.concatenate([total(parts, rows), behind], axis=0)
    out[...] = jnp.broadcast_to(found, out.shape)


def assemble_kernel(parts, mine, near_z, near_y, grad_up, low_grad):
    for tile in range(KV_HEADS * TILES):
        head, inside = tile // TILES, tile % TILES
        column = head * SHARE + inside if inside < SHARE else HEADS + (inside - SHARE) * KV_HEADS + head
        rows = slice(inside * RANK % PART, inside * RANK % PART + RANK)
        grad_up[:, column * D_HEAD : (column + 1) * D_HEAD] = parts[
            2 * head + inside * RANK // PART, rows, :
        ].astype(F32)
    x = lax.axis_index("ctx") // (2 * Z_SIZE)
    after = (x + 1) % X_SIZE * CORES + lax.axis_index("dp") % CORES
    low_grad[0, :RANK, :] = mine[:RANK, :]
    returned = near_z[...] + near_y[...] + parts[after, PART:, :].astype(F32)
    low_grad[0, RANK:, :] = mine[RANK:, :] + returned


def small(kernel, name, out_shape, *operands):
    return pl.pallas_call(
        kernel,
        out_shape=out_shape,
        compiler_params=pltpu.CompilerParams(vmem_limit_bytes=16 * 1024 * 1024),
        name=name,
    )(*operands)


def everywhere(terms, mine, backs):
    by_x, by_z, by_y = lines()
    sent = jax.ShapeDtypeStruct((Z_SIZE, PART + BACK, D_HEAD), BF16)
    near = jax.ShapeDtypeStruct((BACK, ROWS), F32)
    parts = small(along_kernel, "along", sent, exchange(terms, by_x), *backs)
    parts, near_z = small(beside_kernel, "beside", (sent, near), exchange(parts, by_z))
    parts, near_y = small(across_kernel, "across", (sent, near), exchange(parts, by_y))
    parts = exchange(parts, by_x)
    grad_up = jax.ShapeDtypeStruct((RANK, (HEADS + 2 * KV_HEADS) * D_HEAD), F32)
    low_grad = jax.ShapeDtypeStruct((1, 3 * RANK, ROWS), F32)
    grad_up, low_grad = small(
        assemble_kernel, "assemble", (grad_up, low_grad), parts, mine, near_z, near_y
    )
    return jnp.swapaxes(low_grad, 1, 2), grad_up


def shards(frozen_query, frozen_key_value, lowrank, adapter_up_weight, output_gradient):
    spans = lax.axis_size("ctx")
    position = lax.axis_index("ctx") % (GROUP // ROWS)
    light_half = position // 2
    odd = position % 2
    early = lax.axis_index("ctx") % Z_SIZE == 0
    light_place = jnp.stack([light_half, odd, early]).astype(jnp.int32)
    heavy_place = jnp.stack([1 - light_half, odd]).astype(jnp.int32)
    message = jax.ShapeDtypeStruct((MESSAGE, 4 * D_HEAD), BF16)
    message_spec = whole(MESSAGE, 4 * D_HEAD)
    columns_first = jnp.swapaxes(lowrank, 1, 2)
    only = lambda *shape: pl.BlockSpec(shape, lambda i: (0,) * len(shape))
    light, heavy = pl.pallas_call(
        prepare_kernel,
        out_shape=(message, message),
        grid=(1,),
        in_specs=[
            only(1, ROWS, 8 * D_HEAD),
            only(1, 3 * RANK, ROWS),
            pl.BlockSpec((RANK, 8 * D_HEAD), lambda i: (0, HEADS // 8)),
        ],
        out_specs=[only(MESSAGE, 4 * D_HEAD)] * 2,
        compiler_params=pltpu.CompilerParams(vmem_limit_bytes=56 * 1024 * 1024),
        name="prepare",
    )(frozen_key_value, columns_first, adapter_up_weight)

    def send(value, by, step=1):
        return lax.ppermute(value, "ctx", [(i, (i + by) % spans) for i in range(0, spans, step)])

    one = send(light, 1)
    two_even = send(light, 2, 2)
    one_odd = send(heavy, 1, 2)
    wide_out = jax.ShapeDtypeStruct((1, ROWS, HEADS * D_HEAD), BF16)
    terms_out = jax.ShapeDtypeStruct((2 * KV_HEADS, PART, D_HEAD), BF16)
    stacked_out = jax.ShapeDtypeStruct((HEADS * ROWS, D_HEAD), BF16)
    vmem, anywhere = pl.BlockSpec(memory_space=pltpu.VMEM), pl.BlockSpec(memory_space=pl.ANY)
    queries, grads = pl.pallas_call(
        stack_kernel,
        out_shape=(stacked_out, stacked_out),
        in_specs=[anywhere] * 3 + [vmem],
        out_specs=[vmem] * 2,
        scratch_shapes=[
            pltpu.VMEM((KV_HEADS, ROWS, WIDE), BF16),
            pltpu.VMEM((RANK, D_HEAD), BF16),
            pltpu.SemaphoreType.DMA((1 + KV_HEADS + HEADS,)),
        ],
        compiler_params=pltpu.CompilerParams(vmem_limit_bytes=51 * 1024 * 1024),
        cost_estimate=pl.CostEstimate(
            flops=2 * ROWS * RANK * WIDE * 4, bytes_accessed=16 * ROWS * WIDE * 2, transcendentals=0
        ),
        name="stack",
    )(frozen_query, output_gradient, columns_first, adapter_up_weight)
    arguments = (queries, grads) + (adapter_up_weight,) * 3
    light_arguments = (light_place, queries, grads, adapter_up_weight, light)
    light_outs = (wide_out, terms_out, jax.ShapeDtypeStruct((3 * RANK, 2 * ROWS), F32))
    light_call = functools.partial(
        pl.pallas_call,
        out_shape=light_outs,
        out_specs=[anywhere, vmem, vmem],
        scratch_shapes=[pltpu.VMEM((2, 1, ROWS, WIDE), BF16), pltpu.SemaphoreType.DMA((2,))],
        compiler_params=pltpu.CompilerParams(vmem_limit_bytes=28 * 1024 * 1024),
        cost_estimate=cost(2),
    )
    in_smem = [pl.BlockSpec(memory_space=pltpu.SMEM)]
    attended, terms, low_terms = light_call(
        early_kernel, in_specs=in_smem + [vmem] * 4, name="early_heads"
    )(*light_arguments)
    one, two_even, attended = lax.optimization_barrier((one, two_even, attended))
    two_odd = send(one, 1, 2)
    three = send(two_even, 1, 2)
    attended, terms, low_terms = light_call(
        light_kernel,
        in_specs=in_smem + [vmem] * 7 + [anywhere],
        input_output_aliases={8: 0},
        name="light_heads",
    )(*light_arguments, one, terms, low_terms, attended)
    back_out = jax.ShapeDtypeStruct((2 * RANK, ROWS), F32)
    back_spec = whole(2 * RANK, ROWS)
    attended, terms, mine, *backs = pl.pallas_call(
        heavy_kernel,
        out_shape=(wide_out, terms_out, jax.ShapeDtypeStruct((3 * RANK, ROWS), F32)) + (back_out,) * 3,
        grid_spec=pltpu.PrefetchScalarGridSpec(
            num_scalar_prefetch=1,
            grid=(2,),
            in_specs=common_specs()
            + [message_spec] * 6
            + [whole(3 * RANK, 2 * ROWS)]
            + [pl.BlockSpec(memory_space=pl.ANY)] * 2,
            out_specs=[wide_half(), term_half(), whole(3 * RANK, ROWS)] + [back_spec] * 3,
        ),
        input_output_aliases={13: 0, 14: 1},
        compiler_params=params(),
        cost_estimate=cost(4),
        name="heavy_heads",
    )(heavy_place, *arguments, heavy, one, one_odd, two_even, two_odd, three, low_terms, attended, terms)
    grad_low, grad_up = everywhere(terms, mine, backs)
    return (attended, grad_low, grad_up)


def solution(mesh):
    return jax.shard_map(
        shards,
        mesh=mesh,
        in_specs=(
            P("dp", "ctx", None),
            P("dp", "ctx", None),
            P("dp", "ctx", None),
            P(),
            P("dp", "ctx", None),
        ),
        out_specs=(P("dp", "ctx", None), P("dp", "ctx", None), P()),
        check_vma=False,
    )
```

```python
import functools
import math

import jax
import jax.numpy as jnp
from jax import lax
from jax.experimental import pallas as pl
from jax.experimental.pallas import tpu as pltpu
from jax.sharding import PartitionSpec as P

HEADS = 32
KV_HEADS = 4
D_HEAD = 128
RANK = 16
GROUP = 512
ROWS = 128
MESSAGE = ROWS + RANK
SHARE = HEADS // KV_HEADS
WIDE = SHARE * D_HEAD
TILES = SHARE + 2
PART = TILES // 2 * RANK
BACK = 2 * RANK
X_SIZE, Y_LOW, Z_SIZE, CORES = 4, 4, 8, 2
Y_SIZE = 2 * Y_LOW
BLOCKED = -1e30
F32 = jnp.float32
BF16 = jnp.bfloat16


def mul(a, b):
    return lax.dot_general(a, b, (((1,), (0,)), ((), ())), preferred_element_type=F32)


def mul_t(a, b):
    return lax.dot_general(a, b, (((1,), (1,)), ((), ())), preferred_element_type=F32)


def t_mul(a, b):
    return lax.dot_general(a, b, (((0,), (0,)), ((), ())), preferred_element_type=F32)


def prepare_kernel(frozen, low, up, light, heavy):
    low_q, low_k, low_v = (low[0, i * RANK : (i + 1) * RANK, :] for i in range(3))
    wide = KV_HEADS * D_HEAD
    keys = (frozen[0, :, :wide].astype(F32) + 2.0 * t_mul(low_k, up[:, :wide])).astype(BF16)
    values = (frozen[0, :, wide:].astype(F32) + 2.0 * t_mul(low_v, up[:, wide:])).astype(BF16)
    tail = jnp.concatenate([low_k, low_v, low_q, jnp.zeros((RANK, D_HEAD), BF16)], axis=1)
    half = 2 * D_HEAD

    def write(plain, moved):
        plain[:ROWS, :half] = keys[:, :half]
        plain[:ROWS, half:] = values[:, :half]
        plain[ROWS:, :] = tail
        moved[:ROWS, :half] = keys[:, half:]
        moved[:ROWS, half:] = values[:, half:]
        moved[ROWS:, :] = tail

    plain_light = lax.axis_index("ctx") % 4 < 2

    @pl.when(plain_light)
    def _():
        write(light, heavy)

    @pl.when(jnp.logical_not(plain_light))
    def _():
        write(heavy, light)


def stack_kernel(query, grad, low_all, up, queries, grads, held, low, sems):
    copies = [pltpu.make_async_copy(low_all.at[0, pl.ds(0, RANK), :], low, sems.at[0])]
    for i in range(KV_HEADS):
        wide = query.at[0, :, pl.ds(i * WIDE, WIDE)]
        copies.append(pltpu.make_async_copy(wide, held.at[i], sems.at[1 + i]))
    for i in range(HEADS):
        head = grad.at[0, :, pl.ds(i * D_HEAD, D_HEAD)]
        place = grads.at[pl.ds(i * ROWS, ROWS), :]
        copies.append(pltpu.make_async_copy(head, place, sems.at[1 + KV_HEADS + i]))
    for copy in copies:
        copy.start()
    copies[0].wait()
    for i in range(KV_HEADS):
        added = 2.0 * t_mul(low[...], up[:, i * WIDE : (i + 1) * WIDE])
        copies[1 + i].wait()
        found = (held[i].astype(F32) + added).astype(BF16)
        for k in range(SHARE):
            rows = slice((i * SHARE + k) * ROWS, (i * SHARE + k + 1) * ROWS)
            queries[rows, :] = found[:, k * D_HEAD : (k + 1) * D_HEAD]
    for copy in copies[1 + KV_HEADS :]:
        copy.wait()


def attend(place, head, all_queries, all_grads, ups, blocks, closed, attended, terms):
    up_rows, up_k, up_v = ups
    key_cols = pl.ds(pl.multiple_of(head * D_HEAD, D_HEAD), D_HEAD)
    value_cols = pl.ds(pl.multiple_of((head + 2) * D_HEAD, D_HEAD), D_HEAD)
    bias = jnp.where(place[1] == 1, 0.0, BLOCKED).astype(F32)
    scale = 1.0 / math.sqrt(D_HEAD)
    keys = jnp.concatenate([b(slice(0, ROWS), key_cols) for b in blocks], axis=0)
    values = jnp.concatenate([b(slice(0, ROWS), value_cols) for b in blocks], axis=0)
    tail = slice(ROWS, MESSAGE)
    low_k = jnp.concatenate([b(tail, slice(0, D_HEAD)) for b in blocks], axis=1)
    low_v = jnp.concatenate([b(tail, slice(D_HEAD, 2 * D_HEAD)) for b in blocks], axis=1)
    low_q = blocks[0](tail, slice(2 * D_HEAD, 3 * D_HEAD))
    keys_t = keys.T
    values_t = values.T
    wide = 2 * ROWS
    row = lax.broadcasted_iota(jnp.int32, (ROWS, wide), 0)
    col = lax.broadcasted_iota(jnp.int32, (ROWS, wide), 1)
    causal = row <= jnp.where(col >= ROWS, col - ROWS, col)
    pairs = [slice(i * wide, (i + 1) * wide) for i in range(SHARE // 2)]
    products = [(mul_t(keys, all_queries[p]), mul_t(values, all_grads[p])) for p in pairs]
    all_weights, all_scores = [], []
    for logits, prob_grad in products:
        parts = [jnp.where(causal, logits[:ROWS], BLOCKED)]
        for i, shut in enumerate(closed):
            part = logits[(i + 1) * ROWS : (i + 2) * ROWS]
            parts.append(part + bias if shut else part)
        logits = jnp.concatenate(parts, axis=0)
        peak = jnp.max(logits, axis=0, keepdims=True)
        exps = jnp.exp2((logits - peak) * (scale * math.log2(math.e)))
        weights = (exps * (1.0 / jnp.sum(exps, axis=0, keepdims=True))).astype(BF16)
        weights_f = weights.astype(F32)
        product = weights_f * prob_grad
        row_dot = jnp.sum(product, axis=0, keepdims=True)
        all_weights.append(weights)
        all_scores.append((product - weights_f * row_dot).astype(BF16))
    grad_queries = []
    for i in range(SHARE // 2):
        out_t = mul(values_t, all_weights[i])
        grad_query_t = (mul(keys_t, all_scores[i]) * scale).astype(BF16)
        for k in range(2):
            mine = slice(k * ROWS, (k + 1) * ROWS)
            attended(2 * i + k)[...] = out_t[:, mine].T.astype(BF16)
            grad_queries.append(grad_query_t[:, mine])
    stacked = jnp.concatenate(grad_queries, axis=0)
    low_grad = mul(up_rows, stacked)
    found = [2.0 * mul_t(low_q, stacked)]
    grad_keys = mul(jnp.concatenate(all_scores, axis=1), all_queries)
    grad_keys = (grad_keys * scale).astype(BF16)
    grad_values = mul(jnp.concatenate(all_weights, axis=1), all_grads).astype(BF16)
    found += [2.0 * mul(low_k, grad_keys), 2.0 * mul(low_v, grad_values)]
    found = jnp.concatenate(found, axis=1).astype(BF16)
    for tile in range(TILES):
        rows = slice(tile * RANK % PART, tile * RANK % PART + RANK)
        terms(tile * RANK // PART)[rows, :] = found[:, tile * D_HEAD : (tile + 1) * D_HEAD]
    return 2.0 * low_grad, 2.0 * mul_t(up_k, grad_keys), 2.0 * mul_t(up_v, grad_values)


def light_heads(place, query, grad, up, blocks, closed, attended, terms, low_terms, held, sems):
    sums, copies = [], []
    for head in range(2):
        chosen = place[0] * 2 + head
        rows = pl.ds(pl.multiple_of(chosen * WIDE, WIDE), WIDE)
        ups = [
            up[:, pl.ds(pl.multiple_of(first * D_HEAD + chosen * width, D_HEAD), width)]
            for first, width in ((0, WIDE), (HEADS, D_HEAD), (HEADS + KV_HEADS, D_HEAD))
        ]
        found = attend(
            place, head, query[rows, :], grad[rows, :], ups, blocks, closed,
            lambda k, head=head: held.at[head, 0, :, k * D_HEAD : (k + 1) * D_HEAD],
            lambda i, chosen=chosen: terms.at[2 * chosen + i],
        )
        sums = [a + b for a, b in zip(sums, found)] if sums else found
        copies.append(
            pltpu.make_async_copy(held.at[head], attended.at[:, :, rows], sems.at[head])
        )
        copies[-1].start()
    by_query, by_key, by_value = sums
    low_terms[...] = jnp.zeros_like(low_terms)
    reach = by_key.shape[1]
    low_terms[:RANK, :ROWS] = by_query
    low_terms[RANK : 2 * RANK, :reach] = by_key
    low_terms[2 * RANK :, :reach] = by_value
    for copy in copies:
        copy.wait()


def early_kernel(place, query, grad, up, own, attended, terms, low_terms, held, sems):
    @pl.when(place[2] == 1)
    def _():
        blocks = [lambda r, c: own[r, c]]
        light_heads(place, query, grad, up, blocks, [], attended, terms, low_terms, held, sems)


def light_kernel(
    place, query, grad, up, own, one, terms_before, low_before, _attended,
    attended, terms, low_terms, held, sems,
):
    @pl.when(place[2] == 1)
    def _():
        terms[...] = terms_before[...]
        low_terms[...] = low_before[...]

    @pl.when(place[2] == 0)
    def _():
        blocks = [lambda r, c: own[r, c], lambda r, c: one[r, c]]
        light_heads(
            place, query, grad, up, blocks, [True], attended, terms, low_terms, held, sems
        )


def heavy_kernel(
    place, query, grad, up_q, up_k, up_v, own, one_even, one_odd, two_even, two_odd, three, before,
    _attended, _terms, attended, terms, mine, back_one, back_two, back_three,
):
    odd = place[1] == 1
    blocks = [
        lambda r, c: own[r, c],
        lambda r, c: jnp.where(odd, one_odd[r, c], one_even[r, c]),
        lambda r, c: jnp.where(odd, two_odd[r, c], two_even[r, c]),
        lambda r, c: three[r, c],
    ]

    @pl.when(pl.program_id(0) == 0)
    def _():
        mine[...] = before[:, :ROWS]
        back_one[...] = before[RANK:, ROWS:]
        back_two[...] = jnp.zeros_like(back_two)
        back_three[...] = jnp.zeros_like(back_three)

    ups = (up_q[...], up_k[...], up_v[...])
    by_query, by_key, by_value = attend(
        place, pl.program_id(0), query[...], grad[...], ups, blocks, [False, False, True],
        lambda k: attended.at[0, :, k * D_HEAD : (k + 1) * D_HEAD],
        lambda i: terms.at[i],
    )
    mine[:RANK, :] += by_query
    mine[RANK : 2 * RANK, :] += by_key[:, :ROWS]
    mine[2 * RANK :, :] += by_value[:, :ROWS]
    for i, back in enumerate((back_one, back_two, back_three)):
        block = slice((i + 1) * ROWS, (i + 2) * ROWS)
        back[:RANK, :] += by_key[:, block]
        back[RANK:, :] += by_value[:, block]


def whole(*shape):
    return pl.BlockSpec(shape, lambda head, place: (0,) * len(shape))


def at_half(rows, width, first=0):
    return pl.BlockSpec((rows, width), lambda head, place: (0, first + place[0] * 2 + head))


def wide_half():
    return pl.BlockSpec((1, ROWS, WIDE), lambda head, place: (0, 0, place[0] * 2 + head))


def term_half():
    return pl.BlockSpec((2, PART, D_HEAD), lambda head, place: (place[0] * 2 + head, 0, 0))


def common_specs():
    stacked = pl.BlockSpec((SHARE * ROWS, D_HEAD), lambda head, place: (place[0] * 2 + head, 0))
    return [
        stacked,
        stacked,
        at_half(RANK, WIDE),
        at_half(RANK, D_HEAD, HEADS),
        at_half(RANK, D_HEAD, HEADS + KV_HEADS),
    ]


def params():
    return pltpu.CompilerParams(
        dimension_semantics=("arbitrary",), vmem_limit_bytes=28 * 1024 * 1024
    )


def cost(blocks):
    sizes = 16 * blocks * ROWS * ROWS
    return pl.CostEstimate(
        flops=12 * sizes * D_HEAD, bytes_accessed=6 * ROWS * WIDE * 2, transcendentals=sizes
    )


def exchange(value, groups):
    return lax.all_to_all(value, ("dp", "ctx"), 0, 0, axis_index_groups=groups)


def index_of(x, y, z, core):
    dp = y % Y_LOW * CORES + core
    return dp * (2 * X_SIZE * Z_SIZE) + (x * 2 + y // Y_LOW) * Z_SIZE + z


def lines():
    xs, ys, zs, cores = range(X_SIZE), range(Y_SIZE), range(Z_SIZE), range(CORES)
    by_x = [[index_of(x, y, z, c) for x in xs for c in cores] for y in ys for z in zs]
    by_z = [[index_of(x, y, z, c) for z in zs] for x in xs for y in ys for c in cores]
    by_y = [[index_of(x, y, z, c) for y in ys] for x in xs for z in zs for c in cores]
    return by_x, by_z, by_y


def total(parts, rows):
    return jnp.sum(parts[:, :rows, :].astype(F32), axis=0).astype(BF16)


def along_kernel(parts, back_one, back_two, back_three, out):
    rows = parts.shape[1]
    out[:, :rows, :] = jnp.broadcast_to(total(parts, rows), (Z_SIZE, rows, D_HEAD))
    out[:, rows:, :] = jnp.zeros((Z_SIZE, BACK, D_HEAD), BF16)
    z = lax.axis_index("ctx") % Z_SIZE
    for by, back in enumerate((back_one, back_two, back_three)):
        out[(z + Z_SIZE - 1 - by) % Z_SIZE, rows:, :] = back[...].astype(BF16)


def beside_kernel(parts, out, near):
    rows = parts.shape[1] - BACK
    z = lax.axis_index("ctx") % Z_SIZE
    ahead = jnp.zeros((BACK, D_HEAD), F32)
    behind = jnp.zeros((BACK, D_HEAD), F32)
    for i in range(Z_SIZE):
        came = parts[i, rows:, :].astype(F32)
        ahead = ahead + jnp.where(i > z, came, 0.0)
        behind = behind + jnp.where(i > z, 0.0, came)
    near[...] = ahead
    found = jnp.concatenate([total(parts, rows), behind.astype(BF16)], axis=0)
    out[...] = jnp.broadcast_to(found, out.shape)


def across_kernel(parts, out, near):
    rows = parts.shape[1] - BACK
    high = lax.axis_index("ctx") // Z_SIZE % 2
    y = high * Y_LOW + lax.axis_index("dp") // CORES
    came = parts[(y + Y_LOW) % Y_SIZE, rows:, :].astype(F32)
    near[...] = jnp.where(high == 1, 0.0, came)
    behind = jnp.where(high == 1, came, 0.0).astype(BF16)
    found = jnp.concatenate([total(parts, rows), behind], axis=0)
    out[...] = jnp.broadcast_to(found, out.shape)


def assemble_kernel(parts, mine, near_z, near_y, grad_up, low_grad):
    for tile in range(KV_HEADS * TILES):
        head, inside = tile // TILES, tile % TILES
        column = head * SHARE + inside if inside < SHARE else HEADS + (inside - SHARE) * KV_HEADS + head
        rows = slice(inside * RANK % PART, inside * RANK % PART + RANK)
        grad_up[:, column * D_HEAD : (column + 1) * D_HEAD] = parts[
            2 * head + inside * RANK // PART, rows, :
        ].astype(F32)
    x = lax.axis_index("ctx") // (2 * Z_SIZE)
    after = (x + 1) % X_SIZE * CORES + lax.axis_index("dp") % CORES
    low_grad[0, :RANK, :] = mine[:RANK, :]
    returned = near_z[...] + near_y[...] + parts[after, PART:, :].astype(F32)
    low_grad[0, RANK:, :] = mine[RANK:, :] + returned


def small(kernel, name, out_shape, *operands):
    return pl.pallas_call(
        kernel,
        out_shape=out_shape,
        compiler_params=pltpu.CompilerParams(vmem_limit_bytes=16 * 1024 * 1024),
        name=name,
    )(*operands)


def everywhere(terms, mine, backs):
    by_x, by_z, by_y = lines()
    sent = jax.ShapeDtypeStruct((Z_SIZE, PART + BACK, D_HEAD), BF16)
    near = jax.ShapeDtypeStruct((BACK, ROWS), F32)
    parts = small(along_kernel, "along", sent, exchange(terms, by_x), *backs)
    parts, near_z = small(beside_kernel, "beside", (sent, near), exchange(parts, by_z))
    parts, near_y = small(across_kernel, "across", (sent, near), exchange(parts, by_y))
    parts = exchange(parts, by_x)
    grad_up = jax.ShapeDtypeStruct((RANK, (HEADS + 2 * KV_HEADS) * D_HEAD), F32)
    low_grad = jax.ShapeDtypeStruct((1, 3 * RANK, ROWS), F32)
    grad_up, low_grad = small(
        assemble_kernel, "assemble", (grad_up, low_grad), parts, mine, near_z, near_y
    )
    return jnp.swapaxes(low_grad, 1, 2), grad_up


def shards(frozen_query, frozen_key_value, lowrank, adapter_up_weight, output_gradient):
    spans = lax.axis_size("ctx")
    position = lax.axis_index("ctx") % (GROUP // ROWS)
    light_half = position // 2
    odd = position % 2
    early = lax.axis_index("ctx") % Z_SIZE == 0
    light_place = jnp.stack([light_half, odd, early]).astype(jnp.int32)
    heavy_place = jnp.stack([1 - light_half, odd]).astype(jnp.int32)
    message = jax.ShapeDtypeStruct((MESSAGE, 4 * D_HEAD), BF16)
    message_spec = whole(MESSAGE, 4 * D_HEAD)
    columns_first = jnp.swapaxes(lowrank, 1, 2)
    only = lambda *shape: pl.BlockSpec(shape, lambda i: (0,) * len(shape))
    light, heavy = pl.pallas_call(
        prepare_kernel,
        out_shape=(message, message),
        grid=(1,),
        in_specs=[
            only(1, ROWS, 8 * D_HEAD),
            only(1, 3 * RANK, ROWS),
            pl.BlockSpec((RANK, 8 * D_HEAD), lambda i: (0, HEADS // 8)),
        ],
        out_specs=[only(MESSAGE, 4 * D_HEAD)] * 2,
        compiler_params=pltpu.CompilerParams(vmem_limit_bytes=56 * 1024 * 1024),
        name="prepare",
    )(frozen_key_value, columns_first, adapter_up_weight)

    def send(value, by, step=1):
        return lax.ppermute(value, "ctx", [(i, (i + by) % spans) for i in range(0, spans, step)])

    one = send(light, 1)
    two_even = send(light, 2, 2)
    wide_out = jax.ShapeDtypeStruct((1, ROWS, HEADS * D_HEAD), BF16)
    terms_out = jax.ShapeDtypeStruct((2 * KV_HEADS, PART, D_HEAD), BF16)
    stacked_out = jax.ShapeDtypeStruct((HEADS * ROWS, D_HEAD), BF16)
    vmem, anywhere = pl.BlockSpec(memory_space=pltpu.VMEM), pl.BlockSpec(memory_space=pl.ANY)
    queries, grads = pl.pallas_call(
        stack_kernel,
        out_shape=(stacked_out, stacked_out),
        in_specs=[anywhere] * 3 + [vmem],
        out_specs=[vmem] * 2,
        scratch_shapes=[
            pltpu.VMEM((KV_HEADS, ROWS, WIDE), BF16),
            pltpu.VMEM((RANK, D_HEAD), BF16),
            pltpu.SemaphoreType.DMA((1 + KV_HEADS + HEADS,)),
        ],
        compiler_params=pltpu.CompilerParams(vmem_limit_bytes=51 * 1024 * 1024),
        cost_estimate=pl.CostEstimate(
            flops=2 * ROWS * RANK * WIDE * 4, bytes_accessed=16 * ROWS * WIDE * 2, transcendentals=0
        ),
        name="stack",
    )(frozen_query, output_gradient, columns_first, adapter_up_weight)
    queries, sent = lax.optimization_barrier((queries, heavy))
    one_odd = send(sent, 1, 2)
    arguments = (queries, grads) + (adapter_up_weight,) * 3
    light_arguments = (light_place, queries, grads, adapter_up_weight, light)
    light_outs = (wide_out, terms_out, jax.ShapeDtypeStruct((3 * RANK, 2 * ROWS), F32))
    light_call = functools.partial(
        pl.pallas_call,
        out_shape=light_outs,
        out_specs=[anywhere, vmem, vmem],
        scratch_shapes=[pltpu.VMEM((2, 1, ROWS, WIDE), BF16), pltpu.SemaphoreType.DMA((2,))],
        compiler_params=pltpu.CompilerParams(vmem_limit_bytes=28 * 1024 * 1024),
        cost_estimate=cost(2),
    )
    in_smem = [pl.BlockSpec(memory_space=pltpu.SMEM)]
    attended, terms, low_terms = light_call(
        early_kernel, in_specs=in_smem + [vmem] * 4, name="early_heads"
    )(*light_arguments)
    two_even, attended = lax.optimization_barrier((two_even, attended))
    three = send(two_even, 1, 2)
    one, attended = lax.optimization_barrier((one, attended))
    two_odd = send(one, 1, 2)
    attended, terms, low_terms = light_call(
        light_kernel,
        in_specs=in_smem + [vmem] * 7 + [anywhere],
        input_output_aliases={8: 0},
        name="light_heads",
    )(*light_arguments, one, terms, low_terms, attended)
    back_out = jax.ShapeDtypeStruct((2 * RANK, ROWS), F32)
    back_spec = whole(2 * RANK, ROWS)
    attended, terms, mine, *backs = pl.pallas_call(
        heavy_kernel,
        out_shape=(wide_out, terms_out, jax.ShapeDtypeStruct((3 * RANK, ROWS), F32)) + (back_out,) * 3,
        grid_spec=pltpu.PrefetchScalarGridSpec(
            num_scalar_prefetch=1,
            grid=(2,),
            in_specs=common_specs()
            + [message_spec] * 6
            + [whole(3 * RANK, 2 * ROWS)]
            + [pl.BlockSpec(memory_space=pl.ANY)] * 2,
            out_specs=[wide_half(), term_half(), whole(3 * RANK, ROWS)] + [back_spec] * 3,
        ),
        input_output_aliases={13: 0, 14: 1},
        compiler_params=params(),
        cost_estimate=cost(4),
        name="heavy_heads",
    )(heavy_place, *arguments, heavy, one, one_odd, two_even, two_odd, three, low_terms, attended, terms)
    grad_low, grad_up = everywhere(terms, mine, backs)
    return (attended, grad_low, grad_up)


def solution(mesh):
    return jax.shard_map(
        shards,
        mesh=mesh,
        in_specs=(
            P("dp", "ctx", None),
            P("dp", "ctx", None),
            P("dp", "ctx", None),
            P(),
            P("dp", "ctx", None),
        ),
        out_specs=(P("dp", "ctx", None), P("dp", "ctx", None), P()),
        check_vma=False,
    )
```

```python
import math

import jax
import jax.numpy as jnp
from jax import lax
from jax.experimental import pallas as pl
from jax.experimental.pallas import tpu as pltpu
from jax.sharding import PartitionSpec as P

HEADS = 32
KV_HEADS = 4
D_HEAD = 128
RANK = 16
GROUP = 512
ROWS = 128
MESSAGE = ROWS + RANK
SHARE = HEADS // KV_HEADS
WIDE = SHARE * D_HEAD
TILES = SHARE + 2
PART = TILES // 2 * RANK
BACK = 2 * RANK
X_SIZE, Y_LOW, Z_SIZE, CORES = 4, 4, 8, 2
Y_SIZE = 2 * Y_LOW
BLOCKED = -1e30
F32 = jnp.float32
BF16 = jnp.bfloat16


def mul(a, b):
    return lax.dot_general(a, b, (((1,), (0,)), ((), ())), preferred_element_type=F32)


def mul_t(a, b):
    return lax.dot_general(a, b, (((1,), (1,)), ((), ())), preferred_element_type=F32)


def t_mul(a, b):
    return lax.dot_general(a, b, (((0,), (0,)), ((), ())), preferred_element_type=F32)


def prepare_kernel(frozen, low, up, light, heavy):
    low_k, low_v = low[0, RANK : 2 * RANK, :], low[0, 2 * RANK :, :]
    wide = KV_HEADS * D_HEAD
    keys = (frozen[0, :, :wide].astype(F32) + 2.0 * t_mul(low_k, up[:, :wide])).astype(BF16)
    values = (frozen[0, :, wide:].astype(F32) + 2.0 * t_mul(low_v, up[:, wide:])).astype(BF16)
    tail = jnp.concatenate([low_k, low_v, jnp.zeros((RANK, 2 * D_HEAD), BF16)], axis=1)
    half = 2 * D_HEAD

    def write(plain, moved):
        plain[:ROWS, :half] = keys[:, :half]
        plain[:ROWS, half:] = values[:, :half]
        plain[ROWS:, :] = tail
        moved[:ROWS, :half] = keys[:, half:]
        moved[:ROWS, half:] = values[:, half:]
        moved[ROWS:, :] = tail

    plain_light = lax.axis_index("ctx") % 4 < 2

    @pl.when(plain_light)
    def _():
        write(light, heavy)

    @pl.when(jnp.logical_not(plain_light))
    def _():
        write(heavy, light)


def stack_kernel(query, grad, low_all, up, queries, grads, held, low, sems):
    copies = [pltpu.make_async_copy(low_all.at[0, pl.ds(0, RANK), :], low, sems.at[0])]
    for i in range(KV_HEADS):
        wide = query.at[0, :, pl.ds(i * WIDE, WIDE)]
        copies.append(pltpu.make_async_copy(wide, held.at[i], sems.at[1 + i]))
    for i in range(HEADS):
        head = grad.at[0, :, pl.ds(i * D_HEAD, D_HEAD)]
        place = grads.at[pl.ds(i * ROWS, ROWS), :]
        copies.append(pltpu.make_async_copy(head, place, sems.at[1 + KV_HEADS + i]))
    for copy in copies:
        copy.start()
    copies[0].wait()
    for i in range(KV_HEADS):
        added = 2.0 * t_mul(low[...], up[:, i * WIDE : (i + 1) * WIDE])
        copies[1 + i].wait()
        found = (held[i].astype(F32) + added).astype(BF16)
        for k in range(SHARE):
            rows = slice((i * SHARE + k) * ROWS, (i * SHARE + k + 1) * ROWS)
            queries[rows, :] = found[:, k * D_HEAD : (k + 1) * D_HEAD]
    for copy in copies[1 + KV_HEADS :]:
        copy.wait()


def attend(place, query, grad, low, up_q, up_k, up_v, blocks, closed, attended, terms):
    head = pl.program_id(0)
    key_cols = pl.ds(pl.multiple_of(head * D_HEAD, D_HEAD), D_HEAD)
    value_cols = pl.ds(pl.multiple_of((head + 2) * D_HEAD, D_HEAD), D_HEAD)
    bias = jnp.where(place[1] == 1, 0.0, BLOCKED).astype(F32)
    scale = 1.0 / math.sqrt(D_HEAD)
    keys = jnp.concatenate([b(slice(0, ROWS), key_cols) for b in blocks], axis=0)
    values = jnp.concatenate([b(slice(0, ROWS), value_cols) for b in blocks], axis=0)
    tail = slice(ROWS, MESSAGE)
    low_k = jnp.concatenate([b(tail, slice(0, D_HEAD)) for b in blocks], axis=1)
    low_v = jnp.concatenate([b(tail, slice(D_HEAD, 2 * D_HEAD)) for b in blocks], axis=1)
    low_q = low[0, :RANK, :]
    keys_t = keys.T
    values_t = values.T
    up_rows = up_q[...]
    wide = 2 * ROWS
    row = lax.broadcasted_iota(jnp.int32, (ROWS, wide), 0)
    col = lax.broadcasted_iota(jnp.int32, (ROWS, wide), 1)
    causal = row <= jnp.where(col >= ROWS, col - ROWS, col)
    sides = [slice(h * D_HEAD, (h + 1) * D_HEAD) for h in range(SHARE)]
    all_queries = query[...]
    all_grads = grad[...]
    pairs = [slice(i * wide, (i + 1) * wide) for i in range(SHARE // 2)]
    products = [(mul_t(keys, all_queries[p]), mul_t(values, all_grads[p])) for p in pairs]
    all_weights, all_scores = [], []
    for logits, prob_grad in products:
        parts = [jnp.where(causal, logits[:ROWS], BLOCKED)]
        for i, shut in enumerate(closed):
            part = logits[(i + 1) * ROWS : (i + 2) * ROWS]
            parts.append(part + bias if shut else part)
        logits = jnp.concatenate(parts, axis=0)
        peak = jnp.max(logits, axis=0, keepdims=True)
        exps = jnp.exp2((logits - peak) * (scale * math.log2(math.e)))
        weights = (exps * (1.0 / jnp.sum(exps, axis=0, keepdims=True))).astype(BF16)
        weights_f = weights.astype(F32)
        product = weights_f * prob_grad
        row_dot = jnp.sum(product, axis=0, keepdims=True)
        all_weights.append(weights)
        all_scores.append((product - weights_f * row_dot).astype(BF16))
    grad_queries = []
    for i in range(SHARE // 2):
        out_t = mul(values_t, all_weights[i])
        grad_query_t = (mul(keys_t, all_scores[i]) * scale).astype(BF16)
        for k in range(2):
            mine = slice(k * ROWS, (k + 1) * ROWS)
            attended[0, :, sides[2 * i + k]] = out_t[:, mine].T.astype(BF16)
            grad_queries.append(grad_query_t[:, mine])
    stacked = jnp.concatenate(grad_queries, axis=0)
    low_grad = mul(up_rows, stacked)
    found = [2.0 * mul_t(low_q, stacked)]
    grad_keys = mul(jnp.concatenate(all_scores, axis=1), all_queries)
    grad_keys = (grad_keys * scale).astype(BF16)
    grad_values = mul(jnp.concatenate(all_weights, axis=1), all_grads).astype(BF16)
    found += [2.0 * mul(low_k, grad_keys), 2.0 * mul(low_v, grad_values)]
    found = jnp.concatenate(found, axis=1).astype(BF16)
    for tile in range(TILES):
        rows = slice(tile * RANK % PART, tile * RANK % PART + RANK)
        terms[tile * RANK // PART, rows, :] = found[:, tile * D_HEAD : (tile + 1) * D_HEAD]
    return 2.0 * low_grad, 2.0 * mul_t(up_k[...], grad_keys), 2.0 * mul_t(up_v[...], grad_values)


def light_kernel(place, query, grad, low, up_q, up_k, up_v, own, one, attended, terms, low_terms):
    blocks = [lambda r, c: own[r, c], lambda r, c: one[r, c]]
    by_query, by_key, by_value = attend(
        place, query, grad, low, up_q, up_k, up_v, blocks, [True], attended, terms
    )
    found = jnp.concatenate(
        [jnp.concatenate([by_query, jnp.zeros_like(by_query)], axis=1), by_key, by_value], axis=0
    )

    @pl.when(pl.program_id(0) == 0)
    def _():
        low_terms[...] = found

    @pl.when(pl.program_id(0) != 0)
    def _():
        low_terms[...] += found


def heavy_kernel(
    place, query, grad, low, up_q, up_k, up_v, own, one_even, one_odd, two_even, two_odd, three, before,
    _attended, _terms, attended, terms, mine, back_one, back_two, back_three,
):
    odd = place[1] == 1
    blocks = [
        lambda r, c: own[r, c],
        lambda r, c: jnp.where(odd, one_odd[r, c], one_even[r, c]),
        lambda r, c: jnp.where(odd, two_odd[r, c], two_even[r, c]),
        lambda r, c: three[r, c],
    ]

    @pl.when(pl.program_id(0) == 0)
    def _():
        mine[...] = before[:, :ROWS]
        back_one[...] = before[RANK:, ROWS:]
        back_two[...] = jnp.zeros_like(back_two)
        back_three[...] = jnp.zeros_like(back_three)

    by_query, by_key, by_value = attend(
        place, query, grad, low, up_q, up_k, up_v, blocks, [False, False, True], attended, terms
    )
    mine[:RANK, :] += by_query
    mine[RANK : 2 * RANK, :] += by_key[:, :ROWS]
    mine[2 * RANK :, :] += by_value[:, :ROWS]
    for i, back in enumerate((back_one, back_two, back_three)):
        block = slice((i + 1) * ROWS, (i + 2) * ROWS)
        back[:RANK, :] += by_key[:, block]
        back[RANK:, :] += by_value[:, block]


def whole(*shape):
    return pl.BlockSpec(shape, lambda head, place: (0,) * len(shape))


def at_half(rows, width, first=0):
    return pl.BlockSpec((rows, width), lambda head, place: (0, first + place[0] * 2 + head))


def wide_half():
    return pl.BlockSpec((1, ROWS, WIDE), lambda head, place: (0, 0, place[0] * 2 + head))


def term_half():
    return pl.BlockSpec((2, PART, D_HEAD), lambda head, place: (place[0] * 2 + head, 0, 0))


def common_specs():
    stacked = pl.BlockSpec((SHARE * ROWS, D_HEAD), lambda head, place: (place[0] * 2 + head, 0))
    return [
        stacked,
        stacked,
        whole(1, 3 * RANK, ROWS),
        at_half(RANK, WIDE),
        at_half(RANK, D_HEAD, HEADS),
        at_half(RANK, D_HEAD, HEADS + KV_HEADS),
    ]


def params():
    return pltpu.CompilerParams(
        dimension_semantics=("arbitrary",), vmem_limit_bytes=28 * 1024 * 1024
    )


def cost(blocks):
    sizes = 16 * blocks * ROWS * ROWS
    return pl.CostEstimate(
        flops=12 * sizes * D_HEAD, bytes_accessed=6 * ROWS * WIDE * 2, transcendentals=sizes
    )


def exchange(value, groups):
    return lax.all_to_all(value, ("dp", "ctx"), 0, 0, axis_index_groups=groups)


def index_of(x, y, z, core):
    dp = y % Y_LOW * CORES + core
    return dp * (2 * X_SIZE * Z_SIZE) + (x * 2 + y // Y_LOW) * Z_SIZE + z


def lines():
    xs, ys, zs, cores = range(X_SIZE), range(Y_SIZE), range(Z_SIZE), range(CORES)
    by_x = [[index_of(x, y, z, c) for x in xs for c in cores] for y in ys for z in zs]
    by_z = [[index_of(x, y, z, c) for z in zs] for x in xs for y in ys for c in cores]
    by_y = [[index_of(x, y, z, c) for y in ys] for x in xs for z in zs for c in cores]
    return by_x, by_z, by_y


def total(parts, rows):
    return jnp.sum(parts[:, :rows, :].astype(F32), axis=0).astype(BF16)


def along_kernel(parts, back_one, back_two, back_three, out):
    rows = parts.shape[1]
    out[:, :rows, :] = jnp.broadcast_to(total(parts, rows), (Z_SIZE, rows, D_HEAD))
    out[:, rows:, :] = jnp.zeros((Z_SIZE, BACK, D_HEAD), BF16)
    z = lax.axis_index("ctx") % Z_SIZE
    for by, back in enumerate((back_one, back_two, back_three)):
        out[(z + Z_SIZE - 1 - by) % Z_SIZE, rows:, :] = back[...].astype(BF16)


def beside_kernel(parts, out, near):
    rows = parts.shape[1] - BACK
    z = lax.axis_index("ctx") % Z_SIZE
    ahead = jnp.zeros((BACK, D_HEAD), F32)
    behind = jnp.zeros((BACK, D_HEAD), F32)
    for i in range(Z_SIZE):
        came = parts[i, rows:, :].astype(F32)
        ahead = ahead + jnp.where(i > z, came, 0.0)
        behind = behind + jnp.where(i > z, 0.0, came)
    near[...] = ahead
    found = jnp.concatenate([total(parts, rows), behind.astype(BF16)], axis=0)
    out[...] = jnp.broadcast_to(found, out.shape)


def across_kernel(parts, out, near):
    rows = parts.shape[1] - BACK
    high = lax.axis_index("ctx") // Z_SIZE % 2
    y = high * Y_LOW + lax.axis_index("dp") // CORES
    came = parts[(y + Y_LOW) % Y_SIZE, rows:, :].astype(F32)
    near[...] = jnp.where(high == 1, 0.0, came)
    behind = jnp.where(high == 1, came, 0.0).astype(BF16)
    found = jnp.concatenate([total(parts, rows), behind], axis=0)
    out[...] = jnp.broadcast_to(found, out.shape)


def assemble_kernel(parts, mine, near_z, near_y, grad_up, low_grad):
    for tile in range(KV_HEADS * TILES):
        head, inside = tile // TILES, tile % TILES
        column = head * SHARE + inside if inside < SHARE else HEADS + (inside - SHARE) * KV_HEADS + head
        rows = slice(inside * RANK % PART, inside * RANK % PART + RANK)
        grad_up[:, column * D_HEAD : (column + 1) * D_HEAD] = parts[
            2 * head + inside * RANK // PART, rows, :
        ].astype(F32)
    x = lax.axis_index("ctx") // (2 * Z_SIZE)
    after = (x + 1) % X_SIZE * CORES + lax.axis_index("dp") % CORES
    low_grad[0, :RANK, :] = mine[:RANK, :]
    returned = near_z[...] + near_y[...] + parts[after, PART:, :].astype(F32)
    low_grad[0, RANK:, :] = mine[RANK:, :] + returned


def small(kernel, name, out_shape, *operands):
    return pl.pallas_call(
        kernel,
        out_shape=out_shape,
        compiler_params=pltpu.CompilerParams(vmem_limit_bytes=16 * 1024 * 1024),
        name=name,
    )(*operands)


def everywhere(terms, mine, backs):
    by_x, by_z, by_y = lines()
    sent = jax.ShapeDtypeStruct((Z_SIZE, PART + BACK, D_HEAD), BF16)
    near = jax.ShapeDtypeStruct((BACK, ROWS), F32)
    parts = small(along_kernel, "along", sent, exchange(terms, by_x), *backs)
    parts, near_z = small(beside_kernel, "beside", (sent, near), exchange(parts, by_z))
    parts, near_y = small(across_kernel, "across", (sent, near), exchange(parts, by_y))
    parts = exchange(parts, by_x)
    grad_up = jax.ShapeDtypeStruct((RANK, (HEADS + 2 * KV_HEADS) * D_HEAD), F32)
    low_grad = jax.ShapeDtypeStruct((1, 3 * RANK, ROWS), F32)
    grad_up, low_grad = small(
        assemble_kernel, "assemble", (grad_up, low_grad), parts, mine, near_z, near_y
    )
    return jnp.swapaxes(low_grad, 1, 2), grad_up


def shards(frozen_query, frozen_key_value, lowrank, adapter_up_weight, output_gradient):
    spans = lax.axis_size("ctx")
    position = lax.axis_index("ctx") % (GROUP // ROWS)
    light_half = position // 2
    odd = position % 2
    light_place = jnp.stack([light_half, odd]).astype(jnp.int32)
    heavy_place = jnp.stack([1 - light_half, odd]).astype(jnp.int32)
    message = jax.ShapeDtypeStruct((MESSAGE, 4 * D_HEAD), BF16)
    message_spec = whole(MESSAGE, 4 * D_HEAD)
    columns_first = jnp.swapaxes(lowrank, 1, 2)
    only = lambda *shape: pl.BlockSpec(shape, lambda i: (0,) * len(shape))
    light, heavy = pl.pallas_call(
        prepare_kernel,
        out_shape=(message, message),
        grid=(1,),
        in_specs=[
            only(1, ROWS, 8 * D_HEAD),
            only(1, 3 * RANK, ROWS),
            pl.BlockSpec((RANK, 8 * D_HEAD), lambda i: (0, HEADS // 8)),
        ],
        out_specs=[only(MESSAGE, 4 * D_HEAD)] * 2,
        compiler_params=pltpu.CompilerParams(vmem_limit_bytes=56 * 1024 * 1024),
        name="prepare",
    )(frozen_key_value, columns_first, adapter_up_weight)

    def send(value, by, step=1):
        return lax.ppermute(value, "ctx", [(i, (i + by) % spans) for i in range(0, spans, step)])

    one = send(light, 1)
    two_even = send(light, 2, 2)
    one_odd = send(heavy, 1, 2)
    two_odd = send(one, 1, 2)
    three = send(two_even, 1, 2)
    wide_out = jax.ShapeDtypeStruct((1, ROWS, HEADS * D_HEAD), BF16)
    terms_out = jax.ShapeDtypeStruct((2 * KV_HEADS, PART, D_HEAD), BF16)
    stacked_out = jax.ShapeDtypeStruct((HEADS * ROWS, D_HEAD), BF16)
    vmem, anywhere = pl.BlockSpec(memory_space=pltpu.VMEM), pl.BlockSpec(memory_space=pl.ANY)
    queries, grads = pl.pallas_call(
        stack_kernel,
        out_shape=(stacked_out, stacked_out),
        in_specs=[anywhere] * 3 + [vmem],
        out_specs=[vmem] * 2,
        scratch_shapes=[
            pltpu.VMEM((KV_HEADS, ROWS, WIDE), BF16),
            pltpu.VMEM((RANK, D_HEAD), BF16),
            pltpu.SemaphoreType.DMA((1 + KV_HEADS + HEADS,)),
        ],
        compiler_params=pltpu.CompilerParams(vmem_limit_bytes=51 * 1024 * 1024),
        cost_estimate=pl.CostEstimate(
            flops=2 * ROWS * RANK * WIDE * 4, bytes_accessed=16 * ROWS * WIDE * 2, transcendentals=0
        ),
        name="stack",
    )(frozen_query, output_gradient, columns_first, adapter_up_weight)
    arguments = (queries, grads, columns_first) + (adapter_up_weight,) * 3
    attended, terms, low_terms = pl.pallas_call(
        light_kernel,
        out_shape=(wide_out, terms_out, jax.ShapeDtypeStruct((3 * RANK, 2 * ROWS), F32)),
        grid_spec=pltpu.PrefetchScalarGridSpec(
            num_scalar_prefetch=1,
            grid=(2,),
            in_specs=common_specs() + [message_spec] * 2,
            out_specs=[wide_half(), term_half(), whole(3 * RANK, 2 * ROWS)],
        ),
        compiler_params=params(),
        cost_estimate=cost(2),
        name="light_heads",
    )(light_place, *arguments, light, one)
    back_out = jax.ShapeDtypeStruct((2 * RANK, ROWS), F32)
    back_spec = whole(2 * RANK, ROWS)
    attended, terms, mine, *backs = pl.pallas_call(
        heavy_kernel,
        out_shape=(wide_out, terms_out, jax.ShapeDtypeStruct((3 * RANK, ROWS), F32)) + (back_out,) * 3,
        grid_spec=pltpu.PrefetchScalarGridSpec(
            num_scalar_prefetch=1,
            grid=(2,),
            in_specs=common_specs()
            + [message_spec] * 6
            + [whole(3 * RANK, 2 * ROWS)]
            + [pl.BlockSpec(memory_space=pl.ANY)] * 2,
            out_specs=[wide_half(), term_half(), whole(3 * RANK, ROWS)] + [back_spec] * 3,
        ),
        input_output_aliases={14: 0, 15: 1},
        compiler_params=params(),
        cost_estimate=cost(4),
        name="heavy_heads",
    )(heavy_place, *arguments, heavy, one, one_odd, two_even, two_odd, three, low_terms, attended, terms)
    grad_low, grad_up = everywhere(terms, mine, backs)
    return (attended, grad_low, grad_up)


def solution(mesh):
    return jax.shard_map(
        shards,
        mesh=mesh,
        in_specs=(
            P("dp", "ctx", None),
            P("dp", "ctx", None),
            P("dp", "ctx", None),
            P(),
            P("dp", "ctx", None),
        ),
        out_specs=(P("dp", "ctx", None), P("dp", "ctx", None), P()),
        check_vma=False,
    )
```

```python
import functools
import math

import jax
import jax.numpy as jnp
from jax import lax
from jax.experimental import pallas as pl
from jax.experimental.pallas import tpu as pltpu
from jax.sharding import PartitionSpec as P

HEADS = 32
KV_HEADS = 4
D_HEAD = 128
RANK = 16
GROUP = 512
ROWS = 128
MESSAGE = ROWS + RANK
SHARE = HEADS // KV_HEADS
WIDE = SHARE * D_HEAD
TILES = SHARE + 2
PART = TILES // 2 * RANK
BACK = 2 * RANK
X_SIZE, Y_LOW, Z_SIZE, CORES = 4, 4, 8, 2
Y_SIZE = 2 * Y_LOW
BLOCKED = -1e30
F32 = jnp.float32
BF16 = jnp.bfloat16


def mul(a, b):
    return lax.dot_general(a, b, (((1,), (0,)), ((), ())), preferred_element_type=F32)


def mul_t(a, b):
    return lax.dot_general(a, b, (((1,), (1,)), ((), ())), preferred_element_type=F32)


def t_mul(a, b):
    return lax.dot_general(a, b, (((0,), (0,)), ((), ())), preferred_element_type=F32)


def prepare_kernel(frozen, low, up, light, heavy):
    low_q, low_k, low_v = (low[0, i * RANK : (i + 1) * RANK, :] for i in range(3))
    wide = KV_HEADS * D_HEAD
    keys = (frozen[0, :, :wide].astype(F32) + 2.0 * t_mul(low_k, up[:, :wide])).astype(BF16)
    values = (frozen[0, :, wide:].astype(F32) + 2.0 * t_mul(low_v, up[:, wide:])).astype(BF16)
    tail = jnp.concatenate([low_k, low_v, low_q, jnp.zeros((RANK, D_HEAD), BF16)], axis=1)
    half = 2 * D_HEAD

    def write(plain, moved):
        plain[:ROWS, :half] = keys[:, :half]
        plain[:ROWS, half:] = values[:, :half]
        plain[ROWS:, :] = tail
        moved[:ROWS, :half] = keys[:, half:]
        moved[:ROWS, half:] = values[:, half:]
        moved[ROWS:, :] = tail

    plain_light = lax.axis_index("ctx") % 4 < 2

    @pl.when(plain_light)
    def _():
        write(light, heavy)

    @pl.when(jnp.logical_not(plain_light))
    def _():
        write(heavy, light)


def stack_kernel(query, grad, low_all, up, queries, grads, held, low, sems):
    copies = [pltpu.make_async_copy(low_all.at[0, pl.ds(0, RANK), :], low, sems.at[0])]
    for i in range(KV_HEADS):
        wide = query.at[0, :, pl.ds(i * WIDE, WIDE)]
        copies.append(pltpu.make_async_copy(wide, held.at[i], sems.at[1 + i]))
    for i in range(HEADS):
        head = grad.at[0, :, pl.ds(i * D_HEAD, D_HEAD)]
        place = grads.at[pl.ds(i * ROWS, ROWS), :]
        copies.append(pltpu.make_async_copy(head, place, sems.at[1 + KV_HEADS + i]))
    for copy in copies:
        copy.start()
    copies[0].wait()
    for i in range(KV_HEADS):
        added = 2.0 * t_mul(low[...], up[:, i * WIDE : (i + 1) * WIDE])
        copies[1 + i].wait()
        found = (held[i].astype(F32) + added).astype(BF16)
        for k in range(SHARE):
            rows = slice((i * SHARE + k) * ROWS, (i * SHARE + k + 1) * ROWS)
            queries[rows, :] = found[:, k * D_HEAD : (k + 1) * D_HEAD]
    for copy in copies[1 + KV_HEADS :]:
        copy.wait()


def attend(place, head, all_queries, all_grads, ups, blocks, closed, attended, terms):
    up_rows, up_k, up_v = ups
    key_cols = pl.ds(pl.multiple_of(head * D_HEAD, D_HEAD), D_HEAD)
    value_cols = pl.ds(pl.multiple_of((head + 2) * D_HEAD, D_HEAD), D_HEAD)
    bias = jnp.where(place[1] == 1, 0.0, BLOCKED).astype(F32)
    scale = 1.0 / math.sqrt(D_HEAD)
    keys = jnp.concatenate([b(slice(0, ROWS), key_cols) for b in blocks], axis=0)
    values = jnp.concatenate([b(slice(0, ROWS), value_cols) for b in blocks], axis=0)
    tail = slice(ROWS, MESSAGE)
    low_k = jnp.concatenate([b(tail, slice(0, D_HEAD)) for b in blocks], axis=1)
    low_v = jnp.concatenate([b(tail, slice(D_HEAD, 2 * D_HEAD)) for b in blocks], axis=1)
    low_q = blocks[0](tail, slice(2 * D_HEAD, 3 * D_HEAD))
    keys_t = keys.T
    values_t = values.T
    wide = 2 * ROWS
    row = lax.broadcasted_iota(jnp.int32, (ROWS, wide), 0)
    col = lax.broadcasted_iota(jnp.int32, (ROWS, wide), 1)
    causal = row <= jnp.where(col >= ROWS, col - ROWS, col)
    pairs = [slice(i * wide, (i + 1) * wide) for i in range(SHARE // 2)]
    products = [(mul_t(keys, all_queries[p]), mul_t(values, all_grads[p])) for p in pairs]
    all_weights, all_scores = [], []
    for logits, prob_grad in products:
        parts = [jnp.where(causal, logits[:ROWS], BLOCKED)]
        for i, shut in enumerate(closed):
            part = logits[(i + 1) * ROWS : (i + 2) * ROWS]
            parts.append(part + bias if shut else part)
        logits = jnp.concatenate(parts, axis=0)
        peak = jnp.max(logits, axis=0, keepdims=True)
        exps = jnp.exp2((logits - peak) * (scale * math.log2(math.e)))
        weights = (exps * (1.0 / jnp.sum(exps, axis=0, keepdims=True))).astype(BF16)
        weights_f = weights.astype(F32)
        product = weights_f * prob_grad
        row_dot = jnp.sum(product, axis=0, keepdims=True)
        all_weights.append(weights)
        all_scores.append((product - weights_f * row_dot).astype(BF16))
    grad_queries = []
    for i in range(SHARE // 2):
        out_t = mul(values_t, all_weights[i])
        grad_query_t = (mul(keys_t, all_scores[i]) * scale).astype(BF16)
        for k in range(2):
            mine = slice(k * ROWS, (k + 1) * ROWS)
            attended(2 * i + k)[...] = out_t[:, mine].T.astype(BF16)
            grad_queries.append(grad_query_t[:, mine])
    stacked = jnp.concatenate(grad_queries, axis=0)
    low_grad = mul(up_rows, stacked)
    found = [2.0 * mul_t(low_q, stacked)]
    grad_keys = mul(jnp.concatenate(all_scores, axis=1), all_queries)
    grad_keys = (grad_keys * scale).astype(BF16)
    grad_values = mul(jnp.concatenate(all_weights, axis=1), all_grads).astype(BF16)
    found += [2.0 * mul(low_k, grad_keys), 2.0 * mul(low_v, grad_values)]
    found = jnp.concatenate(found, axis=1).astype(BF16)
    for tile in range(TILES):
        rows = slice(tile * RANK % PART, tile * RANK % PART + RANK)
        terms(tile * RANK // PART)[rows, :] = found[:, tile * D_HEAD : (tile + 1) * D_HEAD]
    return 2.0 * low_grad, 2.0 * mul_t(up_k, grad_keys), 2.0 * mul_t(up_v, grad_values)


def light_heads(place, query, grad, up, blocks, closed, attended, terms, low_terms, held, sems):
    sums, copies = [], []
    for head in range(2):
        chosen = place[0] * 2 + head
        rows = pl.ds(pl.multiple_of(chosen * WIDE, WIDE), WIDE)
        ups = [
            up[:, pl.ds(pl.multiple_of(first * D_HEAD + chosen * width, D_HEAD), width)]
            for first, width in ((0, WIDE), (HEADS, D_HEAD), (HEADS + KV_HEADS, D_HEAD))
        ]
        found = attend(
            place, head, query[rows, :], grad[rows, :], ups, blocks, closed,
            lambda k, head=head: held.at[head, 0, :, k * D_HEAD : (k + 1) * D_HEAD],
            lambda i, chosen=chosen: terms.at[2 * chosen + i],
        )
        sums = [a + b for a, b in zip(sums, found)] if sums else found
        copies.append(
            pltpu.make_async_copy(held.at[head], attended.at[:, :, rows], sems.at[head])
        )
        copies[-1].start()
    by_query, by_key, by_value = sums
    low_terms[...] = jnp.zeros_like(low_terms)
    reach = by_key.shape[1]
    low_terms[:RANK, :ROWS] = by_query
    low_terms[RANK : 2 * RANK, :reach] = by_key
    low_terms[2 * RANK :, :reach] = by_value
    for copy in copies:
        copy.wait()


def light_kernel(place, query, grad, up, own, one, attended, terms, low_terms, held, sems):
    blocks = [lambda r, c: own[r, c], lambda r, c: one[r, c]]
    light_heads(place, query, grad, up, blocks, [True], attended, terms, low_terms, held, sems)


def heavy_kernel(
    place, query, grad, up_q, up_k, up_v, own, one_even, one_odd, two_even, two_odd, three, before,
    _attended, _terms, attended, terms, mine, back_one, back_two, back_three,
):
    odd = place[1] == 1
    blocks = [
        lambda r, c: own[r, c],
        lambda r, c: jnp.where(odd, one_odd[r, c], one_even[r, c]),
        lambda r, c: jnp.where(odd, two_odd[r, c], two_even[r, c]),
        lambda r, c: three[r, c],
    ]

    @pl.when(pl.program_id(0) == 0)
    def _():
        mine[...] = before[:, :ROWS]
        back_one[...] = before[RANK:, ROWS:]
        back_two[...] = jnp.zeros_like(back_two)
        back_three[...] = jnp.zeros_like(back_three)

    ups = (up_q[...], up_k[...], up_v[...])
    by_query, by_key, by_value = attend(
        place, pl.program_id(0), query[...], grad[...], ups, blocks, [False, False, True],
        lambda k: attended.at[0, :, k * D_HEAD : (k + 1) * D_HEAD],
        lambda i: terms.at[i],
    )
    mine[:RANK, :] += by_query
    mine[RANK : 2 * RANK, :] += by_key[:, :ROWS]
    mine[2 * RANK :, :] += by_value[:, :ROWS]
    for i, back in enumerate((back_one, back_two, back_three)):
        block = slice((i + 1) * ROWS, (i + 2) * ROWS)
        back[:RANK, :] += by_key[:, block]
        back[RANK:, :] += by_value[:, block]


def whole(*shape):
    return pl.BlockSpec(shape, lambda head, place: (0,) * len(shape))


def at_half(rows, width, first=0):
    return pl.BlockSpec((rows, width), lambda head, place: (0, first + place[0] * 2 + head))


def wide_half():
    return pl.BlockSpec((1, ROWS, WIDE), lambda head, place: (0, 0, place[0] * 2 + head))


def term_half():
    return pl.BlockSpec((2, PART, D_HEAD), lambda head, place: (place[0] * 2 + head, 0, 0))


def common_specs():
    stacked = pl.BlockSpec((SHARE * ROWS, D_HEAD), lambda head, place: (place[0] * 2 + head, 0))
    return [
        stacked,
        stacked,
        at_half(RANK, WIDE),
        at_half(RANK, D_HEAD, HEADS),
        at_half(RANK, D_HEAD, HEADS + KV_HEADS),
    ]


def params():
    return pltpu.CompilerParams(
        dimension_semantics=("arbitrary",), vmem_limit_bytes=28 * 1024 * 1024
    )


def cost(blocks):
    sizes = 16 * blocks * ROWS * ROWS
    return pl.CostEstimate(
        flops=12 * sizes * D_HEAD, bytes_accessed=6 * ROWS * WIDE * 2, transcendentals=sizes
    )


def exchange(value, groups):
    return lax.all_to_all(value, ("dp", "ctx"), 0, 0, axis_index_groups=groups)


def index_of(x, y, z, core):
    dp = y % Y_LOW * CORES + core
    return dp * (2 * X_SIZE * Z_SIZE) + (x * 2 + y // Y_LOW) * Z_SIZE + z


def lines():
    xs, ys, zs, cores = range(X_SIZE), range(Y_SIZE), range(Z_SIZE), range(CORES)
    by_x = [[index_of(x, y, z, c) for x in xs for c in cores] for y in ys for z in zs]
    by_z = [[index_of(x, y, z, c) for z in zs] for x in xs for y in ys for c in cores]
    by_y = [[index_of(x, y, z, c) for y in ys] for x in xs for z in zs for c in cores]
    return by_x, by_z, by_y


def total(parts, rows):
    return jnp.sum(parts[:, :rows, :].astype(F32), axis=0).astype(BF16)


def along_kernel(parts, back_one, back_two, back_three, out):
    rows = parts.shape[1]
    out[:, :rows, :] = jnp.broadcast_to(total(parts, rows), (Z_SIZE, rows, D_HEAD))
    out[:, rows:, :] = jnp.zeros((Z_SIZE, BACK, D_HEAD), BF16)
    z = lax.axis_index("ctx") % Z_SIZE
    for by, back in enumerate((back_one, back_two, back_three)):
        out[(z + Z_SIZE - 1 - by) % Z_SIZE, rows:, :] = back[...].astype(BF16)


def beside_kernel(parts, out, near):
    rows = parts.shape[1] - BACK
    z = lax.axis_index("ctx") % Z_SIZE
    ahead = jnp.zeros((BACK, D_HEAD), F32)
    behind = jnp.zeros((BACK, D_HEAD), F32)
    for i in range(Z_SIZE):
        came = parts[i, rows:, :].astype(F32)
        ahead = ahead + jnp.where(i > z, came, 0.0)
        behind = behind + jnp.where(i > z, 0.0, came)
    near[...] = ahead
    found = jnp.concatenate([total(parts, rows), behind.astype(BF16)], axis=0)
    out[...] = jnp.broadcast_to(found, out.shape)


def across_kernel(parts, out, near):
    rows = parts.shape[1] - BACK
    high = lax.axis_index("ctx") // Z_SIZE % 2
    y = high * Y_LOW + lax.axis_index("dp") // CORES
    came = parts[(y + Y_LOW) % Y_SIZE, rows:, :].astype(F32)
    near[...] = jnp.where(high == 1, 0.0, came)
    behind = jnp.where(high == 1, came, 0.0).astype(BF16)
    found = jnp.concatenate([total(parts, rows), behind], axis=0)
    out[...] = jnp.broadcast_to(found, out.shape)


def assemble_kernel(parts, mine, near_z, near_y, grad_up, low_grad):
    for tile in range(KV_HEADS * TILES):
        head, inside = tile // TILES, tile % TILES
        column = head * SHARE + inside if inside < SHARE else HEADS + (inside - SHARE) * KV_HEADS + head
        rows = slice(inside * RANK % PART, inside * RANK % PART + RANK)
        grad_up[:, column * D_HEAD : (column + 1) * D_HEAD] = parts[
            2 * head + inside * RANK // PART, rows, :
        ].astype(F32)
    x = lax.axis_index("ctx") // (2 * Z_SIZE)
    after = (x + 1) % X_SIZE * CORES + lax.axis_index("dp") % CORES
    low_grad[0, :RANK, :] = mine[:RANK, :]
    returned = near_z[...] + near_y[...] + parts[after, PART:, :].astype(F32)
    low_grad[0, RANK:, :] = mine[RANK:, :] + returned


def small(kernel, name, out_shape, *operands):
    return pl.pallas_call(
        kernel,
        out_shape=out_shape,
        compiler_params=pltpu.CompilerParams(vmem_limit_bytes=16 * 1024 * 1024),
        name=name,
    )(*operands)


def everywhere(terms, mine, backs):
    by_x, by_z, by_y = lines()
    sent = jax.ShapeDtypeStruct((Z_SIZE, PART + BACK, D_HEAD), BF16)
    near = jax.ShapeDtypeStruct((BACK, ROWS), F32)
    parts = small(along_kernel, "along", sent, exchange(terms, by_x), *backs)
    parts, near_z = small(beside_kernel, "beside", (sent, near), exchange(parts, by_z))
    parts, near_y = small(across_kernel, "across", (sent, near), exchange(parts, by_y))
    parts = exchange(parts, by_x)
    grad_up = jax.ShapeDtypeStruct((RANK, (HEADS + 2 * KV_HEADS) * D_HEAD), F32)
    low_grad = jax.ShapeDtypeStruct((1, 3 * RANK, ROWS), F32)
    grad_up, low_grad = small(
        assemble_kernel, "assemble", (grad_up, low_grad), parts, mine, near_z, near_y
    )
    return jnp.swapaxes(low_grad, 1, 2), grad_up


def shards(frozen_query, frozen_key_value, lowrank, adapter_up_weight, output_gradient):
    spans = lax.axis_size("ctx")
    position = lax.axis_index("ctx") % (GROUP // ROWS)
    light_half = position // 2
    odd = position % 2
    light_place = jnp.stack([light_half, odd]).astype(jnp.int32)
    heavy_place = jnp.stack([1 - light_half, odd]).astype(jnp.int32)
    message = jax.ShapeDtypeStruct((MESSAGE, 4 * D_HEAD), BF16)
    message_spec = whole(MESSAGE, 4 * D_HEAD)
    columns_first = jnp.swapaxes(lowrank, 1, 2)
    only = lambda *shape: pl.BlockSpec(shape, lambda i: (0,) * len(shape))
    light, heavy = pl.pallas_call(
        prepare_kernel,
        out_shape=(message, message),
        grid=(1,),
        in_specs=[
            only(1, ROWS, 8 * D_HEAD),
            only(1, 3 * RANK, ROWS),
            pl.BlockSpec((RANK, 8 * D_HEAD), lambda i: (0, HEADS // 8)),
        ],
        out_specs=[only(MESSAGE, 4 * D_HEAD)] * 2,
        compiler_params=pltpu.CompilerParams(vmem_limit_bytes=56 * 1024 * 1024),
        name="prepare",
    )(frozen_key_value, columns_first, adapter_up_weight)

    def send(value, by, step=1):
        return lax.ppermute(value, "ctx", [(i, (i + by) % spans) for i in range(0, spans, step)])

    one = send(light, 1)
    two_even = send(light, 2, 2)
    one_odd = send(heavy, 1, 2)
    two_odd = send(one, 1, 2)
    three = send(two_even, 1, 2)
    wide_out = jax.ShapeDtypeStruct((1, ROWS, HEADS * D_HEAD), BF16)
    terms_out = jax.ShapeDtypeStruct((2 * KV_HEADS, PART, D_HEAD), BF16)
    stacked_out = jax.ShapeDtypeStruct((HEADS * ROWS, D_HEAD), BF16)
    vmem, anywhere = pl.BlockSpec(memory_space=pltpu.VMEM), pl.BlockSpec(memory_space=pl.ANY)
    queries, grads = pl.pallas_call(
        stack_kernel,
        out_shape=(stacked_out, stacked_out),
        in_specs=[anywhere] * 3 + [vmem],
        out_specs=[vmem] * 2,
        scratch_shapes=[
            pltpu.VMEM((KV_HEADS, ROWS, WIDE), BF16),
            pltpu.VMEM((RANK, D_HEAD), BF16),
            pltpu.SemaphoreType.DMA((1 + KV_HEADS + HEADS,)),
        ],
        compiler_params=pltpu.CompilerParams(vmem_limit_bytes=51 * 1024 * 1024),
        cost_estimate=pl.CostEstimate(
            flops=2 * ROWS * RANK * WIDE * 4, bytes_accessed=16 * ROWS * WIDE * 2, transcendentals=0
        ),
        name="stack",
    )(frozen_query, output_gradient, columns_first, adapter_up_weight)
    arguments = (queries, grads) + (adapter_up_weight,) * 3
    light_arguments = (light_place, queries, grads, adapter_up_weight, light)
    light_outs = (wide_out, terms_out, jax.ShapeDtypeStruct((3 * RANK, 2 * ROWS), F32))
    light_call = functools.partial(
        pl.pallas_call,
        out_shape=light_outs,
        out_specs=[anywhere, vmem, vmem],
        scratch_shapes=[pltpu.VMEM((2, 1, ROWS, WIDE), BF16), pltpu.SemaphoreType.DMA((2,))],
        compiler_params=pltpu.CompilerParams(vmem_limit_bytes=28 * 1024 * 1024),
        cost_estimate=cost(2),
    )
    in_smem = [pl.BlockSpec(memory_space=pltpu.SMEM)]
    attended, terms, low_terms = light_call(
        light_kernel, in_specs=in_smem + [vmem] * 5, name="light_heads"
    )(*light_arguments, one)
    back_out = jax.ShapeDtypeStruct((2 * RANK, ROWS), F32)
    back_spec = whole(2 * RANK, ROWS)
    attended, terms, mine, *backs = pl.pallas_call(
        heavy_kernel,
        out_shape=(wide_out, terms_out, jax.ShapeDtypeStruct((3 * RANK, ROWS), F32)) + (back_out,) * 3,
        grid_spec=pltpu.PrefetchScalarGridSpec(
            num_scalar_prefetch=1,
            grid=(2,),
            in_specs=common_specs()
            + [message_spec] * 6
            + [whole(3 * RANK, 2 * ROWS)]
            + [pl.BlockSpec(memory_space=pl.ANY)] * 2,
            out_specs=[wide_half(), term_half(), whole(3 * RANK, ROWS)] + [back_spec] * 3,
        ),
        input_output_aliases={13: 0, 14: 1},
        compiler_params=params(),
        cost_estimate=cost(4),
        name="heavy_heads",
    )(heavy_place, *arguments, heavy, one, one_odd, two_even, two_odd, three, low_terms, attended, terms)
    grad_low, grad_up = everywhere(terms, mine, backs)
    return (attended, grad_low, grad_up)


def solution(mesh):
    return jax.shard_map(
        shards,
        mesh=mesh,
        in_specs=(
            P("dp", "ctx", None),
            P("dp", "ctx", None),
            P("dp", "ctx", None),
            P(),
            P("dp", "ctx", None),
        ),
        out_specs=(P("dp", "ctx", None), P("dp", "ctx", None), P()),
        check_vma=False,
    )
```

```python
import functools
import math

import jax
import jax.numpy as jnp
from jax import lax
from jax.experimental import pallas as pl
from jax.experimental.pallas import tpu as pltpu
from jax.sharding import PartitionSpec as P

HEADS = 32
KV_HEADS = 4
D_HEAD = 128
RANK = 16
GROUP = 512
ROWS = 128
MESSAGE = ROWS + RANK
SHARE = HEADS // KV_HEADS
WIDE = SHARE * D_HEAD
TILES = SHARE + 2
PART = TILES // 2 * RANK
BACK = 2 * RANK
X_SIZE, Y_LOW, Z_SIZE, CORES = 4, 4, 8, 2
Y_SIZE = 2 * Y_LOW
BLOCKED = -1e30
F32 = jnp.float32
BF16 = jnp.bfloat16


def mul(a, b):
    return lax.dot_general(a, b, (((1,), (0,)), ((), ())), preferred_element_type=F32)


def mul_t(a, b):
    return lax.dot_general(a, b, (((1,), (1,)), ((), ())), preferred_element_type=F32)


def t_mul(a, b):
    return lax.dot_general(a, b, (((0,), (0,)), ((), ())), preferred_element_type=F32)


def prepare_kernel(frozen_from, low_from, up_from, light, heavy, frozen, low, up, sems):
    columns = pl.ds(HEADS * D_HEAD, 2 * KV_HEADS * D_HEAD)
    copies = [
        pltpu.make_async_copy(low_from, low, sems.at[0]),
        pltpu.make_async_copy(up_from.at[:, columns], up, sems.at[1]),
        pltpu.make_async_copy(frozen_from, frozen, sems.at[2]),
    ]
    for copy in copies:
        copy.start()
    for copy in copies:
        copy.wait()
    low_q, low_k, low_v = (low[0, i * RANK : (i + 1) * RANK, :] for i in range(3))
    wide = KV_HEADS * D_HEAD
    keys = (frozen[0, :, :wide].astype(F32) + 2.0 * t_mul(low_k, up[:, :wide])).astype(BF16)
    values = (frozen[0, :, wide:].astype(F32) + 2.0 * t_mul(low_v, up[:, wide:])).astype(BF16)
    tail = jnp.concatenate([low_k, low_v, low_q, jnp.zeros((RANK, D_HEAD), BF16)], axis=1)
    half = 2 * D_HEAD

    def write(plain, moved):
        plain[:ROWS, :half] = keys[:, :half]
        plain[:ROWS, half:] = values[:, :half]
        plain[ROWS:, :] = tail
        moved[:ROWS, :half] = keys[:, half:]
        moved[:ROWS, half:] = values[:, half:]
        moved[ROWS:, :] = tail

    plain_light = lax.axis_index("ctx") % 4 < 2

    @pl.when(plain_light)
    def _():
        write(light, heavy)

    @pl.when(jnp.logical_not(plain_light))
    def _():
        write(heavy, light)


def stack_kernel(query, grad, low_all, up, queries, grads, held, low, sems):
    copies = [pltpu.make_async_copy(low_all.at[0, pl.ds(0, RANK), :], low, sems.at[0])]
    for i in range(KV_HEADS):
        wide = query.at[0, :, pl.ds(i * WIDE, WIDE)]
        copies.append(pltpu.make_async_copy(wide, held.at[i], sems.at[1 + i]))
    for i in range(HEADS):
        head = grad.at[0, :, pl.ds(i * D_HEAD, D_HEAD)]
        place = grads.at[pl.ds(i * ROWS, ROWS), :]
        copies.append(pltpu.make_async_copy(head, place, sems.at[1 + KV_HEADS + i]))
    for copy in copies:
        copy.start()
    copies[0].wait()
    for i in range(KV_HEADS):
        added = 2.0 * t_mul(low[...], up[:, i * WIDE : (i + 1) * WIDE])
        copies[1 + i].wait()
        found = (held[i].astype(F32) + added).astype(BF16)
        for k in range(SHARE):
            rows = slice((i * SHARE + k) * ROWS, (i * SHARE + k + 1) * ROWS)
            queries[rows, :] = found[:, k * D_HEAD : (k + 1) * D_HEAD]
    for copy in copies[1 + KV_HEADS :]:
        copy.wait()


def attend(place, head, all_queries, all_grads, ups, blocks, closed, attended, terms):
    up_rows, up_k, up_v = ups
    key_cols = pl.ds(pl.multiple_of(head * D_HEAD, D_HEAD), D_HEAD)
    value_cols = pl.ds(pl.multiple_of((head + 2) * D_HEAD, D_HEAD), D_HEAD)
    bias = jnp.where(place[1] == 1, 0.0, BLOCKED).astype(F32)
    scale = 1.0 / math.sqrt(D_HEAD)
    keys = jnp.concatenate([b(slice(0, ROWS), key_cols) for b in blocks], axis=0)
    values = jnp.concatenate([b(slice(0, ROWS), value_cols) for b in blocks], axis=0)
    tail = slice(ROWS, MESSAGE)
    low_k = jnp.concatenate([b(tail, slice(0, D_HEAD)) for b in blocks], axis=1)
    low_v = jnp.concatenate([b(tail, slice(D_HEAD, 2 * D_HEAD)) for b in blocks], axis=1)
    low_q = blocks[0](tail, slice(2 * D_HEAD, 3 * D_HEAD))
    keys_t = keys.T
    values_t = values.T
    wide = 2 * ROWS
    row = lax.broadcasted_iota(jnp.int32, (ROWS, wide), 0)
    col = lax.broadcasted_iota(jnp.int32, (ROWS, wide), 1)
    causal = row <= jnp.where(col >= ROWS, col - ROWS, col)
    pairs = [slice(i * wide, (i + 1) * wide) for i in range(SHARE // 2)]
    products = [(mul_t(keys, all_queries[p]), mul_t(values, all_grads[p])) for p in pairs]
    all_weights, all_scores = [], []
    for logits, prob_grad in products:
        parts = [jnp.where(causal, logits[:ROWS], BLOCKED)]
        for i, shut in enumerate(closed):
            part = logits[(i + 1) * ROWS : (i + 2) * ROWS]
            parts.append(part + bias if shut else part)
        logits = jnp.concatenate(parts, axis=0)
        peak = jnp.max(logits, axis=0, keepdims=True)
        exps = jnp.exp2((logits - peak) * (scale * math.log2(math.e)))
        weights = (exps * (1.0 / jnp.sum(exps, axis=0, keepdims=True))).astype(BF16)
        weights_f = weights.astype(F32)
        product = weights_f * prob_grad
        row_dot = jnp.sum(product, axis=0, keepdims=True)
        all_weights.append(weights)
        all_scores.append((product - weights_f * row_dot).astype(BF16))
    grad_queries = []
    for i in range(SHARE // 2):
        out_t = mul(values_t, all_weights[i])
        grad_query_t = (mul(keys_t, all_scores[i]) * scale).astype(BF16)
        for k in range(2):
            mine = slice(k * ROWS, (k + 1) * ROWS)
            attended(2 * i + k)[...] = out_t[:, mine].T.astype(BF16)
            grad_queries.append(grad_query_t[:, mine])
    stacked = jnp.concatenate(grad_queries, axis=0)
    low_grad = mul(up_rows, stacked)
    found = [2.0 * mul_t(low_q, stacked)]
    grad_keys = mul(jnp.concatenate(all_scores, axis=1), all_queries)
    grad_keys = (grad_keys * scale).astype(BF16)
    grad_values = mul(jnp.concatenate(all_weights, axis=1), all_grads).astype(BF16)
    found += [2.0 * mul(low_k, grad_keys), 2.0 * mul(low_v, grad_values)]
    found = jnp.concatenate(found, axis=1).astype(BF16)
    for tile in range(TILES):
        rows = slice(tile * RANK % PART, tile * RANK % PART + RANK)
        terms(tile * RANK // PART)[rows, :] = found[:, tile * D_HEAD : (tile + 1) * D_HEAD]
    return 2.0 * low_grad, 2.0 * mul_t(up_k, grad_keys), 2.0 * mul_t(up_v, grad_values)


def light_heads(place, query, grad, up, blocks, closed, attended, terms, low_terms, held, sems):
    sums, copies = [], []
    for head in range(2):
        chosen = place[0] * 2 + head
        rows = pl.ds(pl.multiple_of(chosen * WIDE, WIDE), WIDE)
        ups = [
            up[:, pl.ds(pl.multiple_of(first * D_HEAD + chosen * width, D_HEAD), width)]
            for first, width in ((0, WIDE), (HEADS, D_HEAD), (HEADS + KV_HEADS, D_HEAD))
        ]
        found = attend(
            place, head, query[rows, :], grad[rows, :], ups, blocks, closed,
            lambda k, head=head: held.at[head, 0, :, k * D_HEAD : (k + 1) * D_HEAD],
            lambda i, chosen=chosen: terms.at[2 * chosen + i],
        )
        sums = [a + b for a, b in zip(sums, found)] if sums else found
        copies.append(
            pltpu.make_async_copy(held.at[head], attended.at[:, :, rows], sems.at[head])
        )
        copies[-1].start()
    by_query, by_key, by_value = sums
    low_terms[...] = jnp.zeros_like(low_terms)
    reach = by_key.shape[1]
    low_terms[:RANK, :ROWS] = by_query
    low_terms[RANK : 2 * RANK, :reach] = by_key
    low_terms[2 * RANK :, :reach] = by_value
    for copy in copies:
        copy.wait()


def light_kernel(place, query, grad, up, own, one, attended, terms, low_terms, held, sems):
    blocks = [lambda r, c: own[r, c], lambda r, c: one[r, c]]
    light_heads(place, query, grad, up, blocks, [True], attended, terms, low_terms, held, sems)


def heavy_kernel(
    place, query, grad, up_q, up_k, up_v, own, one_even, one_odd, two_even, two_odd, three, before,
    _attended, _terms, attended, terms, mine, back_one, back_two, back_three,
):
    odd = place[1] == 1
    blocks = [
        lambda r, c: own[r, c],
        lambda r, c: jnp.where(odd, one_odd[r, c], one_even[r, c]),
        lambda r, c: jnp.where(odd, two_odd[r, c], two_even[r, c]),
        lambda r, c: three[r, c],
    ]

    @pl.when(pl.program_id(0) == 0)
    def _():
        mine[...] = before[:, :ROWS]
        back_one[...] = before[RANK:, ROWS:]
        back_two[...] = jnp.zeros_like(back_two)
        back_three[...] = jnp.zeros_like(back_three)

    ups = (up_q[...], up_k[...], up_v[...])
    by_query, by_key, by_value = attend(
        place, pl.program_id(0), query[...], grad[...], ups, blocks, [False, False, True],
        lambda k: attended.at[0, :, k * D_HEAD : (k + 1) * D_HEAD],
        lambda i: terms.at[i],
    )
    mine[:RANK, :] += by_query
    mine[RANK : 2 * RANK, :] += by_key[:, :ROWS]
    mine[2 * RANK :, :] += by_value[:, :ROWS]
    for i, back in enumerate((back_one, back_two, back_three)):
        block = slice((i + 1) * ROWS, (i + 2) * ROWS)
        back[:RANK, :] += by_key[:, block]
        back[RANK:, :] += by_value[:, block]


def whole(*shape):
    return pl.BlockSpec(shape, lambda head, place: (0,) * len(shape))


def at_half(rows, width, first=0):
    return pl.BlockSpec((rows, width), lambda head, place: (0, first + place[0] * 2 + head))


def wide_half():
    return pl.BlockSpec((1, ROWS, WIDE), lambda head, place: (0, 0, place[0] * 2 + head))


def term_half():
    return pl.BlockSpec((2, PART, D_HEAD), lambda head, place: (place[0] * 2 + head, 0, 0))


def common_specs():
    stacked = pl.BlockSpec((SHARE * ROWS, D_HEAD), lambda head, place: (place[0] * 2 + head, 0))
    return [
        stacked,
        stacked,
        at_half(RANK, WIDE),
        at_half(RANK, D_HEAD, HEADS),
        at_half(RANK, D_HEAD, HEADS + KV_HEADS),
    ]


def params():
    return pltpu.CompilerParams(
        dimension_semantics=("arbitrary",), vmem_limit_bytes=28 * 1024 * 1024
    )


def cost(blocks):
    sizes = 16 * blocks * ROWS * ROWS
    return pl.CostEstimate(
        flops=12 * sizes * D_HEAD, bytes_accessed=6 * ROWS * WIDE * 2, transcendentals=sizes
    )


def exchange(value, groups):
    return lax.all_to_all(value, ("dp", "ctx"), 0, 0, axis_index_groups=groups)


def index_of(x, y, z, core):
    dp = y % Y_LOW * CORES + core
    return dp * (2 * X_SIZE * Z_SIZE) + (x * 2 + y // Y_LOW) * Z_SIZE + z


def lines():
    xs, ys, zs, cores = range(X_SIZE), range(Y_SIZE), range(Z_SIZE), range(CORES)
    by_x = [[index_of(x, y, z, c) for x in xs for c in cores] for y in ys for z in zs]
    by_z = [[index_of(x, y, z, c) for z in zs] for x in xs for y in ys for c in cores]
    by_y = [[index_of(x, y, z, c) for y in ys] for x in xs for z in zs for c in cores]
    return by_x, by_z, by_y


def total(parts, rows):
    return jnp.sum(parts[:, :rows, :].astype(F32), axis=0).astype(BF16)


def along_kernel(parts, back_one, back_two, back_three, out):
    rows = parts.shape[1]
    out[:, :rows, :] = jnp.broadcast_to(total(parts, rows), (Z_SIZE, rows, D_HEAD))
    out[:, rows:, :] = jnp.zeros((Z_SIZE, BACK, D_HEAD), BF16)
    z = lax.axis_index("ctx") % Z_SIZE
    for by, back in enumerate((back_one, back_two, back_three)):
        out[(z + Z_SIZE - 1 - by) % Z_SIZE, rows:, :] = back[...].astype(BF16)


def beside_kernel(parts, out, near):
    rows = parts.shape[1] - BACK
    z = lax.axis_index("ctx") % Z_SIZE
    ahead = jnp.zeros((BACK, D_HEAD), F32)
    behind = jnp.zeros((BACK, D_HEAD), F32)
    for i in range(Z_SIZE):
        came = parts[i, rows:, :].astype(F32)
        ahead = ahead + jnp.where(i > z, came, 0.0)
        behind = behind + jnp.where(i > z, 0.0, came)
    near[...] = ahead
    found = jnp.concatenate([total(parts, rows), behind.astype(BF16)], axis=0)
    out[...] = jnp.broadcast_to(found, out.shape)


def across_kernel(parts, out, near):
    rows = parts.shape[1] - BACK
    high = lax.axis_index("ctx") // Z_SIZE % 2
    y = high * Y_LOW + lax.axis_index("dp") // CORES
    came = parts[(y + Y_LOW) % Y_SIZE, rows:, :].astype(F32)
    near[...] = jnp.where(high == 1, 0.0, came)
    behind = jnp.where(high == 1, came, 0.0).astype(BF16)
    found = jnp.concatenate([total(parts, rows), behind], axis=0)
    out[...] = jnp.broadcast_to(found, out.shape)


def assemble_kernel(parts, mine, near_z, near_y, grad_up, low_grad):
    for tile in range(KV_HEADS * TILES):
        head, inside = tile // TILES, tile % TILES
        column = head * SHARE + inside if inside < SHARE else HEADS + (inside - SHARE) * KV_HEADS + head
        rows = slice(inside * RANK % PART, inside * RANK % PART + RANK)
        grad_up[:, column * D_HEAD : (column + 1) * D_HEAD] = parts[
            2 * head + inside * RANK // PART, rows, :
        ].astype(F32)
    x = lax.axis_index("ctx") // (2 * Z_SIZE)
    after = (x + 1) % X_SIZE * CORES + lax.axis_index("dp") % CORES
    low_grad[0, :RANK, :] = mine[:RANK, :]
    returned = near_z[...] + near_y[...] + parts[after, PART:, :].astype(F32)
    low_grad[0, RANK:, :] = mine[RANK:, :] + returned


def small(kernel, name, out_shape, *operands):
    return pl.pallas_call(
        kernel,
        out_shape=out_shape,
        compiler_params=pltpu.CompilerParams(vmem_limit_bytes=16 * 1024 * 1024),
        name=name,
    )(*operands)


def everywhere(terms, mine, backs):
    by_x, by_z, by_y = lines()
    sent = jax.ShapeDtypeStruct((Z_SIZE, PART + BACK, D_HEAD), BF16)
    near = jax.ShapeDtypeStruct((BACK, ROWS), F32)
    parts = small(along_kernel, "along", sent, exchange(terms, by_x), *backs)
    parts, near_z = small(beside_kernel, "beside", (sent, near), exchange(parts, by_z))
    parts, near_y = small(across_kernel, "across", (sent, near), exchange(parts, by_y))
    parts = exchange(parts, by_x)
    grad_up = jax.ShapeDtypeStruct((RANK, (HEADS + 2 * KV_HEADS) * D_HEAD), F32)
    low_grad = jax.ShapeDtypeStruct((1, 3 * RANK, ROWS), F32)
    grad_up, low_grad = small(
        assemble_kernel, "assemble", (grad_up, low_grad), parts, mine, near_z, near_y
    )
    return jnp.swapaxes(low_grad, 1, 2), grad_up


def shards(frozen_query, frozen_key_value, lowrank, adapter_up_weight, output_gradient):
    spans = lax.axis_size("ctx")
    position = lax.axis_index("ctx") % (GROUP // ROWS)
    light_half = position // 2
    odd = position % 2
    light_place = jnp.stack([light_half, odd]).astype(jnp.int32)
    heavy_place = jnp.stack([1 - light_half, odd]).astype(jnp.int32)
    message = jax.ShapeDtypeStruct((MESSAGE, 4 * D_HEAD), BF16)
    message_spec = whole(MESSAGE, 4 * D_HEAD)
    columns_first = jnp.swapaxes(lowrank, 1, 2)
    only = lambda *shape: pl.BlockSpec(shape, lambda i: (0,) * len(shape))
    light, heavy = pl.pallas_call(
        prepare_kernel,
        out_shape=(message, message),
        in_specs=[pl.BlockSpec(memory_space=pl.ANY)] * 3,
        out_specs=[pl.BlockSpec(memory_space=pltpu.VMEM)] * 2,
        scratch_shapes=[
            pltpu.VMEM((1, ROWS, 8 * D_HEAD), BF16),
            pltpu.VMEM((1, 3 * RANK, ROWS), BF16),
            pltpu.VMEM((RANK, 8 * D_HEAD), BF16),
            pltpu.SemaphoreType.DMA((3,)),
        ],
        compiler_params=pltpu.CompilerParams(vmem_limit_bytes=56 * 1024 * 1024),
        name="prepare",
    )(frozen_key_value, columns_first, adapter_up_weight)

    def send(value, by, step=1):
        return lax.ppermute(value, "ctx", [(i, (i + by) % spans) for i in range(0, spans, step)])

    one = send(light, 1)
    two_even = send(light, 2, 2)
    one_odd = send(heavy, 1, 2)
    two_odd = send(one, 1, 2)
    three = send(two_even, 1, 2)
    wide_out = jax.ShapeDtypeStruct((1, ROWS, HEADS * D_HEAD), BF16)
    terms_out = jax.ShapeDtypeStruct((2 * KV_HEADS, PART, D_HEAD), BF16)
    stacked_out = jax.ShapeDtypeStruct((HEADS * ROWS, D_HEAD), BF16)
    vmem, anywhere = pl.BlockSpec(memory_space=pltpu.VMEM), pl.BlockSpec(memory_space=pl.ANY)
    queries, grads = pl.pallas_call(
        stack_kernel,
        out_shape=(stacked_out, stacked_out),
        in_specs=[anywhere] * 3 + [vmem],
        out_specs=[vmem] * 2,
        scratch_shapes=[
            pltpu.VMEM((KV_HEADS, ROWS, WIDE), BF16),
            pltpu.VMEM((RANK, D_HEAD), BF16),
            pltpu.SemaphoreType.DMA((1 + KV_HEADS + HEADS,)),
        ],
        compiler_params=pltpu.CompilerParams(vmem_limit_bytes=51 * 1024 * 1024),
        cost_estimate=pl.CostEstimate(
            flops=2 * ROWS * RANK * WIDE * 4, bytes_accessed=16 * ROWS * WIDE * 2, transcendentals=0
        ),
        name="stack",
    )(frozen_query, output_gradient, columns_first, adapter_up_weight)
    arguments = (queries, grads) + (adapter_up_weight,) * 3
    light_arguments = (light_place, queries, grads, adapter_up_weight, light)
    light_outs = (wide_out, terms_out, jax.ShapeDtypeStruct((3 * RANK, 2 * ROWS), F32))
    light_call = functools.partial(
        pl.pallas_call,
        out_shape=light_outs,
        out_specs=[anywhere, vmem, vmem],
        scratch_shapes=[pltpu.VMEM((2, 1, ROWS, WIDE), BF16), pltpu.SemaphoreType.DMA((2,))],
        compiler_params=pltpu.CompilerParams(vmem_limit_bytes=28 * 1024 * 1024),
        cost_estimate=cost(2),
    )
    in_smem = [pl.BlockSpec(memory_space=pltpu.SMEM)]
    attended, terms, low_terms = light_call(
        light_kernel, in_specs=in_smem + [vmem] * 5, name="light_heads"
    )(*light_arguments, one)
    back_out = jax.ShapeDtypeStruct((2 * RANK, ROWS), F32)
    back_spec = whole(2 * RANK, ROWS)
    attended, terms, mine, *backs = pl.pallas_call(
        heavy_kernel,
        out_shape=(wide_out, terms_out, jax.ShapeDtypeStruct((3 * RANK, ROWS), F32)) + (back_out,) * 3,
        grid_spec=pltpu.PrefetchScalarGridSpec(
            num_scalar_prefetch=1,
            grid=(2,),
            in_specs=common_specs()
            + [message_spec] * 6
            + [whole(3 * RANK, 2 * ROWS)]
            + [pl.BlockSpec(memory_space=pl.ANY)] * 2,
            out_specs=[wide_half(), term_half(), whole(3 * RANK, ROWS)] + [back_spec] * 3,
        ),
        input_output_aliases={13: 0, 14: 1},
        compiler_params=params(),
        cost_estimate=cost(4),
        name="heavy_heads",
    )(heavy_place, *arguments, heavy, one, one_odd, two_even, two_odd, three, low_terms, attended, terms)
    grad_low, grad_up = everywhere(terms, mine, backs)
    return (attended, grad_low, grad_up)


def solution(mesh):
    return jax.shard_map(
        shards,
        mesh=mesh,
        in_specs=(
            P("dp", "ctx", None),
            P("dp", "ctx", None),
            P("dp", "ctx", None),
            P(),
            P("dp", "ctx", None),
        ),
        out_specs=(P("dp", "ctx", None), P("dp", "ctx", None), P()),
        check_vma=False,
    )
```
